256 devices in a mesh: col: 64 (over z, y, core), row: 4 (over x).
Axes of the slice: x: 4, y: 4, z: 8, core: 2. Of those that a mesh axis runs over, the one named last changes fastest.
Arguments:
- diag_blocks: float32 [128, 512, 512], P('col'), may hold values from -1 to 3, as said below
- panel_blocks: float32 [128, 8, 512, 512], P('col', None, 'row'), may hold values from -0.3 to 0.3
- ancestors: int32 [128, 8], P('col'), may hold values from 0 to 63, all different within a row; in each aligned block of 2 rows (0 to 1, 2 to 3, ...) at most 2 rows name the same one
- target_ids: int32 [64], P('col'), may hold values from 0 to 63, each once
- target_tiles: float32 [64, 512, 512], P('col', 'row'), may hold values from -6 to 6
Outputs:
- panel_factor: float32 [128, 8, 512, 512], P('col', None, 'row')
- updated_tiles: float32 [64, 512, 512], P('col', 'row')
The draws below stay inside these ranges and needn't reach their ends.
Inputs may be any that keep to these rules, and one draw needn't show every extreme that they name: `ancestors`: each row names 8 different target blocks; on the supernodes of one index of col a target block is named at most twice, and exactly twice somewhere; every target block is named. `target_ids`: A permutation of the target blocks. `diag_blocks`: each block is symmetric and positive definite, with smallest eigenvalue 0.05 or more.
All inputs are finite; a program needn't handle non-finite values.
Results may differ from the reference program's by a relative error of at most 0.0029.
Values may be sent and summed in bfloat16 or wider, within the bound.
No kernel may reach another device: no remote copies, remote signals or barrier semaphores. Data moves between devices by JAX's collectives and lax.ppermute only.
A program may use at most 128 MiB of HBM per device.

```python
import math
import jax
import jax.numpy as jnp
import numpy as np
from jax import lax

W = 512
ANC = 8
SN_DEV = 2
NS = 128
NT = 64


def gram_block(mixing, shift):
    gram = jnp.dot(mixing, mixing.T, precision=lax.Precision.HIGHEST) * (0.5 / W)
    gram = 0.5 * (gram + gram.T)
    return gram + shift * jnp.eye(W, dtype=jnp.float32)


def draw_diag_blocks(key, part):
    key = jax.random.fold_in(key, 11)
    key_mix, key_shift = jax.random.split(key)
    block_keys = jax.random.split(key_mix, NS)
    shifts = jnp.exp(jax.random.uniform(key_shift, (NS,), jnp.float32, math.log(0.1), math.log(0.5)))

    def one_block(args):
        block_key, shift = args
        mixing = jax.random.truncated_normal(block_key, -4.0, 4.0, (W, 2 * W), jnp.float32)
        return gram_block(mixing, shift)
    return lax.map(one_block, (block_keys, shifts)).astype(jnp.float32)


def block_levels(rng, shape, shards, low, top_value):
    loudness, own = 1.0, jax.random.fold_in(rng, 6)
    for axis_at, shards_of in shards:
        draws = jnp.exp(jax.random.uniform(jax.random.fold_in(own, axis_at), (shards_of,), jnp.float32, low / len(shards), top_value / len(shards)))
        loudness = loudness * jnp.repeat(draws, shape[axis_at] // shards_of).reshape([-1 if axis == axis_at else 1 for axis in range(len(shape))])
    return loudness


def shared_out(rng, own, number, rows, number_of, top, limit, slope):
    sequence = jax.random.permutation(rng, number_of)
    crowded, ordinary = shares(number_of, rows * top, limit, slope, True), shares(number_of, rows * top, limit, slope, False)
    places = jnp.arange(number_of)

    def named(lengths, offset_by):
        used = int((lengths > 0).sum())
        fixed = max(1, used // 4)
        moved = fixed + (places - fixed + offset_by * (used - fixed)) % max(1, number_of - fixed)
        return jnp.zeros((number_of,), jnp.int32).at[sequence[jnp.where(places < fixed, places, moved)]].set(jnp.asarray(lengths, jnp.int32))

    lengths = jnp.where(number % 4 == 0, named(crowded, number // 4), named(ordinary, number - number // 4 - 1))
    mixed = jax.random.permutation(jax.random.fold_in(own, 3), number_of)
    giver, sink = mixed[0:number_of // 2 * 2:2], mixed[1:number_of // 2 * 2:2]
    margin = jnp.minimum(lengths[giver] - 1, limit - lengths[sink]) // 2
    margin = jnp.where((giver == sequence[0]) | (sink == sequence[0]) | (lengths[sink] == 0), 0, jnp.maximum(margin, 0))
    moved = jax.random.randint(jax.random.fold_in(own, 4), (number_of // 2,), 0, 1 << 20) % (margin + 1)
    lengths = lengths.at[giver].add(-moved).at[sink].add(moved)
    items = jnp.searchsorted(jnp.cumsum(lengths), jnp.arange(rows * top), side="right").astype(jnp.int32)
    table = items.reshape(top, rows).T
    table = table[jax.random.permutation(jax.random.fold_in(own, 1), rows)]
    offset_by = jax.random.randint(jax.random.fold_in(own, 2), (rows, 1), 0, top)
    return jnp.take_along_axis(table, (jnp.arange(top)[None, :] + offset_by) % top, axis=1)


def shares(amount, total, bound, slope, full):
    loads = [(1 << 20) // math.isqrt(rank ** slope) + 1 for rank in range(1, amount + 1)]
    largest = bound if full else min(bound, max(-(-total // amount), total * loads[0] // sum(loads)))
    least = 1 if total - largest >= amount - 1 else 0
    holding, rest = [largest] + [least] * (amount - 1), total - largest - least * (amount - 1)
    while rest > 0:
        free = [i for i in range(1, amount) if holding[i] < largest] or [i for i in range(1, amount) if holding[i] < bound]
        whole, left = sum([loads[i] for i in free]), rest
        for i in free:
            extra = min(bound - holding[i], max(1, left * loads[i] // whole), rest)
            holding[i] = holding[i] + extra
            rest = rest - extra
    return np.array(holding)


def normal_values(stream_key, dims, width, bound, cuts=(), kind=jnp.bfloat16):
    gain = block_levels(stream_key, dims, cuts, -0.22, 0.18) if cuts else 1.0
    values = jax.random.normal(stream_key, dims, jnp.float32) * width * gain
    return jnp.minimum(jnp.maximum(values, -bound), bound).astype(kind)


def setup_inputs(seed: int = 0) -> dict:
    seeds = jax.random.split(jax.random.key(seed), 6)
    diag_blocks = draw_diag_blocks(jax.random.fold_in(seeds[5], 71), 0)
    panel_blocks = normal_values(seeds[1], (NS, ANC, W, W), 0.05, 0.3, ((0, 64), (2, 4)), jnp.float32)
    ancestors_keys = jax.random.split(jax.random.fold_in(seeds[2], 1), NS // SN_DEV)
    ancestors_turns = jax.random.permutation(jax.random.fold_in(seeds[2], 3), NS // SN_DEV)
    ancestors = jax.vmap(lambda own, number: shared_out(jax.random.fold_in(seeds[2], 2), own, number, SN_DEV, NT, ANC, 2, 2))(ancestors_keys, ancestors_turns).reshape((NS, ANC))
    target_ids = jax.random.permutation(seeds[3], NT).astype(jnp.int32)
    target_tiles = normal_values(seeds[4], (NT, W, W), 1.0, 6.0, ((0, 64), (1, 4)), jnp.float32)
    return dict(diag_blocks=diag_blocks, panel_blocks=panel_blocks, ancestors=ancestors, target_ids=target_ids, target_tiles=target_tiles)


def solve_panel(args):
    diag_block, panel = args
    factor = jnp.linalg.cholesky(diag_block)
    rhs = jnp.swapaxes(panel.reshape(ANC * W, W), 0, 1)
    solved = jax.scipy.linalg.solve_triangular(factor, rhs, lower=True)
    return jnp.swapaxes(solved, 0, 1).reshape(ANC, W, W)

def reference(diag_blocks, panel_blocks, ancestors, target_ids, target_tiles):
    panel_factor = lax.map(solve_panel, (diag_blocks, panel_blocks))
    rounded = panel_factor.astype(jnp.bfloat16)
    matches = ancestors[:, :, None] == target_ids[None, None, :]
    position = jnp.sum(jnp.where(matches, jnp.arange(NT, dtype=jnp.int32)[None, None, :], 0), axis=2).astype(jnp.int32)
    flat_pos = position.reshape(NS * ANC)

    def accumulate(index, total):
        s_idx = index // ANC
        j_idx = index % ANC
        tile = rounded[s_idx, j_idx]
        product = jnp.dot(tile.astype(jnp.float32), tile.T.astype(jnp.float32), preferred_element_type=jnp.float32)
        return total.at[flat_pos[index]].add(product)
    update = lax.fori_loop(0, NS * ANC, accumulate, jnp.zeros((NT, W, W), jnp.float32))
    return (panel_factor, target_tiles - update)
```

```python
import functools

import jax
import jax.numpy as jnp
from jax import lax
from jax.experimental import pallas as pl
from jax.experimental.pallas import tpu as pltpu
from jax.sharding import Mesh, PartitionSpec as P

F32 = jnp.float32
BF16 = jnp.bfloat16
BLK = 128
PAN = 16
VMEM_LIMIT = 48 * 1024 * 1024
COL = ("z", "y", "core")


def split3(x):
    a = x.astype(BF16)
    rest = x - a.astype(F32)
    b = rest.astype(BF16)
    c = (rest - b.astype(F32)).astype(BF16)
    return a, b, c


def split2(x):
    a = x.astype(BF16)
    return a, (x - a.astype(F32)).astype(BF16)


def outer_product(left, right):
    a, b, c = split3(left)
    p, q, r = split3(right)
    return lax.dot_general(
        jnp.concatenate([a, a, a, b, b, c], axis=0),
        jnp.concatenate([p, q, r, p, q, p], axis=0),
        (((0,), (0,)), ((), ())),
        preferred_element_type=F32,
    )


def dot_dims(a, b, dims, precision=None):
    return lax.dot_general(a, b, (dims, ((), ())), precision=precision, preferred_element_type=F32)


def refined_reciprocal(d):
    r = pl.reciprocal(d, approx=True)
    r = r * (2.0 - d * r)
    return r * (2.0 - d * r)


def factor_panel(panel, k):
    half = PAN // 2
    lane1 = lax.broadcasted_iota(jnp.int32, (1, BLK), 1)
    sub = lax.broadcasted_iota(jnp.int32, (half, BLK), 0)
    lane = lax.broadcasted_iota(jnp.int32, (half, BLK), 1)
    top, bot = panel[:half], panel[half:]
    tops = [jnp.broadcast_to(top[:, k + c : k + c + 1], (half, BLK)) for c in range(PAN)]
    bots = [jnp.broadcast_to(bot[:, k + c : k + c + 1], (half, BLK)) for c in range(PAN)]
    diag_top = jnp.ones((half, BLK), F32)
    diag_bot = jnp.ones((half, BLK), F32)
    for i in range(PAN):
        if i < half:
            d = tops[i][i : i + 1]
            r = refined_reciprocal(d)
            mt = jnp.where(sub > i, tops[i] * r, 0.0)
            mb = bots[i] * r
            diag_top = jnp.where(sub == i, d, diag_top)
            for c in range(i + 1, PAN):
                row = tops[c][i : i + 1]
                tops[c] = tops[c] - mt * row
                bots[c] = bots[c] - mb * row
            pivot = top[i : i + 1] + jnp.where(lane1 == k + i, 1.0, 0.0)
            top = top - mt * pivot
            bot = bot - mb * pivot
        else:
            h = i - half
            d = bots[i][h : h + 1]
            r = refined_reciprocal(d)
            mb = jnp.where(sub > h, bots[i] * r, 0.0)
            diag_bot = jnp.where(sub == h, d, diag_bot)
            for c in range(i + 1, PAN):
                bots[c] = bots[c] - mb * bots[c][h : h + 1]
            pivot = bot[h : h + 1] + jnp.where(lane1 == k + i, 1.0, 0.0)
            bot = bot - mb * pivot

    def finish(rows, diag, first):
        at = lane - k - first
        rows = jnp.where(at == sub, 1.0, jnp.where((at > sub) & (lane < k + PAN), 0.0, rows))
        return rows * lax.rsqrt(diag)

    return jnp.concatenate([finish(top, diag_top, 0), finish(bot, diag_bot, half)], axis=0)


def factor_blocks(blocks):
    mats = list(blocks)
    done = [[] for _ in mats]
    for k in range(0, BLK, PAN):
        lane = lax.broadcasted_iota(jnp.int32, (PAN, BLK), 1)
        for s in range(len(mats)):
            rows = factor_panel(mats[s][:PAN], k)
            done[s].append(jnp.where(lane < k + PAN, rows, 0.0))
            if k + PAN < BLK:
                ahead = jnp.where(lane >= k + PAN, rows, 0.0)
                rest = mats[s][PAN:]
                at = lax.broadcasted_iota(jnp.int32, rest.shape, 1)
                rest = jnp.where((at >= k) & (at < k + PAN), 0.0, rest)
                mats[s] = rest - outer_product(ahead, rows)[k + PAN :]
    return [jnp.concatenate(rows, axis=0) for rows in done]


def factor_kernel(k, sn, *refs):
    diag_ref, w_prev, w_ref = refs[0], refs[1 : 1 + k], refs[1 + k]
    width = diag_ref.shape[2]
    rows = []
    for s in range(sn):
        row = diag_ref[s]
        if k:
            lane = lax.broadcasted_iota(jnp.int32, (BLK, width), 1)
            left = jnp.concatenate([w[s, :, BLK * k : BLK * (k + 1)] for w in w_prev], axis=0)
            right = jnp.concatenate(
                [
                    jnp.where((lane >= BLK * (i + 1)) & (lane < BLK * k), 0.0, w[s])
                    for i, w in enumerate(w_prev)
                ],
                axis=0,
            )
            row = jnp.where(lane < BLK * k, 0.0, row)
            row = row - dot_dims(left, right, ((0,), (0,)), lax.Precision.HIGHEST)
        rows.append(row)
    here = slice(BLK * k, BLK * (k + 1))
    inverses = factor_blocks([row[:, here] for row in rows])
    for s in range(sn):
        scaled = dot_dims(inverses[s], rows[s], ((1,), (0,)), lax.Precision.HIGHEST)
        lane = lax.broadcasted_iota(jnp.int32, (BLK, width), 1)
        inside = (lane >= BLK * k) & (lane < BLK * (k + 1))
        spread = jnp.concatenate([inverses[s]] * (width // BLK), axis=1)
        w_ref[s] = jnp.where(inside, spread, scaled)


def whole(shape):
    return pl.BlockSpec(shape, lambda i: (0,) * len(shape))


def factor_rows(k, diag_blocks, w_prev):
    sn, width, _ = diag_blocks.shape
    return pl.pallas_call(
        functools.partial(factor_kernel, k, sn),
        grid=(1,),
        in_specs=[pl.BlockSpec((sn, BLK, width), lambda i: (0, k, 0))] + [whole((sn, BLK, width))] * k,
        out_specs=whole((sn, BLK, width)),
        out_shape=jax.ShapeDtypeStruct((sn, BLK, width), F32),
        compiler_params=pltpu.CompilerParams(vmem_limit_bytes=VMEM_LIMIT),
        cost_estimate=pl.CostEstimate(flops=10**10, bytes_accessed=10**7, transcendentals=0),
        name="factor_rows",
    )(diag_blocks, *w_prev)


def solve_kernel(k, sn, info_ref, w_ref, b_ref, *refs):
    x_ref, r_ref, half_ref = refs[-3:]
    used = BLK * (k + 1)
    tile = 256
    for s in range(sn):
        w_hi, w_lo = split2(w_ref[s, :, :used])

        def step(t, carry):
            at = pl.ds(pl.multiple_of(t * tile, tile), tile)
            b_hi, b_lo = split2(b_ref[s, at, :])
            nt = ((1,), (1,))
            x = dot_dims(b_hi, w_hi, nt) + (dot_dims(b_hi, w_lo, nt) + dot_dims(b_lo, w_hi, nt))
            x_ref[s, at, :] = x
            r_ref[s, at, :] = x.astype(BF16)
            return carry

        lax.fori_loop(0, b_ref.shape[1] // tile, step, 0)
    half_ref[...] = r_ref[jnp.where(info_ref[0] < 2, 1, 0)]


def solve_chunk(k, row, w, panel, solved):
    sn, rows, width = panel.shape
    args = [row, w, panel]
    in_specs = [
        pl.BlockSpec(memory_space=pltpu.SMEM),
        whole((sn, BLK, width)),
        whole((sn, rows, BLK * (k + 1))),
    ]
    aliases = {}
    if k:
        args.append(solved)
        in_specs.append(pl.BlockSpec(memory_space=pl.ANY))
        aliases = {len(args) - 1: 0}
    return pl.pallas_call(
        functools.partial(solve_kernel, k, sn),
        grid=(1,),
        in_specs=in_specs,
        out_specs=[
            pl.BlockSpec((sn, rows, BLK), lambda i: (0, 0, k)),
            whole((sn, rows, BLK)),
            whole((rows, BLK)),
        ],
        out_shape=[
            jax.ShapeDtypeStruct((sn, rows, width), F32),
            jax.ShapeDtypeStruct((sn, rows, BLK), BF16),
            jax.ShapeDtypeStruct((rows, BLK), BF16),
        ],
        input_output_aliases=aliases,
        compiler_params=pltpu.CompilerParams(vmem_limit_bytes=VMEM_LIMIT),
        cost_estimate=pl.CostEstimate(flops=10**9, bytes_accessed=10**7, transcendentals=0),
        name="solve_chunk",
    )(*args)


def products_kernel(n, info_ref, *refs):
    own, right, across = refs[:n], refs[n : 2 * n], refs[2 * n : 3 * n]
    out_ref = refs[3 * n]
    half = out_ref.shape[0] // 2
    first = jnp.where(info_ref[0] < 2, 0, half)
    nt = ((1,), (1,))

    def step(c, carry):
        mine = jnp.concatenate([r[c] for r in own], axis=1)
        other = jnp.concatenate([r[c] for r in right], axis=1)
        out_ref[c, :, :BLK] = dot_dims(mine, mine, nt)
        out_ref[c, :, BLK : 2 * BLK] = dot_dims(mine, other, nt)
        return carry

    lax.fori_loop(0, 2 * half, step, 0)

    def step_across(c, carry):
        mine = jnp.concatenate([r[first + c] for r in own], axis=1)
        other = jnp.concatenate([r[c] for r in across], axis=1)
        out_ref[first + c, :, 2 * BLK :] = dot_dims(mine, other, nt)
        out_ref[half - first + c, :, 2 * BLK :] = jnp.zeros((BLK, BLK), F32)
        return carry

    lax.fori_loop(0, half, step_across, 0)


def make_products(row, own, right, across):
    count = own[0].shape[0]
    n = 3 * len(own)
    return pl.pallas_call(
        functools.partial(products_kernel, len(own)),
        in_specs=[pl.BlockSpec(memory_space=pltpu.SMEM)] + [pl.BlockSpec(memory_space=pltpu.VMEM)] * n,
        out_shape=jax.ShapeDtypeStruct((count, BLK, 3 * BLK), F32),
        compiler_params=pltpu.CompilerParams(vmem_limit_bytes=VMEM_LIMIT),
        name="products",
    )(row, *own, *right, *across)


def pack(block):
    lane = lax.broadcasted_iota(jnp.int32, (BLK, BLK), 1)
    row = lax.broadcasted_iota(jnp.int32, (BLK, BLK), 0)
    first = block[:, :BLK]
    hi = first.astype(BF16).astype(F32)
    rest = jnp.sum(jnp.where(lane == row, first - hi, 0.0), axis=1, keepdims=True)
    first = jnp.where(lane > row, 0.0, first)
    first = jnp.where(lane == row + 1, rest, first)
    last = jnp.sum(jnp.where((lane == row) & (row == BLK - 1), block[:, :BLK] - hi, 0.0), keepdims=True)
    first = jnp.where((row == 0) & (lane == BLK - 1), last, first)
    return jnp.concatenate([first, block[:, BLK:]], axis=1).astype(BF16)


def unpack(block):
    lane = lax.broadcasted_iota(jnp.int32, (BLK, BLK), 1)
    row = lax.broadcasted_iota(jnp.int32, (BLK, BLK), 0)
    block = block.astype(F32)
    first = block[:, :BLK]
    last = jnp.sum(jnp.where((row == 0) & (lane == BLK - 1), first, 0.0), keepdims=True)
    rest = jnp.sum(jnp.where(lane == row + 1, first, 0.0), axis=1, keepdims=True)
    rest = jnp.where((row == BLK - 1), last, rest)
    first = jnp.where(lane == row, first + rest, first)
    first = jnp.where(lane > row, 0.0, first)
    return jnp.concatenate([first, block[:, BLK:]], axis=1)


def scatter_kernel(info_ref, mine_ref, theirs_ref, own_ref, *rest):
    sends, acc = rest[:-1], rest[-1]
    core, y, ny = info_ref[0], info_ref[1], 4
    acc[...] = jnp.zeros_like(acc)
    count = mine_ref.shape[0]
    for which, ref in enumerate((mine_ref, theirs_ref)):

        def add(c, carry):
            p = info_ref[2 + which * count + c]

            @pl.when(lax.rem(p, 2) == core)
            def _():
                at = lax.div(p, 2)
                acc[at] += ref[c]

            return carry

        lax.fori_loop(0, count, add, 0)

    def emit(z, carry):
        for d in range(ny):
            block = acc[z * ny + lax.rem(y + d, ny)]
            if d == 0:
                own_ref[z] = block
            else:
                sends[d - 1][z] = pack(block)
        return carry

    lax.fori_loop(0, own_ref.shape[0], emit, 0)


def scatter(info, mine, theirs, nz, ny):
    shape = mine.shape[1:]
    return pl.pallas_call(
        scatter_kernel,
        in_specs=[pl.BlockSpec(memory_space=pltpu.SMEM)] + [pl.BlockSpec(memory_space=pltpu.VMEM)] * 2,
        out_shape=[jax.ShapeDtypeStruct((nz, *shape), F32)]
        + [jax.ShapeDtypeStruct((nz, *shape), BF16)] * (ny - 1),
        scratch_shapes=[pltpu.VMEM((nz * ny, *shape), F32)],
        compiler_params=pltpu.CompilerParams(vmem_limit_bytes=VMEM_LIMIT),
        name="scatter",
    )(info, mine, theirs)


def sum_y_kernel(info_ref, own_ref, *refs):
    ny, nz = 4, own_ref.shape[0]
    got, out_ref, sends = refs[: ny - 1], refs[ny - 1], refs[ny:]
    z = info_ref[0]
    for d in range(nz):
        at = lax.rem(z + d, nz)
        total = own_ref[at]
        for ref in got:
            total += unpack(ref[at])
        if d == 0:
            out_ref[...] = total
        else:
            sends[d - 1][...] = pack(total)


def sum_y(info, own, got):
    nz, *shape = own.shape
    return pl.pallas_call(
        sum_y_kernel,
        in_specs=[pl.BlockSpec(memory_space=pltpu.SMEM)] + [pl.BlockSpec(memory_space=pltpu.VMEM)] * 4,
        out_shape=[jax.ShapeDtypeStruct(tuple(shape), F32)]
        + [jax.ShapeDtypeStruct(tuple(shape), BF16)] * (nz - 1),
        compiler_params=pltpu.CompilerParams(vmem_limit_bytes=VMEM_LIMIT),
        name="sum_y",
    )(info, own, *got)


def sum_z_kernel(own_ref, *refs):
    got, out_ref = refs[:-1], refs[-1]
    total = own_ref[...]
    for ref in got:
        total += unpack(ref[...])
    for b in range(3):
        out_ref[b] = total[:, BLK * b : BLK * (b + 1)]


def sum_z(own, got):
    return pl.pallas_call(
        sum_z_kernel,
        out_shape=jax.ShapeDtypeStruct((3, BLK, BLK), F32),
        compiler_params=pltpu.CompilerParams(vmem_limit_bytes=VMEM_LIMIT),
        name="sum_z",
    )(own, *got)


def finish_kernel(info_ref, tile_ref, blocks_ref, left_ref, across_ref, out_ref):
    row, n = info_ref[0], 4
    r = lax.broadcasted_iota(jnp.int32, (BLK, BLK), 0)
    c = lax.broadcasted_iota(jnp.int32, (BLK, BLK), 1)
    low = blocks_ref[0]
    diag = jnp.where(c > r, low.T, low)

    def put(at, value):
        cols = pl.ds(pl.multiple_of(at * BLK, BLK), BLK)
        out_ref[:, cols] = tile_ref[:, cols] - value

    put(row, diag)
    put(lax.rem(row + 1, n), blocks_ref[1])
    put(lax.rem(row + 3, n), left_ref[...].T)
    put(lax.rem(row + 2, n), blocks_ref[2] + across_ref[...].T)


def finish(info, tile, blocks, left, across):
    return pl.pallas_call(
        finish_kernel,
        in_specs=[pl.BlockSpec(memory_space=pltpu.SMEM)] + [pl.BlockSpec(memory_space=pltpu.VMEM)] * 4,
        out_shape=jax.ShapeDtypeStruct(tile.shape, F32),
        name="finish",
    )(info, tile, blocks, left, across)


def ring(n, d):
    return [(i, (i + d) % n) for i in range(n)]


def on_device(diag_blocks, panel_blocks, ancestors, target_ids, target_tiles):
    nz, ny = lax.axis_size("z"), lax.axis_size("y")
    sn, anc, rows, width = panel_blocks.shape
    count = sn * anc
    z, y, core, row = (lax.axis_index(a).astype(jnp.int32) for a in ("z", "y", "core", "row"))
    at_row = row[None]
    panel = panel_blocks.reshape(sn, anc * rows, width)
    w_prev, own, right, across, solved = [], [], [], [], None
    for k in range(width // BLK):
        w = factor_rows(k, diag_blocks, w_prev)
        if k >= 1:
            w, right[k - 1], across[k - 1] = lax.optimization_barrier(
                (w, right[k - 1], across[k - 1])
            )
        w_prev.append(w)
        solved, rounded, half = solve_chunk(k, at_row, w, panel, solved)
        rounded = rounded.reshape(count, rows, BLK)
        own.append(rounded)
        right.append(lax.ppermute(rounded, "row", ring(4, -1)))
        across.append(lax.ppermute(half.reshape(count // sn, rows, BLK), "row", ring(4, 2)))

    target_ids, own[-1] = lax.optimization_barrier((target_ids, own[-1]))
    all_ids = lax.all_gather(target_ids, COL, axis=0, tiled=True)
    matches = ancestors.reshape(count)[:, None] == all_ids[None, :]
    places = jnp.arange(all_ids.shape[0], dtype=jnp.int32)
    position = jnp.sum(jnp.where(matches, places[None, :], 0), axis=1).astype(jnp.int32)
    their_position = lax.ppermute(position, "core", ring(2, 1))
    at_row, their_position = lax.optimization_barrier((at_row, their_position))
    products = make_products(at_row, own, right, across)
    their_products = lax.ppermute(products, "core", ring(2, 1))
    info = jnp.concatenate([core[None], y[None], position, their_position])
    mine, *sends = scatter(info, products, their_products, nz, ny)
    got = [lax.ppermute(s, "y", ring(ny, d + 1)) for d, s in enumerate(sends)]
    mine, *sends = sum_y(z[None], mine, got)
    got = [lax.ppermute(s, "z", ring(nz, d + 1)) for d, s in enumerate(sends)]
    blocks = sum_z(mine, got)
    from_left = lax.ppermute(blocks[1], "row", ring(4, 1))
    from_across = lax.ppermute(blocks[2], "row", ring(4, 2))
    updated = finish(at_row, target_tiles.reshape(rows, width), blocks, from_left, from_across)
    return solved.reshape(panel_blocks.shape), updated.reshape(target_tiles.shape)


def solution(mesh):
    devices = mesh.devices
    nz, ny = 8, 4
    fine = Mesh(devices.reshape(nz, ny, 2, devices.shape[1]), ("z", "y", "core", "row"))
    in_specs = (
        P(COL, None, None),
        P(COL, None, "row", None),
        P(COL, None),
        P(COL),
        P(COL, "row", None),
    )
    out_specs = (P(COL, None, "row", None), P(COL, "row", None))
    return jax.shard_map(
        on_device, mesh=fine, in_specs=in_specs, out_specs=out_specs, check_vma=False
    )
```

```python
import functools

import jax
import jax.numpy as jnp
from jax import lax
from jax.experimental import pallas as pl
from jax.experimental.pallas import tpu as pltpu
from jax.sharding import Mesh, PartitionSpec as P

F32 = jnp.float32
BF16 = jnp.bfloat16
BLK = 128
CHUNK = 256
PAN = 16
VMEM_LIMIT = 48 * 1024 * 1024
COL = ("z", "y", "core")
COST = pl.CostEstimate(flops=10**6, bytes_accessed=10**4, transcendentals=0)


def split3(x):
    a = x.astype(BF16)
    rest = x - a.astype(F32)
    b = rest.astype(BF16)
    c = (rest - b.astype(F32)).astype(BF16)
    return a, b, c


def split2(x):
    a = x.astype(BF16)
    return a, (x - a.astype(F32)).astype(BF16)


def outer_product(left, right):
    a, b, c = split3(left)
    p, q, r = split3(right)
    return lax.dot_general(
        jnp.concatenate([a, a, a, b, b, c], axis=0),
        jnp.concatenate([p, q, r, p, q, p], axis=0),
        (((0,), (0,)), ((), ())),
        preferred_element_type=F32,
    )


def dot_dims(a, b, dims, precision=None):
    return lax.dot_general(a, b, (dims, ((), ())), precision=precision, preferred_element_type=F32)


def refined_reciprocal(d):
    r = pl.reciprocal(d, approx=True)
    r = r * (2.0 - d * r)
    return r * (2.0 - d * r)


def factor_panel(panel, k):
    half = PAN // 2
    lane1 = lax.broadcasted_iota(jnp.int32, (1, BLK), 1)
    sub = lax.broadcasted_iota(jnp.int32, (half, BLK), 0)
    lane = lax.broadcasted_iota(jnp.int32, (half, BLK), 1)
    top, bot = panel[:half], panel[half:]
    tops = [jnp.broadcast_to(top[:, k + c : k + c + 1], (half, BLK)) for c in range(PAN)]
    bots = [jnp.broadcast_to(bot[:, k + c : k + c + 1], (half, BLK)) for c in range(PAN)]
    diag_top = jnp.ones((half, BLK), F32)
    diag_bot = jnp.ones((half, BLK), F32)
    for i in range(PAN):
        if i < half:
            d = tops[i][i : i + 1]
            r = refined_reciprocal(d)
            mt = jnp.where(sub > i, tops[i] * r, 0.0)
            mb = bots[i] * r
            diag_top = jnp.where(sub == i, d, diag_top)
            for c in range(i + 1, PAN):
                row = tops[c][i : i + 1]
                tops[c] = tops[c] - mt * row
                bots[c] = bots[c] - mb * row
            pivot = top[i : i + 1] + jnp.where(lane1 == k + i, 1.0, 0.0)
            top = top - mt * pivot
            bot = bot - mb * pivot
        else:
            h = i - half
            d = bots[i][h : h + 1]
            r = refined_reciprocal(d)
            mb = jnp.where(sub > h, bots[i] * r, 0.0)
            diag_bot = jnp.where(sub == h, d, diag_bot)
            for c in range(i + 1, PAN):
                bots[c] = bots[c] - mb * bots[c][h : h + 1]
            pivot = bot[h : h + 1] + jnp.where(lane1 == k + i, 1.0, 0.0)
            bot = bot - mb * pivot

    def finish(rows, diag, first):
        at = lane - k - first
        rows = jnp.where(at == sub, 1.0, jnp.where((at > sub) & (lane < k + PAN), 0.0, rows))
        return rows * lax.rsqrt(diag)

    return jnp.concatenate([finish(top, diag_top, 0), finish(bot, diag_bot, half)], axis=0)


def factor_blocks(blocks):
    mats = list(blocks)
    done = [[] for _ in mats]
    for k in range(0, BLK, PAN):
        lane = lax.broadcasted_iota(jnp.int32, (PAN, BLK), 1)
        for s in range(len(mats)):
            rows = factor_panel(mats[s][:PAN], k)
            done[s].append(jnp.where(lane < k + PAN, rows, 0.0))
            if k + PAN < BLK:
                ahead = jnp.where(lane >= k + PAN, rows, 0.0)
                rest = mats[s][PAN:]
                at = lax.broadcasted_iota(jnp.int32, rest.shape, 1)
                rest = jnp.where((at >= k) & (at < k + PAN), 0.0, rest)
                mats[s] = rest - outer_product(ahead, rows)[k + PAN :]
    return [jnp.concatenate(rows, axis=0) for rows in done]


def factor_rows(k, s, row, w_prev):
    if not k:
        return row
    lane = lax.broadcasted_iota(jnp.int32, row.shape, 1)
    left = jnp.concatenate([w[:, BLK * k : BLK * (k + 1)] for w in w_prev], axis=0)
    right = jnp.concatenate(
        [jnp.where((lane >= BLK * (i + 1)) & (lane < BLK * k), 0.0, w) for i, w in enumerate(w_prev)],
        axis=0,
    )
    row = jnp.where(lane < BLK * k, 0.0, row)
    return row - dot_dims(left, right, ((0,), (0,)), lax.Precision.HIGHEST)


def factor_part(chunk, sn, diag_ref, w_old, w_ref):
    per = CHUNK // BLK
    width = diag_ref.shape[2]
    w_prev = [[w_old[s, BLK * i : BLK * (i + 1), :] for i in range(per * chunk)] for s in range(sn)]
    for at in range(per):
        k = per * chunk + at
        here = slice(BLK * k, BLK * (k + 1))
        rows = [
            factor_rows(k, s, diag_ref[s, BLK * at : BLK * (at + 1), :], w_prev[s]) for s in range(sn)
        ]
        inverses = factor_blocks([row[:, here] for row in rows])
        for s in range(sn):
            scaled = dot_dims(inverses[s], rows[s], ((1,), (0,)), lax.Precision.HIGHEST)
            lane = lax.broadcasted_iota(jnp.int32, (BLK, width), 1)
            inside = (lane >= BLK * k) & (lane < BLK * (k + 1))
            spread = jnp.concatenate([inverses[s]] * (width // BLK), axis=1)
            scaled = jnp.where(inside, spread, scaled)
            w_prev[s].append(scaled)
            w_ref[s, BLK * at : BLK * (at + 1), :] = scaled


def solve_part(chunk, sn, info_ref, w_ref, b_ref, x_ref, r_refs, half_ref):
    used = CHUNK * (chunk + 1)
    tile = 256
    nt = ((1,), (1,))
    for s in range(sn):
        lane = lax.broadcasted_iota(jnp.int32, (CHUNK, used), 1)
        row = lax.broadcasted_iota(jnp.int32, (CHUNK, used), 0) + CHUNK * chunk
        w_hi, w_lo = split2(jnp.where(lane <= row, w_ref[s, :, :used], 0.0))

        def step(t, carry):
            at = pl.ds(pl.multiple_of(t * tile, tile), tile)
            b_hi, b_lo = split2(b_ref[s, at, :])
            x = dot_dims(b_hi, w_hi, nt) + (dot_dims(b_hi, w_lo, nt) + dot_dims(b_lo, w_hi, nt))
            x_ref[s, at, :] = x
            r_refs[s][at, :] = x.astype(BF16)
            return carry

        lax.fori_loop(0, b_ref.shape[1] // tile, step, 0, unroll=2)
    half_ref[...] = jnp.where(info_ref[0] < 2, r_refs[1][...], r_refs[0][...])


def first_kernel(sn, info_ref, diag_ref, b_hbm, w_ref, x_ref, *refs):
    r_refs, (half_ref, b_ref, sem) = refs[:sn], refs[sn:]
    copy = pltpu.make_async_copy(b_hbm.at[:, :, pl.ds(0, CHUNK)], b_ref, sem)
    copy.start()
    factor_part(0, sn, diag_ref, None, w_ref)
    copy.wait()
    solve_part(0, sn, info_ref, w_ref, b_ref, x_ref, r_refs, half_ref)


def second_kernel(sn, info_ref, w_ref, *refs):
    own_refs, (b_ref, _, x_ref), refs = refs[:sn], refs[sn : sn + 3], refs[sn + 3 :]
    r_ref, half_ref, diag_ref = refs
    r_refs = [r_ref.at[s] for s in range(sn)]
    solve_part(1, sn, info_ref, w_ref, b_ref, x_ref, r_refs, half_ref)
    anc = b_ref.shape[1] // BLK

    for s in range(sn):

        def square(c, carry):
            at = pl.ds(pl.multiple_of(c * BLK, BLK), BLK)
            mine = jnp.concatenate([own_refs[s][c], r_refs[s][at, :]], axis=1)
            diag_ref[s * anc + c] = dot_dims(mine, mine, ((1,), (1,)))
            return carry

        lax.fori_loop(0, anc, square, 0, unroll=4)


def whole(shape):
    return pl.BlockSpec(shape, lambda i: (0,) * len(shape))


def grid_call(kernel, args, in_specs, outs, name, scratch=(), aliases={}):
    return pl.pallas_call(
        kernel,
        grid=(1,),
        in_specs=in_specs,
        out_specs=[spec for spec, _ in outs],
        out_shape=[shape for _, shape in outs],
        scratch_shapes=list(scratch),
        input_output_aliases=aliases,
        compiler_params=pltpu.CompilerParams(vmem_limit_bytes=VMEM_LIMIT),
        cost_estimate=COST,
        name=name,
    )(*args)


def chunk_outs(chunk, sn, rows, width):
    outs = [(pl.BlockSpec((sn, rows, CHUNK), lambda i: (0, 0, chunk)), f32_out(sn, rows, width))]
    shapes = [(sn, rows, CHUNK)] if chunk else [(rows, CHUNK)] * sn
    return outs + [(whole(shape), bf16_out(*shape)) for shape in shapes + [(rows, CHUNK)]]


def diag_rows(chunk, sn, width):
    return pl.BlockSpec((sn, CHUNK, width), lambda i: (0, chunk, 0))


SMEM_SPEC = pl.BlockSpec(memory_space=pltpu.SMEM)
ANY_SPEC = pl.BlockSpec(memory_space=pl.ANY)


def first_chunk(row, diag_blocks, panel):
    sn, rows, width = panel.shape
    return grid_call(
        functools.partial(first_kernel, sn),
        [row, diag_blocks, panel],
        [SMEM_SPEC, diag_rows(0, sn, width), ANY_SPEC],
        [(whole((sn, CHUNK, width)), f32_out(sn, CHUNK, width))] + chunk_outs(0, sn, rows, width),
        "first_chunk",
        [pltpu.VMEM((sn, rows, CHUNK), F32), pltpu.SemaphoreType.DMA],
    )


def second_factor(diag_blocks, w):
    sn, _, width = diag_blocks.shape
    return grid_call(
        functools.partial(factor_part, 1, sn),
        [diag_blocks, w],
        [diag_rows(1, sn, width), whole(w.shape)],
        [(whole(w.shape), f32_out(*w.shape))],
        "second_factor",
    )[0]


def second_chunk(row, w, own, panel, solved):
    sn, rows, width = panel.shape
    count = sn * own[0].shape[0]
    return grid_call(
        functools.partial(second_kernel, sn),
        [row, w, *own, panel, solved],
        [SMEM_SPEC, whole(w.shape)] + [whole(o.shape) for o in own] + [whole(panel.shape), ANY_SPEC],
        chunk_outs(1, sn, rows, width) + [(whole((count, BLK, BLK)), f32_out(count, BLK, BLK))],
        "second_chunk",
        aliases={3 + sn: 0},
    )


def call(kernel, args, out_shape, scratch=(), name=None, smem=1, **kwargs):
    specs = [pl.BlockSpec(memory_space=pltpu.SMEM)] * smem
    specs += [pl.BlockSpec(memory_space=pltpu.VMEM)] * (len(args) - smem)
    return pl.pallas_call(
        kernel,
        in_specs=specs,
        out_shape=out_shape,
        scratch_shapes=list(scratch),
        compiler_params=pltpu.CompilerParams(vmem_limit_bytes=VMEM_LIMIT),
        cost_estimate=COST,
        name=name,
        **kwargs,
    )(*args)


def products_kernel(n, more, info_ref, *refs):
    own, right_in, refs = refs[:n], refs[n : 2 * n], refs[2 * n :]
    across_in, accs, (right_ref, across_ref) = refs[0], refs[1 : 1 + 2 * more], refs[1 + 2 * more :]
    half, sn = across_ref.shape[0], right_ref.shape[0] // across_ref.shape[0]
    nt = ((1,), (1,))
    own = own if n == sn else [own[0].at[pl.ds(s * half, half)] for s in range(sn)]
    right_in = right_in if n == sn else [right_in[0].at[pl.ds(s * half, half)] for s in range(sn)]
    for s in range(sn):

        def step(c, carry):
            product = dot_dims(own[s][c], right_in[s][c], nt)
            right_ref[s * half + c] = accs[0][s * half + c] + product if more else product
            return carry

        lax.fori_loop(0, half, step, 0, unroll=4)

        def step_across(c, carry):
            product = dot_dims(own[s][c], across_in[c], nt)
            across_ref[c] = accs[1][c] + product if more else product
            return carry

        @pl.when((info_ref[0] < 2) == (s == 0))
        def _():
            lax.fori_loop(0, half, step_across, 0, unroll=4)


def multiply(row, own, right, across, accs=()):
    half, count = across.shape[0], len(own) * own[0].shape[0]
    return call(
        functools.partial(products_kernel, len(own), len(accs) > 0),
        [row, *own, *right, across, *accs],
        [f32_out(count, BLK, BLK), f32_out(half, BLK, BLK)],
        name="products",
    )


def pack(block):
    lane = lax.broadcasted_iota(jnp.int32, (BLK, BLK), 1)
    row = lax.broadcasted_iota(jnp.int32, (BLK, BLK), 0)
    first = block
    hi = first.astype(BF16).astype(F32)
    rest = jnp.sum(jnp.where(lane == row, first - hi, 0.0), axis=1, keepdims=True)
    first = jnp.where(lane > row, 0.0, first)
    first = jnp.where(lane == row + 1, rest, first)
    last = jnp.sum(jnp.where((lane == row) & (row == BLK - 1), block - hi, 0.0), keepdims=True)
    first = jnp.where((row == 0) & (lane == BLK - 1), last, first)
    return first.astype(BF16)


def unpack(block):
    lane = lax.broadcasted_iota(jnp.int32, (BLK, BLK), 1)
    row = lax.broadcasted_iota(jnp.int32, (BLK, BLK), 0)
    first = block.astype(F32)
    last = jnp.sum(jnp.where((row == 0) & (lane == BLK - 1), first, 0.0), keepdims=True)
    rest = jnp.sum(jnp.where(lane == row + 1, first, 0.0), axis=1, keepdims=True)
    rest = jnp.where((row == BLK - 1), last, rest)
    first = jnp.where(lane == row, first + rest, first)
    first = jnp.where(lane > row, 0.0, first)
    return first


def add_blocks(info_ref, offset, ref, acc, lanes):
    core = info_ref[0]

    def add(c, carry):
        p = info_ref[offset + c]

        @pl.when(lax.rem(p, 2) == core)
        def _():
            at = lax.div(p, 2)
            acc[at, :, lanes] += ref[c]

        return carry

    lax.fori_loop(0, ref.shape[0], add, 0)


def scatter_diag_kernel(ny, info_ref, mine_ref, theirs_ref, own_ref, *rest):
    sends, acc = rest[:-1], rest[-1]
    y, count = info_ref[1], mine_ref.shape[0]
    acc[...] = jnp.zeros_like(acc)
    add_blocks(info_ref, 4, mine_ref, acc, slice(None))
    add_blocks(info_ref, 4 + count, theirs_ref, acc, slice(None))

    def emit(z, carry):
        for d in range(ny):
            block = acc[z * ny + lax.rem(y + d, ny)]
            if d == 0:
                own_ref[z] = block
            else:
                sends[d - 1][z] = pack(block)
        return carry

    lax.fori_loop(0, own_ref.shape[0], emit, 0)


def scatter_off_kernel(ny, info_ref, mine_ref, across_ref, theirs_ref, their_across_ref, own_ref, *rest):
    sends, acc = rest[:-1], rest[-1]
    y, count = info_ref[1], mine_ref.shape[0]
    half = across_ref.shape[0]
    first = jnp.where(info_ref[3] < 2, 0, half)
    acc[...] = jnp.zeros_like(acc)
    for which, (right, across) in enumerate(((mine_ref, across_ref), (theirs_ref, their_across_ref))):
        add_blocks(info_ref, 4 + count * which, right, acc, slice(0, BLK))
        add_blocks(info_ref, 4 + count * which + first, across, acc, slice(BLK, 2 * BLK))

    def emit(z, carry):
        for d in range(ny):
            block = acc[z * ny + lax.rem(y + d, ny)]
            if d == 0:
                own_ref[z] = block
            else:
                sends[d - 1][z] = block.astype(BF16)
        return carry

    lax.fori_loop(0, own_ref.shape[0], emit, 0)


def sum_diag_kernel(info_ref, own_ref, *refs):
    got, out_ref, send_ref = refs[:-2], refs[-2], refs[-1]
    z = info_ref[2]

    def step(at, carry):
        total = own_ref[at]
        for ref in got:
            total += unpack(ref[at])
        send_ref[at] = pack(total)

        @pl.when(at == z)
        def _():
            out_ref[...] = total

        return carry

    lax.fori_loop(0, own_ref.shape[0], step, 0)


def sum_off_kernel(info_ref, own_ref, *refs):
    nz = own_ref.shape[0]
    got, out_ref, sends = refs[:-nz], refs[-nz], refs[len(refs) - nz + 1 :]
    z = info_ref[2]
    for d in range(nz):
        at = lax.rem(z + d, nz)
        total = own_ref[at]
        for ref in got:
            total += ref[at].astype(F32)
        if d == 0:
            out_ref[...] = total
        else:
            sends[d - 1][...] = total.astype(BF16)


def last_sum_kernel(own_ref, *refs):
    got, outs = refs[:-2], refs[-2:]
    total = own_ref[...]
    for ref in got:
        total += ref[...].astype(F32)
    for b, ref in enumerate(outs):
        ref[...] = total[:, BLK * b : BLK * (b + 1)]


def finish_kernel(info_ref, tile_ref, diag_ref, got_ref, right_ref, across_ref, left_in, across_in, out_ref):
    row, z, n = info_ref[3], info_ref[2], 4
    r = lax.broadcasted_iota(jnp.int32, (BLK, BLK), 0)
    c = lax.broadcasted_iota(jnp.int32, (BLK, BLK), 1)

    def step(at, low):
        return low + jnp.where(at == z, 0.0, unpack(got_ref[at]))

    low = lax.fori_loop(0, got_ref.shape[0], step, diag_ref[...])

    def put(at, value):
        cols = pl.ds(pl.multiple_of(at * BLK, BLK), BLK)
        out_ref[:, cols] = tile_ref[:, cols] - value

    put(row, jnp.where(c > r, low.T, low))
    put(lax.rem(row + 1, n), right_ref[...])
    put(lax.rem(row + 3, n), left_in[...].T)
    put(lax.rem(row + 2, n), across_ref[...] + across_in[...].T)


def after(value, *deps):
    return lax.optimization_barrier((value, *deps))[0]


def ring(n, d):
    return [(i, (i + d) % n) for i in range(n)]


def f32_out(*shape):
    return jax.ShapeDtypeStruct(shape, F32)


def bf16_out(*shape):
    return jax.ShapeDtypeStruct(shape, BF16)


def on_device(diag_blocks, panel_blocks, ancestors, target_ids, target_tiles):
    nz, ny = lax.axis_size("z"), lax.axis_size("y")
    sn, anc, rows, width = panel_blocks.shape
    count = sn * anc
    half = count // sn
    z, y, core, row = (lax.axis_index(a).astype(jnp.int32) for a in ("z", "y", "core", "row"))
    at_row = row[None]
    panel = panel_blocks.reshape(sn, anc * rows, width)

    names = ancestors.reshape(count)
    known = jnp.concatenate([jnp.broadcast_to(target_ids, (128,)), jnp.pad(names, (0, 128 - count))])
    known = jnp.pad(known.reshape(2, 128), ((0, 62), (0, 0)))
    known = lax.all_gather(known[None], COL, axis=0, tiled=True)

    def send(blocks, distance):
        return lax.ppermute(blocks, "row", ring(4, distance))

    def by_block(parts):
        return [part.reshape(-1, rows, CHUNK) for part in parts]

    w, solved, *parts = first_chunk(at_row, diag_blocks, panel)
    *own_0, part = by_block(parts)
    hop = send(part, 1)
    right_0 = [send(o, -1) for o in own_0]
    w = second_factor(diag_blocks, w)
    w, hop, right_0[0] = lax.optimization_barrier((w, hop, right_0[0]))
    solved, *parts, diag = second_chunk(at_row, w, own_0, panel, solved)
    across_0 = send(hop, 1)
    *own_1, part = by_block(parts)
    hop = send(part, 1)
    right_1 = [send(o, -1) for o in own_1]
    diag = after(diag, across_0, right_0[1])
    their_diag = lax.ppermute(diag, "core", ring(2, 1))
    accs = multiply(at_row, own_0, right_0, across_0)
    known = after(known, accs[0])
    ids = known[:, 0, 0]
    their_names = known[(z * ny + y) * 2 + 1 - core, 1, :count]
    places = jnp.arange(ids.shape[0], dtype=jnp.int32)
    both = jnp.concatenate([names, their_names])
    position = jnp.sum(jnp.where(both[:, None] == ids[None, :], places[None, :], 0), axis=1)
    info = jnp.concatenate([jnp.stack([core, y, z, row]), position.astype(jnp.int32)])

    own_diag, *sends = call(
        functools.partial(scatter_diag_kernel, ny),
        [after(info, accs[0]), diag, their_diag],
        [f32_out(nz, BLK, BLK)] + [bf16_out(nz, BLK, BLK)] * (ny - 1),
        [pltpu.VMEM((nz * ny, BLK, BLK), F32)],
        name="scatter_diag",
    )
    got_diag = [lax.ppermute(s, "y", ring(ny, d + 1)) for d, s in enumerate(sends)]
    across_1 = send(after(hop, own_diag), 1)

    off_right, off_across = multiply(after(at_row, *got_diag), own_1, right_1, across_1, accs)
    their_right = lax.ppermute(off_right, "core", ring(2, 1))
    their_across = lax.ppermute(off_across, "core", ring(2, 1))
    own_off, *sends = call(
        functools.partial(scatter_off_kernel, ny),
        [info, off_right, off_across, their_right, their_across],
        [f32_out(nz, BLK, 2 * BLK)] + [bf16_out(nz, BLK, 2 * BLK)] * (ny - 1),
        [pltpu.VMEM((nz * ny, BLK, 2 * BLK), F32)],
        name="scatter_off",
    )
    got_off = [lax.ppermute(s, "y", ring(ny, d + 1)) for d, s in enumerate(sends)]

    own_diag, send = call(
        sum_diag_kernel,
        [after(info, own_off), own_diag, *got_diag],
        [f32_out(BLK, BLK), bf16_out(nz, BLK, BLK)],
        name="sum_diag",
    )
    got_diag = lax.all_to_all(send, "z", 0, 0, tiled=True)
    own_off, *sends = call(
        sum_off_kernel,
        [after(info, got_diag), own_off, *got_off],
        [f32_out(BLK, 2 * BLK)] + [bf16_out(BLK, 2 * BLK)] * (nz - 1),
        name="sum_off",
    )
    got_off = [lax.ppermute(s, "z", ring(nz, d + 1)) for d, s in enumerate(sends)]
    off_right, off_across = call(
        last_sum_kernel, [own_off, *got_off], [f32_out(BLK, BLK)] * 2, name="last_sum", smem=0
    )
    from_left = lax.ppermute(off_right, "row", ring(4, 1))
    from_across = lax.ppermute(off_across, "row", ring(4, 2))
    updated = call(
        finish_kernel,
        [info, target_tiles.reshape(rows, width), own_diag, got_diag]
        + [off_right, off_across, from_left, from_across],
        f32_out(rows, width),
        name="finish",
    )
    return solved.reshape(panel_blocks.shape), updated.reshape(target_tiles.shape)


def solution(mesh):
    devices = mesh.devices
    nz, ny = 8, 4
    fine = Mesh(devices.reshape(nz, ny, 2, devices.shape[1]), ("z", "y", "core", "row"))
    in_specs = (
        P(COL, None, None),
        P(COL, None, "row", None),
        P(COL, None),
        P(COL),
        P(COL, "row", None),
    )
    out_specs = (P(COL, None, "row", None), P(COL, "row", None))
    return jax.shard_map(
        on_device, mesh=fine, in_specs=in_specs, out_specs=out_specs, check_vma=False
    )
```

```python
import functools

import jax
import jax.numpy as jnp
from jax import lax
from jax.experimental import pallas as pl
from jax.experimental.pallas import tpu as pltpu
from jax.sharding import Mesh, PartitionSpec as P

F32 = jnp.float32
BF16 = jnp.bfloat16
BLK = 128
CHUNK = 256
PAN = 16
VMEM_LIMIT = 24 * 1024 * 1024
SMALL_LIMIT = 8 * 1024 * 1024
COL = ("z", "y", "core")
COST = pl.CostEstimate(flops=10**6, bytes_accessed=10**4, transcendentals=0)


def split3(x):
    a = x.astype(BF16)
    rest = x - a.astype(F32)
    b = rest.astype(BF16)
    c = (rest - b.astype(F32)).astype(BF16)
    return a, b, c


def split2(x):
    a = x.astype(BF16)
    return a, (x - a.astype(F32)).astype(BF16)


def outer_product(left, right):
    a, b, c = split3(left)
    p, q, r = split3(right)
    return lax.dot_general(
        jnp.concatenate([a, a, a, b, b, c], axis=0),
        jnp.concatenate([p, q, r, p, q, p], axis=0),
        (((0,), (0,)), ((), ())),
        preferred_element_type=F32,
    )


def dot_dims(a, b, dims, precision=None):
    return lax.dot_general(a, b, (dims, ((), ())), precision=precision, preferred_element_type=F32)


def refined_reciprocal(d):
    r = pl.reciprocal(d, approx=True)
    r = r * (2.0 - d * r)
    return r * (2.0 - d * r)


def factor_panel(panel, k):
    half = PAN // 2
    lane1 = lax.broadcasted_iota(jnp.int32, (1, BLK), 1)
    sub = lax.broadcasted_iota(jnp.int32, (half, BLK), 0)
    lane = lax.broadcasted_iota(jnp.int32, (half, BLK), 1)
    top, bot = panel[:half], panel[half:]
    tops = [jnp.broadcast_to(top[:, k + c : k + c + 1], (half, BLK)) for c in range(PAN)]
    bots = [jnp.broadcast_to(bot[:, k + c : k + c + 1], (half, BLK)) for c in range(PAN)]
    diag_top = jnp.ones((half, BLK), F32)
    diag_bot = jnp.ones((half, BLK), F32)
    for i in range(PAN):
        if i < half:
            d = tops[i][i : i + 1]
            r = refined_reciprocal(d)
            mt = jnp.where(sub > i, tops[i] * r, 0.0)
            mb = bots[i] * r
            diag_top = jnp.where(sub == i, d, diag_top)
            for c in range(i + 1, PAN):
                row = tops[c][i : i + 1]
                tops[c] = tops[c] - mt * row
                bots[c] = bots[c] - mb * row
            pivot = top[i : i + 1] + jnp.where(lane1 == k + i, 1.0, 0.0)
            top = top - mt * pivot
            bot = bot - mb * pivot
        else:
            h = i - half
            d = bots[i][h : h + 1]
            r = refined_reciprocal(d)
            mb = jnp.where(sub > h, bots[i] * r, 0.0)
            diag_bot = jnp.where(sub == h, d, diag_bot)
            for c in range(i + 1, PAN):
                bots[c] = bots[c] - mb * bots[c][h : h + 1]
            pivot = bot[h : h + 1] + jnp.where(lane1 == k + i, 1.0, 0.0)
            bot = bot - mb * pivot

    def finish(rows, diag, first):
        at = lane - k - first
        rows = jnp.where(at == sub, 1.0, jnp.where((at > sub) & (lane < k + PAN), 0.0, rows))
        return rows * lax.rsqrt(diag)

    return jnp.concatenate([finish(top, diag_top, 0), finish(bot, diag_bot, half)], axis=0)


def factor_blocks(blocks):
    mats = list(blocks)
    done = [[] for _ in mats]
    for k in range(0, BLK, PAN):
        lane = lax.broadcasted_iota(jnp.int32, (PAN, BLK), 1)
        for s in range(len(mats)):
            rows = factor_panel(mats[s][:PAN], k)
            done[s].append(jnp.where(lane < k + PAN, rows, 0.0))
            if k + PAN < BLK:
                ahead = jnp.where(lane >= k + PAN, rows, 0.0)
                rest = mats[s][PAN:]
                at = lax.broadcasted_iota(jnp.int32, rest.shape, 1)
                rest = jnp.where((at >= k) & (at < k + PAN), 0.0, rest)
                mats[s] = rest - outer_product(ahead, rows)[k + PAN :]
    return [jnp.concatenate(rows, axis=0) for rows in done]


def factor_rows(k, s, row, w_prev):
    if not k:
        return row
    lane = lax.broadcasted_iota(jnp.int32, row.shape, 1)
    left = jnp.concatenate([w[:, BLK * k : BLK * (k + 1)] for w in w_prev], axis=0)
    right = jnp.concatenate(
        [jnp.where((lane >= BLK * (i + 1)) & (lane < BLK * k), 0.0, w) for i, w in enumerate(w_prev)],
        axis=0,
    )
    row = jnp.where(lane < BLK * k, 0.0, row)
    return row - dot_dims(left, right, ((0,), (0,)), lax.Precision.HIGHEST)


def factor_part(chunk, sn, diag_ref, w_old, w_ref):
    per = CHUNK // BLK
    width = diag_ref.shape[2]
    w_prev = [[w_old[s, BLK * i : BLK * (i + 1), :] for i in range(per * chunk)] for s in range(sn)]
    for at in range(per):
        k = per * chunk + at
        here = slice(BLK * k, BLK * (k + 1))
        rows = [
            factor_rows(k, s, diag_ref[s, BLK * at : BLK * (at + 1), :], w_prev[s]) for s in range(sn)
        ]
        inverses = factor_blocks([row[:, here] for row in rows])
        for s in range(sn):
            scaled = dot_dims(inverses[s], rows[s], ((1,), (0,)), lax.Precision.HIGHEST)
            lane = lax.broadcasted_iota(jnp.int32, (BLK, width), 1)
            inside = (lane >= BLK * k) & (lane < BLK * (k + 1))
            spread = jnp.concatenate([inverses[s]] * (width // BLK), axis=1)
            scaled = jnp.where(inside, spread, scaled)
            w_prev[s].append(scaled)
            w_ref[s, BLK * at : BLK * (at + 1), :] = scaled


def solve_part(chunk, sn, info_ref, w_ref, b_ref, x_ref, r_refs, half_ref):
    used = CHUNK * (chunk + 1)
    tile = 256
    nt = ((1,), (1,))
    for s in range(sn):
        lane = lax.broadcasted_iota(jnp.int32, (CHUNK, used), 1)
        row = lax.broadcasted_iota(jnp.int32, (CHUNK, used), 0) + CHUNK * chunk
        w_hi, w_lo = split2(jnp.where(lane <= row, w_ref[s, :, :used], 0.0))

        def step(t, carry):
            at = pl.ds(pl.multiple_of(t * tile, tile), tile)
            b_hi, b_lo = split2(b_ref[s, at, :])
            x = dot_dims(b_hi, w_hi, nt) + (dot_dims(b_hi, w_lo, nt) + dot_dims(b_lo, w_hi, nt))
            x_ref[s, at, :] = x
            r_refs[s][at, :] = x.astype(BF16)
            return carry

        lax.fori_loop(0, b_ref.shape[1] // tile, step, 0, unroll=True)
    half_ref[...] = jnp.where(info_ref[0] < 2, r_refs[1][...], r_refs[0][...])


def first_kernel(sn, info_ref, diag_ref, b_hbm, w_ref, x_ref, *refs):
    r_refs, (half_ref, b_ref, sem) = refs[:sn], refs[sn:]
    copy = pltpu.make_async_copy(b_hbm.at[:, :, pl.ds(0, CHUNK)], b_ref, sem)
    copy.start()
    factor_part(0, sn, diag_ref, None, w_ref)
    copy.wait()
    solve_part(0, sn, info_ref, w_ref, b_ref, x_ref, r_refs, half_ref)


def second_kernel(sn, n_deps, info_ref, w_ref, *refs):
    own_refs, b_ref, refs = refs[:sn], refs[sn], refs[sn + 2 + n_deps :]
    x_ref, *refs = refs
    r_ref, half_ref, diag_ref, packed_ref = refs
    r_refs = [r_ref.at[s] for s in range(sn)]
    solve_part(1, sn, info_ref, w_ref, b_ref, x_ref, r_refs, half_ref)
    anc = b_ref.shape[1] // BLK

    for s in range(sn):

        def square(c, carry):
            at = pl.ds(pl.multiple_of(c * BLK, BLK), BLK)
            mine = jnp.concatenate([own_refs[s][c], r_refs[s][at, :]], axis=1)
            product = dot_dims(mine, mine, ((1,), (1,)))
            diag_ref[s * anc + c] = product
            packed_ref[s * anc + c] = pack(product)
            return carry

        lax.fori_loop(0, anc, square, 0, unroll=4)


def whole(shape):
    return pl.BlockSpec(shape, lambda i: (0,) * len(shape))


def grid_call(kernel, args, in_specs, outs, name, scratch=(), aliases={}):
    return pl.pallas_call(
        kernel,
        grid=(1,),
        in_specs=in_specs,
        out_specs=[spec for spec, _ in outs],
        out_shape=[shape for _, shape in outs],
        scratch_shapes=list(scratch),
        input_output_aliases=aliases,
        compiler_params=pltpu.CompilerParams(vmem_limit_bytes=VMEM_LIMIT),
        cost_estimate=COST,
        name=name,
    )(*args)


def chunk_outs(chunk, sn, rows, width):
    outs = [(pl.BlockSpec((sn, rows, CHUNK), lambda i: (0, 0, chunk)), f32_out(sn, rows, width))]
    shapes = [(sn, rows, CHUNK)] if chunk else [(rows, CHUNK)] * sn
    return outs + [(whole(shape), bf16_out(*shape)) for shape in shapes + [(rows, CHUNK)]]


def diag_rows(chunk, sn, width):
    return pl.BlockSpec((sn, CHUNK, width), lambda i: (0, chunk, 0))


SMEM_SPEC = pl.BlockSpec(memory_space=pltpu.SMEM)
ANY_SPEC = pl.BlockSpec(memory_space=pl.ANY)


def first_chunk(row, diag_blocks, panel):
    sn, rows, width = panel.shape
    return grid_call(
        functools.partial(first_kernel, sn),
        [row, diag_blocks, panel],
        [SMEM_SPEC, diag_rows(0, sn, width), ANY_SPEC],
        [(whole((sn, CHUNK, width)), f32_out(sn, CHUNK, width))] + chunk_outs(0, sn, rows, width),
        "first_chunk",
        [pltpu.VMEM((sn, rows, CHUNK), F32), pltpu.SemaphoreType.DMA],
    )


def second_factor(diag_blocks, w):
    sn, _, width = diag_blocks.shape
    return grid_call(
        functools.partial(factor_part, 1, sn),
        [diag_blocks, w],
        [diag_rows(1, sn, width), whole(w.shape)],
        [(whole(w.shape), f32_out(*w.shape))],
        "second_factor",
    )[0]


def second_chunk(row, w, own, panel, solved, deps):
    sn, rows, width = panel.shape
    count = sn * own[0].shape[0]
    return grid_call(
        functools.partial(second_kernel, sn, len(deps)),
        [row, w, *own, panel, solved, *deps],
        [SMEM_SPEC, whole(w.shape)] + [whole(o.shape) for o in own] + [whole(panel.shape), ANY_SPEC] + [ANY_SPEC] * len(deps),
        chunk_outs(1, sn, rows, width)
        + [(whole((count, BLK, BLK)), out(count, BLK, BLK)) for out in (f32_out, bf16_out)],
        "second_chunk",
        aliases={3 + sn: 0},
    )


def call(kernel, args, out_shape, scratch=(), name=None, smem=1, deps=(), through=()):
    n_args, n_more = len(args), len(deps) + len(through)
    n_outs = len(out_shape)
    specs = [SMEM_SPEC] * smem
    specs += [pl.BlockSpec(memory_space=pltpu.VMEM)] * (n_args - smem)

    def body(*refs):
        outs = refs[n_args + n_more : n_args + n_more + n_outs]
        kernel(*refs[:n_args], *outs, *refs[n_args + n_more + n_outs + len(through) :])

    return pl.pallas_call(
        body,
        in_specs=specs + [ANY_SPEC] * n_more,
        out_specs=[pl.BlockSpec(memory_space=pltpu.VMEM)] * n_outs + [ANY_SPEC] * len(through),
        out_shape=list(out_shape) + [jax.ShapeDtypeStruct(t.shape, t.dtype) for t in through],
        scratch_shapes=list(scratch),
        input_output_aliases={n_args + len(deps) + i: n_outs + i for i in range(len(through))},
        compiler_params=pltpu.CompilerParams(vmem_limit_bytes=SMALL_LIMIT),
        cost_estimate=COST,
        name=name,
    )(*args, *deps, *through)


def products_kernel(n, more, info_ref, *refs):
    own, right_in, refs = refs[:n], refs[n : 2 * n], refs[2 * n :]
    across_in, accs, (right_ref, across_ref) = refs[0], refs[1 : 1 + 2 * more], refs[1 + 2 * more :]
    half, sn = across_ref.shape[0], right_ref.shape[0] // across_ref.shape[0]
    nt = ((1,), (1,))
    own = own if n == sn else [own[0].at[pl.ds(s * half, half)] for s in range(sn)]
    right_in = right_in if n == sn else [right_in[0].at[pl.ds(s * half, half)] for s in range(sn)]
    for s in range(sn):

        def step(c, carry):
            product = dot_dims(own[s][c], right_in[s][c], nt)
            right_ref[s * half + c] = accs[0][s * half + c] + product if more else product
            return carry

        lax.fori_loop(0, half, step, 0, unroll=4)

        def step_across(c, carry):
            product = dot_dims(own[s][c], across_in[c], nt)
            across_ref[c] = accs[1][c] + product if more else product
            return carry

        @pl.when((info_ref[0] < 2) == (s == 0))
        def _():
            lax.fori_loop(0, half, step_across, 0, unroll=4)


def multiply(row, own, right, across, accs=(), deps=()):
    half, count = across.shape[0], len(own) * own[0].shape[0]
    return call(
        functools.partial(products_kernel, len(own), len(accs) > 0),
        [row, *own, *right, across, *accs],
        [f32_out(count, BLK, BLK), f32_out(half, BLK, BLK)],
        name="products",
        deps=deps,
    )


def pack(block):
    lane = lax.broadcasted_iota(jnp.int32, (BLK, BLK), 1)
    row = lax.broadcasted_iota(jnp.int32, (BLK, BLK), 0)
    first = block
    hi = first.astype(BF16).astype(F32)
    rest = jnp.sum(jnp.where(lane == row, first - hi, 0.0), axis=1, keepdims=True)
    first = jnp.where(lane > row, 0.0, first)
    first = jnp.where(lane == row + 1, rest, first)
    last = jnp.sum(jnp.where((lane == row) & (row == BLK - 1), block - hi, 0.0), keepdims=True)
    first = jnp.where((row == 0) & (lane == BLK - 1), last, first)
    return first.astype(BF16)


def unpack(block):
    lane = lax.broadcasted_iota(jnp.int32, (BLK, BLK), 1)
    row = lax.broadcasted_iota(jnp.int32, (BLK, BLK), 0)
    first = block.astype(F32)
    last = jnp.sum(jnp.where((row == 0) & (lane == BLK - 1), first, 0.0), keepdims=True)
    rest = jnp.sum(jnp.where(lane == row + 1, first, 0.0), axis=1, keepdims=True)
    rest = jnp.where((row == BLK - 1), last, rest)
    first = jnp.where(lane == row, first + rest, first)
    first = jnp.where(lane > row, 0.0, first)
    return first


def known_kernel(info_ref, id_ref, names_ref, out_ref):
    me = info_ref[4]
    count = names_ref.shape[0]
    per = BLK // count
    lane = lax.broadcasted_iota(jnp.int32, out_ref.shape, 1)
    row = lax.broadcasted_iota(jnp.int32, out_ref.shape, 0)
    table = jnp.where((row == 0) & (lane == id_ref[0]), me, 0)
    mine = row == 1 + lax.div(me, per)
    for c in range(count):
        table = jnp.where(mine & (lane == lax.rem(me, per) * count + c), names_ref[c], table)
    out_ref[...] = table


def add_blocks(info_ref, known_ref, names, ref, acc, lanes, widen=lambda block: block):
    core = info_ref[0]

    def add(c, carry):
        p = known_ref[0, names(c)]

        @pl.when(lax.rem(p, 2) == core)
        def _():
            at = lax.div(p, 2)
            acc[at, :, lanes] += widen(ref[c])

        return carry

    lax.fori_loop(0, ref.shape[0], add, 0)


def name_tables(info_ref, known_ref, names_ref, count):
    other = info_ref[4] + 1 - 2 * info_ref[0]
    per = BLK // count
    return [
        lambda c: names_ref[c],
        lambda c: known_ref[1 + lax.div(other, per), lax.rem(other, per) * count + c],
    ]


def scatter_diag_kernel(ny, info_ref, known_ref, names_ref, mine_ref, theirs_ref, own_ref, *rest):
    sends, acc = rest[:-1], rest[-1]
    y, count = info_ref[1], mine_ref.shape[0]
    acc[...] = jnp.zeros_like(acc)
    tables = name_tables(info_ref, known_ref, names_ref, count)
    add_blocks(info_ref, known_ref, tables[0], mine_ref, acc, slice(None))
    add_blocks(info_ref, known_ref, tables[1], theirs_ref, acc, slice(None), unpack)

    def emit(z, carry):
        for d in range(ny):
            block = acc[z * ny + lax.rem(y + d, ny)]
            if d == 0:
                own_ref[z] = block
            else:
                sends[d - 1][z] = pack(block)
        return carry

    lax.fori_loop(0, own_ref.shape[0], emit, 0)


def scatter_off_kernel(ny, info_ref, known_ref, names_ref, *refs):
    (mine_ref, across_ref, theirs_ref, their_across_ref, own_ref), rest = refs[:5], refs[5:]
    sends, acc = rest[:-1], rest[-1]
    y, count = info_ref[1], mine_ref.shape[0]
    half = across_ref.shape[0]
    first = jnp.where(info_ref[3] < 2, 0, half)
    acc[...] = jnp.zeros_like(acc)
    tables = name_tables(info_ref, known_ref, names_ref, count)
    blocks = ((mine_ref, across_ref), (theirs_ref, their_across_ref))
    for names, (right, across) in zip(tables, blocks):
        add_blocks(info_ref, known_ref, names, right, acc, slice(0, BLK))
        add_blocks(info_ref, known_ref, lambda c: names(first + c), across, acc, slice(BLK, 2 * BLK))

    def emit(z, carry):
        for d in range(ny):
            block = acc[z * ny + lax.rem(y + d, ny)]
            if d == 0:
                own_ref[z] = block
            else:
                sends[d - 1][z] = block.astype(BF16)
        return carry

    lax.fori_loop(0, own_ref.shape[0], emit, 0)


def sum_diag_kernel(info_ref, own_ref, *refs):
    got, out_ref, send_ref = refs[:-2], refs[-2], refs[-1]
    z = info_ref[2]

    def step(at, carry):
        total = own_ref[at]
        for ref in got:
            total += unpack(ref[at])
        send_ref[at] = pack(total)

        @pl.when(at == z)
        def _():
            out_ref[...] = total

        return carry

    lax.fori_loop(0, own_ref.shape[0], step, 0)


def sum_off_kernel(info_ref, own_ref, *refs):
    nz = own_ref.shape[0]
    got, out_ref, sends = refs[:-nz], refs[-nz], refs[len(refs) - nz + 1 :]
    z = info_ref[2]
    for d in range(nz):
        at = lax.rem(z + d, nz)
        total = own_ref[at]
        for ref in got:
            total += ref[at].astype(F32)
        if d == 0:
            out_ref[...] = total
        else:
            sends[d - 1][...] = total.astype(BF16)


def last_sum_kernel(own_ref, *refs):
    got, outs = refs[:-2], refs[-2:]
    total = own_ref[...]
    for ref in got:
        total += ref[...].astype(F32)
    for b, ref in enumerate(outs):
        ref[...] = total[:, BLK * b : BLK * (b + 1)]


def finish_kernel(info_ref, tile_ref, diag_ref, got_ref, right_ref, across_ref, left_in, across_in, out_ref):
    row, z, n = info_ref[3], info_ref[2], 4
    r = lax.broadcasted_iota(jnp.int32, (BLK, BLK), 0)
    c = lax.broadcasted_iota(jnp.int32, (BLK, BLK), 1)

    def step(at, low):
        return low + jnp.where(at == z, 0.0, unpack(got_ref[at]))

    low = lax.fori_loop(0, got_ref.shape[0], step, diag_ref[...])

    def put(at, value):
        cols = pl.ds(pl.multiple_of(at * BLK, BLK), BLK)
        out_ref[:, cols] = tile_ref[:, cols] - value

    put(row, jnp.where(c > r, low.T, low))
    put(lax.rem(row + 1, n), right_ref[...])
    put(lax.rem(row + 3, n), left_in[...].T)
    put(lax.rem(row + 2, n), across_ref[...] + across_in[...].T)


def ring(n, d):
    return [(i, (i + d) % n) for i in range(n)]


def f32_out(*shape):
    return jax.ShapeDtypeStruct(shape, F32)


def bf16_out(*shape):
    return jax.ShapeDtypeStruct(shape, BF16)


def on_device(diag_blocks, panel_blocks, ancestors, target_ids, target_tiles):
    nz, ny = lax.axis_size("z"), lax.axis_size("y")
    sn, anc, rows, width = panel_blocks.shape
    count = sn * anc
    half = count // sn
    z, y, core, row = (lax.axis_index(a).astype(jnp.int32) for a in ("z", "y", "core", "row"))
    info = jnp.stack([core, y, z, row, (z * ny + y) * 2 + core])
    at_row = row[None]
    panel = panel_blocks.reshape(sn, anc * rows, width)
    names = ancestors.reshape(count)

    def send(blocks, distance):
        return lax.ppermute(blocks, "row", ring(4, distance))

    def by_block(parts):
        return [part.reshape(-1, rows, CHUNK) for part in parts]

    w, solved, *parts = first_chunk(at_row, diag_blocks, panel)
    *own_0, part = by_block(parts)
    hop = send(part, 1)
    right_0 = [send(o, -1) for o in own_0]
    w = second_factor(diag_blocks, w)
    (hop,) = call(lambda info: None, [info], [], name="pass_on", deps=[w], through=[hop])
    across_0 = send(hop, 1)
    solved, *parts, diag, packed = second_chunk(at_row, w, own_0, panel, solved, [hop, right_0[0]])
    *own_1, part = by_block(parts)
    hop = send(part, 1)
    right_1 = [send(o, -1) for o in own_1]
    their_diag = lax.ppermute(packed, "core", ring(2, 1))

    (known,) = call(
        known_kernel,
        [info, target_ids, names],
        [jax.ShapeDtypeStruct((1 + nz * ny * 2 * count // BLK, BLK), jnp.int32)],
        name="known",
        smem=3,
        deps=[diag, across_0, right_0[1]],
    )
    known = lax.psum(known, COL)
    accs = multiply(at_row, own_0, right_0, across_0, deps=[known])
    own_diag, *sends, hop = call(
        functools.partial(scatter_diag_kernel, ny),
        [info, known, names, diag, their_diag],
        [f32_out(nz, BLK, BLK)] + [bf16_out(nz, BLK, BLK)] * (ny - 1),
        [pltpu.VMEM((nz * ny, BLK, BLK), F32)],
        name="scatter_diag",
        smem=3,
        deps=[accs[0]],
        through=[hop],
    )
    got_diag = [lax.ppermute(s, "y", ring(ny, d + 1)) for d, s in enumerate(sends)]
    across_1 = send(hop, 1)
    off_right, off_across = multiply(at_row, own_1, right_1, across_1, accs, deps=got_diag)
    their_right = lax.ppermute(off_right, "core", ring(2, 1))
    their_across = lax.ppermute(off_across, "core", ring(2, 1))
    own_off, *sends = call(
        functools.partial(scatter_off_kernel, ny),
        [info, known, names, off_right, off_across, their_right, their_across],
        [f32_out(nz, BLK, 2 * BLK)] + [bf16_out(nz, BLK, 2 * BLK)] * (ny - 1),
        [pltpu.VMEM((nz * ny, BLK, 2 * BLK), F32)],
        name="scatter_off",
        smem=3,
    )
    got_off = [lax.ppermute(s, "y", ring(ny, d + 1)) for d, s in enumerate(sends)]

    own_diag, send_diag = call(
        sum_diag_kernel,
        [info, own_diag, *got_diag],
        [f32_out(BLK, BLK), bf16_out(nz, BLK, BLK)],
        name="sum_diag",
        deps=[own_off],
    )
    got_diag = lax.all_to_all(send_diag, "z", 0, 0, tiled=True)
    own_off, *sends = call(
        sum_off_kernel,
        [info, own_off, *got_off],
        [f32_out(BLK, 2 * BLK)] + [bf16_out(BLK, 2 * BLK)] * (nz - 1),
        name="sum_off",
        deps=[got_diag],
    )
    got_off = [lax.ppermute(s, "z", ring(nz, d + 1)) for d, s in enumerate(sends)]
    off_right, off_across = call(
        last_sum_kernel, [own_off, *got_off], [f32_out(BLK, BLK)] * 2, name="last_sum", smem=0
    )
    from_left = send(off_right, 1)
    from_across = send(off_across, 2)
    (updated,) = call(
        finish_kernel,
        [info, target_tiles.reshape(rows, width), own_diag, got_diag]
        + [off_right, off_across, from_left, from_across],
        [f32_out(rows, width)],
        name="finish",
    )
    return solved.reshape(panel_blocks.shape), updated.reshape(target_tiles.shape)


def solution(mesh):
    devices = mesh.devices
    nz, ny = 8, 4
    fine = Mesh(devices.reshape(nz, ny, 2, devices.shape[1]), ("z", "y", "core", "row"))
    in_specs = (
        P(COL, None, None),
        P(COL, None, "row", None),
        P(COL, None),
        P(COL),
        P(COL, "row", None),
    )
    out_specs = (P(COL, None, "row", None), P(COL, "row", None))
    return jax.shard_map(
        on_device, mesh=fine, in_specs=in_specs, out_specs=out_specs, check_vma=False
    )
```

```python
import functools

import jax
import jax.numpy as jnp
from jax import lax
from jax.experimental import pallas as pl
from jax.experimental.pallas import tpu as pltpu
from jax.sharding import Mesh, PartitionSpec as P

F32 = jnp.float32
BF16 = jnp.bfloat16
BLK = 128
FIRST = 256
PAN = 16
FIRST_LIMIT = 58 * 1024 * 1024
VMEM_LIMIT = 24 * 1024 * 1024
SMALL_LIMIT = 8 * 1024 * 1024
COL = ("z", "y", "core")
COST = pl.CostEstimate(flops=10**6, bytes_accessed=10**4, transcendentals=0)


def split3(x):
    a = x.astype(BF16)
    rest = x - a.astype(F32)
    b = rest.astype(BF16)
    c = (rest - b.astype(F32)).astype(BF16)
    return a, b, c


def split2(x):
    a = x.astype(BF16)
    return a, (x - a.astype(F32)).astype(BF16)


def outer_product(left, right):
    a, b, c = split3(left)
    p, q, r = split3(right)
    return lax.dot_general(
        jnp.concatenate([a, a, a, b, b, c], axis=0),
        jnp.concatenate([p, q, r, p, q, p], axis=0),
        (((0,), (0,)), ((), ())),
        preferred_element_type=F32,
    )


def dot_dims(a, b, dims, precision=None):
    return lax.dot_general(a, b, (dims, ((), ())), precision=precision, preferred_element_type=F32)


def refined_reciprocal(d):
    r = pl.reciprocal(d, approx=True)
    r = r * (2.0 - d * r)
    return r * (2.0 - d * r)


def factor_panel(panel, k):
    half = PAN // 2
    lane1 = lax.broadcasted_iota(jnp.int32, (1, BLK), 1)
    sub = lax.broadcasted_iota(jnp.int32, (half, BLK), 0)
    lane = lax.broadcasted_iota(jnp.int32, (half, BLK), 1)
    top, bot = panel[:half], panel[half:]
    tops = [jnp.broadcast_to(top[:, k + c : k + c + 1], (half, BLK)) for c in range(PAN)]
    bots = [jnp.broadcast_to(bot[:, k + c : k + c + 1], (half, BLK)) for c in range(PAN)]
    diag_top = jnp.ones((half, BLK), F32)
    diag_bot = jnp.ones((half, BLK), F32)
    for i in range(PAN):
        if i < half:
            d = tops[i][i : i + 1]
            r = refined_reciprocal(d)
            mt = jnp.where(sub > i, tops[i] * r, 0.0)
            mb = bots[i] * r
            diag_top = jnp.where(sub == i, d, diag_top)
            for c in range(i + 1, PAN):
                row = tops[c][i : i + 1]
                tops[c] = tops[c] - mt * row
                bots[c] = bots[c] - mb * row
            pivot = top[i : i + 1] + jnp.where(lane1 == k + i, 1.0, 0.0)
            top = top - mt * pivot
            bot = bot - mb * pivot
        else:
            h = i - half
            d = bots[i][h : h + 1]
            r = refined_reciprocal(d)
            mb = jnp.where(sub > h, bots[i] * r, 0.0)
            diag_bot = jnp.where(sub == h, d, diag_bot)
            for c in range(i + 1, PAN):
                bots[c] = bots[c] - mb * bots[c][h : h + 1]
            pivot = bot[h : h + 1] + jnp.where(lane1 == k + i, 1.0, 0.0)
            bot = bot - mb * pivot

    def finish(rows, diag, first):
        at = lane - k - first
        rows = jnp.where(at == sub, 1.0, jnp.where((at > sub) & (lane < k + PAN), 0.0, rows))
        return rows * lax.rsqrt(diag)

    return jnp.concatenate([finish(top, diag_top, 0), finish(bot, diag_bot, half)], axis=0)


def factor_blocks(blocks):
    mats = list(blocks)
    done = [[] for _ in mats]
    for k in range(0, BLK, PAN):
        lane = lax.broadcasted_iota(jnp.int32, (PAN, BLK), 1)
        for s in range(len(mats)):
            rows = factor_panel(mats[s][:PAN], k)
            done[s].append(jnp.where(lane < k + PAN, rows, 0.0))
            if k + PAN < BLK:
                ahead = jnp.where(lane >= k + PAN, rows, 0.0)
                rest = mats[s][PAN:]
                at = lax.broadcasted_iota(jnp.int32, rest.shape, 1)
                rest = jnp.where((at >= k) & (at < k + PAN), 0.0, rest)
                mats[s] = rest - outer_product(ahead, rows)[k + PAN :]
    return [jnp.concatenate(rows, axis=0) for rows in done]


def factor_rows(k, s, row, w_prev):
    if not k:
        return row
    lane = lax.broadcasted_iota(jnp.int32, row.shape, 1)
    left = jnp.concatenate([w[:, BLK * k : BLK * (k + 1)] for w in w_prev], axis=0)
    right = jnp.concatenate(
        [jnp.where((lane >= BLK * (i + 1)) & (lane < BLK * k), 0.0, w) for i, w in enumerate(w_prev)],
        axis=0,
    )
    row = jnp.where(lane < BLK * k, 0.0, row)
    return row - dot_dims(left, right, ((0,), (0,)), lax.Precision.HIGHEST)


def factor_part(first, sn, diag_ref, *refs):
    w_ref = refs[-1]
    width = diag_ref.shape[2]
    w_prev = [
        [w[s, BLK * i : BLK * (i + 1), :] for w in refs[:-1] for i in range(w.shape[1] // BLK)]
        for s in range(sn)
    ]
    for at in range(diag_ref.shape[1] // BLK):
        k = first + at
        here = slice(BLK * k, BLK * (k + 1))
        rows = [
            factor_rows(k, s, diag_ref[s, BLK * at : BLK * (at + 1), :], w_prev[s]) for s in range(sn)
        ]
        inverses = factor_blocks([row[:, here] for row in rows])
        for s in range(sn):
            scaled = dot_dims(inverses[s], rows[s], ((1,), (0,)), lax.Precision.HIGHEST)
            lane = lax.broadcasted_iota(jnp.int32, (BLK, width), 1)
            inside = (lane >= BLK * k) & (lane < BLK * (k + 1))
            spread = jnp.concatenate([inverses[s]] * (width // BLK), axis=1)
            scaled = jnp.where(inside, spread, scaled)
            w_prev[s].append(scaled)
            w_ref[s, BLK * at : BLK * (at + 1), :] = scaled


def solve_part(start, stop, sn, info_ref, w_ref, b_ref, x_ref, r_refs, half_ref):
    tile = 256
    nt = ((1,), (1,))
    for s in range(sn):
        lane = lax.broadcasted_iota(jnp.int32, (stop - start, stop), 1)
        row = lax.broadcasted_iota(jnp.int32, (stop - start, stop), 0) + start
        w_hi, w_lo = split2(jnp.where(lane <= row, w_ref[s, :, :stop], 0.0))

        def step(t, carry):
            at = pl.ds(pl.multiple_of(t * tile, tile), tile)
            b_hi, b_lo = split2(b_ref[s, at, :])
            x = dot_dims(b_hi, w_hi, nt) + (dot_dims(b_hi, w_lo, nt) + dot_dims(b_lo, w_hi, nt))
            x_ref[s, at, :] = x
            r_refs[s][at, :] = x.astype(BF16)
            return carry

        lax.fori_loop(0, b_ref.shape[1] // tile, step, 0, unroll=True)
    half_ref[...] = jnp.where(info_ref[0] < 2, r_refs[1][...], r_refs[0][...])


def first_kernel(sn, info_ref, diag_ref, b_hbm, w_ref, x_ref, *refs):
    r_refs, (half_ref, b_ref, sem) = refs[:sn], refs[sn:]
    copy = pltpu.make_async_copy(b_hbm.at[:, :, pl.ds(0, FIRST)], b_ref, sem)
    copy.start()
    factor_part(0, sn, diag_ref, w_ref)
    copy.wait()
    solve_part(0, FIRST, sn, info_ref, w_ref, b_ref, x_ref, r_refs, half_ref)


def chunk_kernel(k, sn, n_own, n_more, n_through, info_ref, w_ref, b_ref, *refs):
    own_refs, refs = refs[:n_own], refs[n_own + 1 + n_more :]
    x_ref, r_ref, half_ref, *products = refs[: len(refs) - n_through]
    r_refs = [r_ref.at[s] for s in range(sn)]
    solve_part(BLK * k, BLK * (k + 1), sn, info_ref, w_ref, b_ref, x_ref, r_refs, half_ref)
    if products:
        diag_ref, packed_ref = products
        anc = b_ref.shape[1] // BLK
        for s in range(sn):

            def square(c, carry):
                at = pl.ds(pl.multiple_of(c * BLK, BLK), BLK)
                parts = [own_refs[s][c]] + [r[s * anc + c] for r in own_refs[sn:]] + [r_refs[s][at, :]]
                mine = jnp.concatenate(parts, axis=1)
                product = dot_dims(mine, mine, ((1,), (1,)))
                diag_ref[s * anc + c] = product
                packed_ref[s * anc + c] = pack(product)
                return carry

            lax.fori_loop(0, anc, square, 0, unroll=4)


def whole(shape):
    return pl.BlockSpec(shape, lambda i: (0,) * len(shape))


def grid_call(kernel, args, in_specs, outs, name, scratch=(), aliases={}, limit=VMEM_LIMIT, deps=()):
    n_args = len(args)

    def body(*refs):
        kernel(*refs[:n_args], *refs[n_args + len(deps) :])

    return pl.pallas_call(
        body,
        grid=(1,),
        in_specs=in_specs + [ANY_SPEC] * len(deps),
        out_specs=[spec for spec, _ in outs],
        out_shape=[shape for _, shape in outs],
        scratch_shapes=list(scratch),
        input_output_aliases=aliases,
        compiler_params=pltpu.CompilerParams(vmem_limit_bytes=limit),
        cost_estimate=COST,
        name=name,
    )(*args, *deps)


SMEM_SPEC = pl.BlockSpec(memory_space=pltpu.SMEM)
ANY_SPEC = pl.BlockSpec(memory_space=pl.ANY)


def first_chunk(row, diag_blocks, panel, deps):
    sn, rows, width = panel.shape
    return grid_call(
        functools.partial(first_kernel, sn),
        [row, diag_blocks, panel],
        [SMEM_SPEC, pl.BlockSpec((sn, FIRST, width), lambda i: (0, 0, 0)), ANY_SPEC],
        [
            (whole((sn, FIRST, width)), f32_out(sn, FIRST, width)),
            (pl.BlockSpec((sn, rows, FIRST), lambda i: (0, 0, 0)), f32_out(sn, rows, width)),
        ]
        + [(whole((rows, FIRST)), bf16_out(rows, FIRST))] * (sn + 1),
        "first_chunk",
        [pltpu.VMEM((sn, rows, FIRST), F32), pltpu.SemaphoreType.DMA],
        limit=FIRST_LIMIT,
        deps=deps,
    )


def factor_more(k, diag_blocks, w_prev, deps):
    sn, _, width = diag_blocks.shape
    return grid_call(
        functools.partial(factor_part, k, sn),
        [diag_blocks, *w_prev],
        [pl.BlockSpec((sn, BLK, width), lambda i: (0, k, 0))] + [whole(w.shape) for w in w_prev],
        [(whole((sn, BLK, width)), f32_out(sn, BLK, width))],
        "factor_more",
        deps=deps,
    )[0]


def solve_more(k, row, w, panel, solved, own=(), deps=(), through=()):
    sn, rows, width = panel.shape
    count = sn * rows // BLK
    outs = [
        (pl.BlockSpec((sn, rows, BLK), lambda i: (0, 0, k)), f32_out(sn, rows, width)),
        (whole((sn, rows, BLK)), bf16_out(sn, rows, BLK)),
        (whole((rows, BLK)), bf16_out(rows, BLK)),
    ]
    if own:
        outs += [(whole((count, BLK, BLK)), out(count, BLK, BLK)) for out in (f32_out, bf16_out)]
    aliases = {3 + len(own): 0}
    for i, t in enumerate(through):
        aliases[4 + len(own) + len(deps) + i] = len(outs)
        outs.append((ANY_SPEC, jax.ShapeDtypeStruct(t.shape, t.dtype)))
    n_more = len(deps) + len(through)
    return grid_call(
        functools.partial(chunk_kernel, k, sn, len(own), n_more, len(through)),
        [row, w, panel, *own, solved, *deps, *through],
        [SMEM_SPEC, whole(w.shape), whole((sn, rows, BLK * (k + 1)))]
        + [whole(o.shape) for o in own]
        + [ANY_SPEC] * (1 + n_more),
        outs,
        "solve_more",
        aliases=aliases,
    )


def call(kernel, args, out_shape, scratch=(), name=None, smem=1, deps=(), through=()):
    n_args, n_more = len(args), len(deps) + len(through)
    n_outs = len(out_shape)
    specs = [SMEM_SPEC] * smem
    specs += [pl.BlockSpec(memory_space=pltpu.VMEM)] * (n_args - smem)

    def body(*refs):
        outs = refs[n_args + n_more : n_args + n_more + n_outs]
        kernel(*refs[:n_args], *outs, *refs[n_args + n_more + n_outs + len(through) :])

    return pl.pallas_call(
        body,
        in_specs=specs + [ANY_SPEC] * n_more,
        out_specs=[pl.BlockSpec(memory_space=pltpu.VMEM)] * n_outs + [ANY_SPEC] * len(through),
        out_shape=list(out_shape) + [jax.ShapeDtypeStruct(t.shape, t.dtype) for t in through],
        scratch_shapes=list(scratch),
        input_output_aliases={n_args + len(deps) + i: n_outs + i for i in range(len(through))},
        compiler_params=pltpu.CompilerParams(vmem_limit_bytes=SMALL_LIMIT),
        cost_estimate=COST,
        name=name,
    )(*args, *deps, *through)


def products_kernel(n, info_ref, *refs):
    own, right, across, (right_ref, across_ref) = refs[:n], refs[n : 2 * n], refs[2 * n : -2], refs[-2:]
    half = across_ref.shape[0]
    nt = ((1,), (1,))
    for s in range(2):

        def joined(group, c):
            return jnp.concatenate([group[s][c]] + [r[s * half + c] for r in group[2:]], axis=1)

        def step(c, carry):
            right_ref[s * half + c] = dot_dims(joined(own, c), joined(right, c), nt)
            return carry

        def step_across(c, carry):
            other = jnp.concatenate([r[c] for r in across], axis=1)
            across_ref[c] = dot_dims(joined(own, c), other, nt)
            return carry

        lax.fori_loop(0, half, step, 0, unroll=4)

        @pl.when((info_ref[0] < 2) == (s == 0))
        def _():
            lax.fori_loop(0, half, step_across, 0, unroll=4)


def pack(block):
    lane = lax.broadcasted_iota(jnp.int32, (BLK, BLK), 1)
    row = lax.broadcasted_iota(jnp.int32, (BLK, BLK), 0)
    first = block
    hi = first.astype(BF16).astype(F32)
    rest = jnp.sum(jnp.where(lane == row, first - hi, 0.0), axis=1, keepdims=True)
    first = jnp.where(lane > row, 0.0, first)
    first = jnp.where(lane == row + 1, rest, first)
    last = jnp.sum(jnp.where((lane == row) & (row == BLK - 1), block - hi, 0.0), keepdims=True)
    first = jnp.where((row == 0) & (lane == BLK - 1), last, first)
    return first.astype(BF16)


def unpack(block):
    lane = lax.broadcasted_iota(jnp.int32, (BLK, BLK), 1)
    row = lax.broadcasted_iota(jnp.int32, (BLK, BLK), 0)
    first = block.astype(F32)
    last = jnp.sum(jnp.where((row == 0) & (lane == BLK - 1), first, 0.0), keepdims=True)
    rest = jnp.sum(jnp.where(lane == row + 1, first, 0.0), axis=1, keepdims=True)
    rest = jnp.where((row == BLK - 1), last, rest)
    first = jnp.where(lane == row, first + rest, first)
    first = jnp.where(lane > row, 0.0, first)
    return first


def known_kernel(info_ref, id_ref, names_ref, out_ref):
    me = info_ref[4]
    count = names_ref.shape[0]
    per = BLK // count
    lane = lax.broadcasted_iota(jnp.int32, out_ref.shape, 1)
    row = lax.broadcasted_iota(jnp.int32, out_ref.shape, 0)
    table = jnp.where((row == 0) & (lane == id_ref[0]), me, 0)
    mine = row == 1 + lax.div(me, per)
    for c in range(count):
        table = jnp.where(mine & (lane == lax.rem(me, per) * count + c), names_ref[c], table)
    out_ref[...] = table


def add_blocks(info_ref, known_ref, names, ref, acc, lanes, widen=lambda block: block):
    core = info_ref[0]

    def add(c, carry):
        p = known_ref[0, names(c)]

        @pl.when(lax.rem(p, 2) == core)
        def _():
            at = lax.div(p, 2)
            acc[at, :, lanes] += widen(ref[c])

        return carry

    lax.fori_loop(0, ref.shape[0], add, 0)


def name_tables(info_ref, known_ref, names_ref, count):
    other = info_ref[4] + 1 - 2 * info_ref[0]
    per = BLK // count
    return [
        lambda c: names_ref[c],
        lambda c: known_ref[1 + lax.div(other, per), lax.rem(other, per) * count + c],
    ]


def emit_y(ny, y, acc, own_ref, sends, narrow):
    def emit(z, carry):
        for d in range(ny):
            block = acc[z * ny + lax.rem(y + d, ny)]
            if d == 0:
                own_ref[z] = block
            else:
                sends[d - 1][z] = narrow(block)
        return carry

    lax.fori_loop(0, own_ref.shape[0], emit, 0)


def scatter_diag_kernel(ny, info_ref, known_ref, names_ref, mine_ref, theirs_ref, own_ref, *rest):
    sends, acc = rest[:-1], rest[-1]
    acc[...] = jnp.zeros_like(acc)
    mine, theirs = name_tables(info_ref, known_ref, names_ref, names_ref.shape[0])
    add_blocks(info_ref, known_ref, mine, mine_ref, acc, slice(None))
    add_blocks(info_ref, known_ref, theirs, theirs_ref, acc, slice(None), unpack)
    emit_y(ny, info_ref[1], acc, own_ref, sends, pack)


def scatter_off_kernel(ny, info_ref, known_ref, names_ref, *refs):
    (mine_ref, across_ref, theirs_ref, their_across_ref, own_ref), rest = refs[:5], refs[5:]
    sends, acc = rest[:-1], rest[-1]
    first = jnp.where(info_ref[3] < 2, 0, across_ref.shape[0])
    acc[...] = jnp.zeros_like(acc)
    tables = name_tables(info_ref, known_ref, names_ref, names_ref.shape[0])
    blocks = ((mine_ref, across_ref), (theirs_ref, their_across_ref))
    for names, (right, across) in zip(tables, blocks):
        add_blocks(info_ref, known_ref, names, right, acc, slice(0, BLK))
        add_blocks(info_ref, known_ref, lambda c: names(first + c), across, acc, slice(BLK, 2 * BLK))
    emit_y(ny, info_ref[1], acc, own_ref, sends, lambda block: block.astype(BF16))


def sum_y_kernel(diag, info_ref, own_ref, *refs):
    got, (out_ref, send_ref) = refs[:-2], refs[-2:]
    widen = unpack if diag else lambda block: block.astype(F32)
    narrow = pack if diag else lambda block: block.astype(BF16)

    def step(at, carry):
        total = own_ref[at]
        for ref in got:
            total += widen(ref[at])
        send_ref[at] = narrow(total)

        @pl.when(at == info_ref[2])
        def _():
            out_ref[...] = total

        return carry

    lax.fori_loop(0, own_ref.shape[0], step, 0)


def sum_z_kernel(info_ref, own_ref, got_ref, *out_refs):
    total = own_ref[...]
    for at in range(got_ref.shape[0]):
        total += jnp.where(info_ref[2] == at, 0.0, got_ref[at].astype(F32))
    for b, ref in enumerate(out_refs):
        ref[...] = total[:, BLK * b : BLK * (b + 1)]


def finish_kernel(info_ref, tile_ref, diag_ref, got_ref, right_ref, across_ref, left_in, across_in, out_ref):
    row, n = info_ref[3], 4
    r = lax.broadcasted_iota(jnp.int32, (BLK, BLK), 0)
    c = lax.broadcasted_iota(jnp.int32, (BLK, BLK), 1)
    low = diag_ref[...]
    for at in range(got_ref.shape[0]):
        low += jnp.where(info_ref[2] == at, 0.0, unpack(got_ref[at]))

    def put(at, value):
        cols = pl.ds(pl.multiple_of(at * BLK, BLK), BLK)
        out_ref[:, cols] = tile_ref[:, cols] - value

    put(row, jnp.where(c > r, low.T, low))
    put(lax.rem(row + 1, n), right_ref[...])
    put(lax.rem(row + 3, n), left_in[...].T)
    put(lax.rem(row + 2, n), across_ref[...] + across_in[...].T)


def ring(n, d):
    return [(i, (i + d) % n) for i in range(n)]


def f32_out(*shape):
    return jax.ShapeDtypeStruct(shape, F32)


def bf16_out(*shape):
    return jax.ShapeDtypeStruct(shape, BF16)


def on_device(diag_blocks, panel_blocks, ancestors, target_ids, target_tiles):
    nz, ny = lax.axis_size("z"), lax.axis_size("y")
    sn, anc, rows, width = panel_blocks.shape
    count = sn * anc
    half = count // sn
    z, y, core, row = (lax.axis_index(a).astype(jnp.int32) for a in ("z", "y", "core", "row"))
    info = jnp.stack([core, y, z, row, (z * ny + y) * 2 + core])
    at_row = row[None]
    panel = panel_blocks.reshape(sn, anc * rows, width)
    names = ancestors.reshape(count)

    def send(blocks, distance):
        return lax.ppermute(blocks, "row", ring(4, distance))

    def blocks(part):
        return part.reshape(-1, rows, part.shape[-1])

    def after_scatter(kernel, args, wide, name, **kwargs):
        return call(
            functools.partial(kernel, ny),
            [info, known, names, *args],
            [f32_out(nz, BLK, wide)] + [bf16_out(nz, BLK, wide)] * (ny - 1),
            [pltpu.VMEM((nz * ny, BLK, wide), F32)],
            name=name,
            smem=3,
            **kwargs,
        )

    def along_y(sends):
        return [lax.ppermute(s, "y", ring(ny, d + 1)) for d, s in enumerate(sends)]

    def sum_y(own, got, name, deps=(), diag=False):
        wide = own.shape[2]
        outs = [f32_out(BLK, wide), bf16_out(nz, BLK, wide)]
        kernel = functools.partial(sum_y_kernel, diag)
        own, sends = call(kernel, [info, own, *got], outs, name=name, deps=deps)
        return own, lax.all_to_all(sends, "z", 0, 0, tiled=True)

    (known,) = call(
        known_kernel,
        [info, target_ids, names],
        [jax.ShapeDtypeStruct((1 + nz * ny * 2 * count // BLK, BLK), jnp.int32)],
        name="known",
        smem=3,
    )
    steps = [("core", 2, 1), ("y", ny, 1), ("y", ny, 2), ("z", nz, 1), ("z", nz, 2), ("z", nz, 4)]

    def swap(step):
        axis, n, bit = steps[step]
        return lax.ppermute(known, axis, [(i, i ^ bit) for i in range(n)])

    came = swap(0)
    w, solved, *parts = first_chunk(at_row, diag_blocks, panel, [came])
    known = known + came
    came = swap(1)
    *own, part = [blocks(p) for p in parts]
    hop_0 = send(part, 1)
    right = [send(o, -1) for o in own]
    ws = [w, factor_more(2, diag_blocks, [w], [came])]
    known = known + came
    came = swap(2)
    solved, rounded, part, hop_0 = solve_more(
        2, at_row, ws[1], panel, solved, deps=[right[0], came], through=[hop_0]
    )
    known = known + came
    came = swap(3)
    own.append(blocks(rounded))
    right.append(send(own[-1], -1))
    hop_1 = send(blocks(part), 1)
    across = [send(hop_0, 1)]
    ws.append(factor_more(3, diag_blocks, ws, [came]))
    known = known + came
    came = swap(4)
    solved, rounded, part, diag, packed = solve_more(
        3, at_row, ws[2], panel, solved, own, [across[0], right[1], came]
    )
    known = known + came
    known = known + swap(5)
    own.append(blocks(rounded))
    right.append(send(own[-1], -1))
    their_diag = lax.ppermute(packed, "core", ring(2, 1))
    hop_2 = send(blocks(part), 1)
    across.append(send(hop_1, 1))
    own_diag, *sends = after_scatter(
        scatter_diag_kernel, [diag, their_diag], BLK, "scatter_diag", deps=[across[1], right[2]]
    )
    got_diag = along_y(sends)
    (hop_2,) = call(lambda info: None, [info], [], name="pass_on", deps=[own_diag], through=[hop_2])
    across.append(send(hop_2, 1))
    off_right, off_across = call(
        functools.partial(products_kernel, len(own)),
        [at_row, *own, *right, *across],
        [f32_out(count, BLK, BLK), f32_out(half, BLK, BLK)],
        name="products",
        deps=[got_diag[0], got_diag[2]],
    )
    their_right = lax.ppermute(off_right, "core", ring(2, 1))
    their_across = lax.ppermute(off_across, "core", ring(2, 1))
    own_off, *sends = after_scatter(
        scatter_off_kernel, [off_right, off_across, their_right, their_across], 2 * BLK, "scatter_off"
    )
    got_off = along_y(sends)
    own_diag, got_diag = sum_y(own_diag, got_diag, "sum_diag", [own_off], diag=True)
    own_off, got_off = sum_y(own_off, got_off, "sum_off", [got_diag])
    off_right, off_across = call(
        sum_z_kernel, [info, own_off, got_off], [f32_out(BLK, BLK)] * 2, name="last_sum"
    )
    from_left = send(off_right, 1)
    from_across = send(off_across, 2)
    (updated,) = call(
        finish_kernel,
        [info, target_tiles.reshape(rows, width), own_diag, got_diag]
        + [off_right, off_across, from_left, from_across],
        [f32_out(rows, width)],
        name="finish",
    )
    return solved.reshape(panel_blocks.shape), updated.reshape(target_tiles.shape)


def solution(mesh):
    devices = mesh.devices
    nz, ny = 8, 4
    fine = Mesh(devices.reshape(nz, ny, 2, devices.shape[1]), ("z", "y", "core", "row"))
    in_specs = (
        P(COL, None, None),
        P(COL, None, "row", None),
        P(COL, None),
        P(COL),
        P(COL, "row", None),
    )
    out_specs = (P(COL, None, "row", None), P(COL, "row", None))
    return jax.shard_map(
        on_device, mesh=fine, in_specs=in_specs, out_specs=out_specs, check_vma=False
    )
```

```python
import functools

import jax
import jax.numpy as jnp
from jax import lax
from jax.experimental import pallas as pl
from jax.experimental.pallas import tpu as pltpu
from jax.sharding import Mesh, PartitionSpec as P

F32 = jnp.float32
BF16 = jnp.bfloat16
BLK = 128
FIRST = 256
PAN = 16
FIRST_LIMIT = 48 * 1024 * 1024
VMEM_LIMIT = 24 * 1024 * 1024
SMALL_LIMIT = 8 * 1024 * 1024
COL = ("z", "y", "core")
COST = pl.CostEstimate(flops=10**6, bytes_accessed=10**4, transcendentals=0)


def split3(x):
    a = x.astype(BF16)
    rest = x - a.astype(F32)
    b = rest.astype(BF16)
    c = (rest - b.astype(F32)).astype(BF16)
    return a, b, c


def split2(x):
    a = x.astype(BF16)
    return a, (x - a.astype(F32)).astype(BF16)


def outer_product(left, right):
    a, b, c = split3(left)
    p, q, r = split3(right)
    return lax.dot_general(
        jnp.concatenate([a, a, a, b, b, c], axis=0),
        jnp.concatenate([p, q, r, p, q, p], axis=0),
        (((0,), (0,)), ((), ())),
        preferred_element_type=F32,
    )


def dot_dims(a, b, dims, precision=None):
    return lax.dot_general(a, b, (dims, ((), ())), precision=precision, preferred_element_type=F32)


def refined_reciprocal(d):
    r = pl.reciprocal(d, approx=True)
    r = r * (2.0 - d * r)
    return r * (2.0 - d * r)


def factor_panel(panel, k):
    half = PAN // 2
    lane1 = lax.broadcasted_iota(jnp.int32, (1, BLK), 1)
    sub = lax.broadcasted_iota(jnp.int32, (half, BLK), 0)
    lane = lax.broadcasted_iota(jnp.int32, (half, BLK), 1)
    top, bot = panel[:half], panel[half:]
    tops = [jnp.broadcast_to(top[:, k + c : k + c + 1], (half, BLK)) for c in range(PAN)]
    bots = [jnp.broadcast_to(bot[:, k + c : k + c + 1], (half, BLK)) for c in range(PAN)]
    diag_top = jnp.ones((half, BLK), F32)
    diag_bot = jnp.ones((half, BLK), F32)
    for i in range(PAN):
        if i < half:
            d = tops[i][i : i + 1]
            r = refined_reciprocal(d)
            mt = jnp.where(sub > i, tops[i] * r, 0.0)
            mb = bots[i] * r
            diag_top = jnp.where(sub == i, d, diag_top)
            for c in range(i + 1, PAN):
                row = tops[c][i : i + 1]
                tops[c] = tops[c] - mt * row
                bots[c] = bots[c] - mb * row
            pivot = top[i : i + 1] + jnp.where(lane1 == k + i, 1.0, 0.0)
            top = top - mt * pivot
            bot = bot - mb * pivot
        else:
            h = i - half
            d = bots[i][h : h + 1]
            r = refined_reciprocal(d)
            mb = jnp.where(sub > h, bots[i] * r, 0.0)
            diag_bot = jnp.where(sub == h, d, diag_bot)
            for c in range(i + 1, PAN):
                bots[c] = bots[c] - mb * bots[c][h : h + 1]
            pivot = bot[h : h + 1] + jnp.where(lane1 == k + i, 1.0, 0.0)
            bot = bot - mb * pivot

    def finish(rows, diag, first):
        at = lane - k - first
        rows = jnp.where(at == sub, 1.0, jnp.where((at > sub) & (lane < k + PAN), 0.0, rows))
        return rows * lax.rsqrt(diag)

    return jnp.concatenate([finish(top, diag_top, 0), finish(bot, diag_bot, half)], axis=0)


def factor_blocks(blocks):
    mats = list(blocks)
    done = [[] for _ in mats]
    for k in range(0, BLK, PAN):
        lane = lax.broadcasted_iota(jnp.int32, (PAN, BLK), 1)
        for s in range(len(mats)):
            rows = factor_panel(mats[s][:PAN], k)
            done[s].append(jnp.where(lane < k + PAN, rows, 0.0))
            if k + PAN < BLK:
                ahead = jnp.where(lane >= k + PAN, rows, 0.0)
                rest = mats[s][PAN:]
                at = lax.broadcasted_iota(jnp.int32, rest.shape, 1)
                rest = jnp.where((at >= k) & (at < k + PAN), 0.0, rest)
                mats[s] = rest - outer_product(ahead, rows)[k + PAN :]
    return [jnp.concatenate(rows, axis=0) for rows in done]


def factor_rows(k, s, row, w_prev):
    if not k:
        return row
    lane = lax.broadcasted_iota(jnp.int32, row.shape, 1)
    left = jnp.concatenate([w[:, BLK * k : BLK * (k + 1)] for w in w_prev], axis=0)
    right = jnp.concatenate(
        [jnp.where((lane >= BLK * (i + 1)) & (lane < BLK * k), 0.0, w) for i, w in enumerate(w_prev)],
        axis=0,
    )
    row = jnp.where(lane < BLK * k, 0.0, row)
    return row - dot_dims(left, right, ((0,), (0,)), lax.Precision.HIGHEST)


def factor_part(first, sn, diag_ref, *refs):
    w_ref = refs[-1]
    width = diag_ref.shape[2]
    w_prev = [
        [w[s, BLK * i : BLK * (i + 1), :] for w in refs[:-1] for i in range(w.shape[1] // BLK)]
        for s in range(sn)
    ]
    for at in range(diag_ref.shape[1] // BLK):
        k = first + at
        here = slice(BLK * k, BLK * (k + 1))
        rows = [
            factor_rows(k, s, diag_ref[s, BLK * at : BLK * (at + 1), :], w_prev[s]) for s in range(sn)
        ]
        inverses = factor_blocks([row[:, here] for row in rows])
        for s in range(sn):
            scaled = dot_dims(inverses[s], rows[s], ((1,), (0,)), lax.Precision.HIGHEST)
            lane = lax.broadcasted_iota(jnp.int32, (BLK, width), 1)
            inside = (lane >= BLK * k) & (lane < BLK * (k + 1))
            spread = jnp.concatenate([inverses[s]] * (width // BLK), axis=1)
            scaled = jnp.where(inside, spread, scaled)
            w_prev[s].append(scaled)
            w_ref[s, BLK * at : BLK * (at + 1), :] = scaled


def solve_part(start, stop, sn, info_ref, w_ref, b_ref, x_ref, r_refs, half_ref):
    tile = 256
    nt = ((1,), (1,))
    for s in range(sn):
        lane = lax.broadcasted_iota(jnp.int32, (stop - start, stop), 1)
        row = lax.broadcasted_iota(jnp.int32, (stop - start, stop), 0) + start
        w_hi, w_lo = split2(jnp.where(lane <= row, w_ref[s, :, :stop], 0.0))

        def step(t, carry):
            at = pl.ds(pl.multiple_of(t * tile, tile), tile)
            b_hi, b_lo = split2(b_ref[s, at, :])
            x = dot_dims(b_hi, w_hi, nt) + (dot_dims(b_hi, w_lo, nt) + dot_dims(b_lo, w_hi, nt))
            x_ref[s, at, :] = x
            r_refs[s][at, :] = x.astype(BF16)
            return carry

        lax.fori_loop(0, b_ref.shape[1] // tile, step, 0, unroll=True)
    chosen = jnp.where(info_ref[0] < 2, r_refs[1][...], r_refs[0][...])
    half_ref[:, half_ref.shape[1] - (stop - start) :] = chosen


def first_kernel(sn, info_ref, diag_ref, b_hbm, w_ref, x_ref, *refs):
    r_ref, half_ref, b_ref, sem = refs
    r_refs = [r_ref.at[s] for s in range(sn)]
    copy = pltpu.make_async_copy(b_hbm.at[:, :, pl.ds(0, FIRST)], b_ref, sem)
    copy.start()
    factor_part(0, sn, diag_ref, w_ref)
    copy.wait()
    solve_part(0, FIRST, sn, info_ref, w_ref, b_ref, x_ref, r_refs, half_ref)


def chunk_kernel(k, sn, n_own, n_more, n_through, info_ref, w_ref, b_ref, *refs):
    own_refs, refs = refs[:n_own], refs[n_own + 1 + n_more :]
    part_refs, own_refs = own_refs[2:], own_refs[:2]
    x_ref, r_ref, half_ref, *products = refs[: len(refs) - n_through]
    r_refs = [r_ref.at[s] for s in range(sn)]
    for ref in part_refs:
        half_ref[:, : ref.shape[1]] = ref[...]
    solve_part(BLK * k, BLK * (k + 1), sn, info_ref, w_ref, b_ref, x_ref, r_refs, half_ref)
    if products:
        diag_ref, packed_ref = products
        anc = b_ref.shape[1] // BLK
        for s in range(sn):

            def square(c, carry):
                at = pl.ds(pl.multiple_of(c * BLK, BLK), BLK)
                parts = [r[s * anc + c] for r in own_refs] + [r_refs[s][at, :]]
                mine = jnp.concatenate(parts, axis=1)
                product = dot_dims(mine, mine, ((1,), (1,)))
                diag_ref[s * anc + c] = product
                packed_ref[s * anc + c] = pack(product)
                return carry

            lax.fori_loop(0, anc, square, 0, unroll=4)


def whole(shape):
    return pl.BlockSpec(shape, lambda i: (0,) * len(shape))


def grid_call(kernel, args, in_specs, outs, name, scratch=(), aliases={}, limit=VMEM_LIMIT, deps=()):
    n_args = len(args)

    def body(*refs):
        kernel(*refs[:n_args], *refs[n_args + len(deps) :])

    return pl.pallas_call(
        body,
        grid=(1,),
        in_specs=in_specs + [ANY_SPEC] * len(deps),
        out_specs=[spec for spec, _ in outs],
        out_shape=[shape for _, shape in outs],
        scratch_shapes=list(scratch),
        input_output_aliases=aliases,
        compiler_params=pltpu.CompilerParams(vmem_limit_bytes=limit),
        cost_estimate=COST,
        name=name,
    )(*args, *deps)


SMEM_SPEC = pl.BlockSpec(memory_space=pltpu.SMEM)
ANY_SPEC = pl.BlockSpec(memory_space=pl.ANY)


def first_chunk(row, diag_blocks, panel, deps):
    sn, rows, width = panel.shape
    return grid_call(
        functools.partial(first_kernel, sn),
        [row, diag_blocks, panel],
        [SMEM_SPEC, pl.BlockSpec((sn, FIRST, width), lambda i: (0, 0, 0)), ANY_SPEC],
        [
            (whole((sn, FIRST, width)), f32_out(sn, FIRST, width)),
            (pl.BlockSpec((sn, rows, FIRST), lambda i: (0, 0, 0)), f32_out(sn, rows, width)),
            (whole((sn, rows, FIRST)), bf16_out(sn, rows, FIRST)),
            (whole((rows, FIRST)), bf16_out(rows, FIRST)),
        ],
        "first_chunk",
        [pltpu.VMEM((sn, rows, FIRST), F32), pltpu.SemaphoreType.DMA],
        limit=FIRST_LIMIT,
        deps=deps,
    )


def factor_more(k, diag_blocks, w_prev, deps):
    sn, _, width = diag_blocks.shape
    return grid_call(
        functools.partial(factor_part, k, sn),
        [diag_blocks, *w_prev],
        [pl.BlockSpec((sn, BLK, width), lambda i: (0, k, 0))] + [whole(w.shape) for w in w_prev],
        [(whole((sn, BLK, width)), f32_out(sn, BLK, width))],
        "factor_more",
        deps=deps,
    )[0]


def solve_more(k, row, w, panel, solved, own=(), deps=(), through=()):
    sn, rows, width = panel.shape
    count = sn * rows // BLK
    outs = [
        (pl.BlockSpec((sn, rows, BLK), lambda i: (0, 0, k)), f32_out(sn, rows, width)),
        (whole((sn, rows, BLK)), bf16_out(sn, rows, BLK)),
    ]
    wide = BLK * 2 if own else BLK
    outs.append((whole((rows, wide)), bf16_out(rows, wide)))
    if own:
        outs += [(whole((count, BLK, BLK)), out(count, BLK, BLK)) for out in (f32_out, bf16_out)]
    aliases = {3 + len(own): 0}
    for i, t in enumerate(through):
        aliases[4 + len(own) + len(deps) + i] = len(outs)
        outs.append((ANY_SPEC, jax.ShapeDtypeStruct(t.shape, t.dtype)))
    n_more = len(deps) + len(through)
    return grid_call(
        functools.partial(chunk_kernel, k, sn, len(own), n_more, len(through)),
        [row, w, panel, *own, solved, *deps, *through],
        [SMEM_SPEC, whole(w.shape), whole((sn, rows, BLK * (k + 1)))]
        + [whole(o.shape) for o in own]
        + [ANY_SPEC] * (1 + n_more),
        outs,
        "solve_more",
        aliases=aliases,
    )


def call(kernel, args, out_shape, scratch=(), name=None, smem=1, deps=(), through=()):
    n_args, n_more = len(args), len(deps) + len(through)
    n_outs = len(out_shape)
    specs = [SMEM_SPEC] * smem
    specs += [pl.BlockSpec(memory_space=pltpu.VMEM)] * (n_args - smem)

    def body(*refs):
        outs = refs[n_args + n_more : n_args + n_more + n_outs]
        kernel(*refs[:n_args], *outs, *refs[n_args + n_more + n_outs + len(through) :])

    return pl.pallas_call(
        body,
        in_specs=specs + [ANY_SPEC] * n_more,
        out_specs=[pl.BlockSpec(memory_space=pltpu.VMEM)] * n_outs + [ANY_SPEC] * len(through),
        out_shape=list(out_shape) + [jax.ShapeDtypeStruct(t.shape, t.dtype) for t in through],
        scratch_shapes=list(scratch),
        input_output_aliases={n_args + len(deps) + i: n_outs + i for i in range(len(through))},
        compiler_params=pltpu.CompilerParams(vmem_limit_bytes=SMALL_LIMIT),
        cost_estimate=COST,
        name=name,
    )(*args, *deps, *through)


def products_kernel(n, info_ref, *refs):
    own, right, across, (right_ref, across_ref) = refs[:n], refs[n : 2 * n], refs[2 * n : -2], refs[-2:]
    half = across_ref.shape[0]
    nt = ((1,), (1,))
    for s in range(2):

        def joined(group, c):
            return jnp.concatenate([r[s * half + c] for r in group], axis=1)

        def step(c, carry):
            right_ref[s * half + c] = dot_dims(joined(own, c), joined(right, c), nt)
            return carry

        def step_across(c, carry):
            other = jnp.concatenate([r[c] for r in across], axis=1)
            across_ref[c] = dot_dims(joined(own, c), other, nt)
            return carry

        lax.fori_loop(0, half, step, 0, unroll=4)

        @pl.when((info_ref[0] < 2) == (s == 0))
        def _():
            lax.fori_loop(0, half, step_across, 0, unroll=4)


def pack(block):
    lane = lax.broadcasted_iota(jnp.int32, (BLK, BLK), 1)
    row = lax.broadcasted_iota(jnp.int32, (BLK, BLK), 0)
    first = block
    hi = first.astype(BF16).astype(F32)
    rest = jnp.sum(jnp.where(lane == row, first - hi, 0.0), axis=1, keepdims=True)
    first = jnp.where(lane > row, 0.0, first)
    first = jnp.where(lane == row + 1, rest, first)
    last = jnp.sum(jnp.where((lane == row) & (row == BLK - 1), block - hi, 0.0), keepdims=True)
    first = jnp.where((row == 0) & (lane == BLK - 1), last, first)
    return first.astype(BF16)


def unpack(block):
    lane = lax.broadcasted_iota(jnp.int32, (BLK, BLK), 1)
    row = lax.broadcasted_iota(jnp.int32, (BLK, BLK), 0)
    first = block.astype(F32)
    last = jnp.sum(jnp.where((row == 0) & (lane == BLK - 1), first, 0.0), keepdims=True)
    rest = jnp.sum(jnp.where(lane == row + 1, first, 0.0), axis=1, keepdims=True)
    rest = jnp.where((row == BLK - 1), last, rest)
    first = jnp.where(lane == row, first + rest, first)
    first = jnp.where(lane > row, 0.0, first)
    return first


def known_kernel(info_ref, id_ref, names_ref, out_ref):
    me = info_ref[4]
    count = names_ref.shape[0]
    per = BLK // count
    lane = lax.broadcasted_iota(jnp.int32, out_ref.shape, 1)
    row = lax.broadcasted_iota(jnp.int32, out_ref.shape, 0)
    table = jnp.where((row == 0) & (lane == id_ref[0]), me, 0)
    mine = row == 1 + lax.div(me, per)
    for c in range(count):
        table = jnp.where(mine & (lane == lax.rem(me, per) * count + c), names_ref[c], table)
    out_ref[...] = table


def add_blocks(info_ref, known_ref, names, ref, acc, lanes, widen=lambda block: block):
    core = info_ref[0]

    def add(c, carry):
        p = known_ref[0, names(c)]

        @pl.when(lax.rem(p, 2) == core)
        def _():
            at = lax.div(p, 2)
            acc[at, :, lanes] += widen(ref[c])

        return carry

    lax.fori_loop(0, ref.shape[0], add, 0)


def name_tables(info_ref, known_ref, names_ref, count):
    other = info_ref[4] + 1 - 2 * info_ref[0]
    per = BLK // count
    return [
        lambda c: names_ref[c],
        lambda c: known_ref[1 + lax.div(other, per), lax.rem(other, per) * count + c],
    ]


def emit_y(ny, y, acc, own_ref, sends, narrow):
    def emit(z, carry):
        for d in range(ny):
            block = acc[z * ny + lax.rem(y + d, ny)]
            if d == 0:
                own_ref[z] = block
            else:
                sends[d - 1][z] = narrow(block)
        return carry

    lax.fori_loop(0, own_ref.shape[0], emit, 0)


def scatter_diag_kernel(ny, info_ref, known_ref, names_ref, mine_ref, theirs_ref, own_ref, *rest):
    sends, acc = rest[:-1], rest[-1]
    acc[...] = jnp.zeros_like(acc)
    mine, theirs = name_tables(info_ref, known_ref, names_ref, names_ref.shape[0])
    add_blocks(info_ref, known_ref, mine, mine_ref, acc, slice(None))
    add_blocks(info_ref, known_ref, theirs, theirs_ref, acc, slice(None), unpack)
    emit_y(ny, info_ref[1], acc, own_ref, sends, pack)


def scatter_off_kernel(ny, info_ref, known_ref, names_ref, *refs):
    (mine_ref, across_ref, theirs_ref, their_across_ref, own_ref), rest = refs[:5], refs[5:]
    sends, acc = rest[:-1], rest[-1]
    first = jnp.where(info_ref[3] < 2, 0, across_ref.shape[0])
    acc[...] = jnp.zeros_like(acc)
    tables = name_tables(info_ref, known_ref, names_ref, names_ref.shape[0])
    blocks = ((mine_ref, across_ref), (theirs_ref, their_across_ref))
    for names, (right, across) in zip(tables, blocks):
        add_blocks(info_ref, known_ref, names, right, acc, slice(0, BLK))
        add_blocks(info_ref, known_ref, lambda c: names(first + c), across, acc, slice(BLK, 2 * BLK))
    emit_y(ny, info_ref[1], acc, own_ref, sends, lambda block: block.astype(BF16))


def sum_y_kernel(diag, info_ref, own_ref, *refs):
    got, (out_ref, send_ref) = refs[:-2], refs[-2:]
    widen = unpack if diag else lambda block: block.astype(F32)
    narrow = pack if diag else lambda block: block.astype(BF16)

    def step(at, carry):
        total = own_ref[at]
        for ref in got:
            total += widen(ref[at])
        send_ref[at] = narrow(total)

        @pl.when(at == info_ref[2])
        def _():
            out_ref[...] = total

        return carry

    lax.fori_loop(0, own_ref.shape[0], step, 0)


def sum_z_kernel(info_ref, own_ref, got_ref, *out_refs):
    total = own_ref[...]
    for at in range(got_ref.shape[0]):
        total += jnp.where(info_ref[2] == at, 0.0, got_ref[at].astype(F32))
    for b, ref in enumerate(out_refs):
        ref[...] = total[:, BLK * b : BLK * (b + 1)]


def finish_kernel(info_ref, tile_ref, diag_ref, got_ref, right_ref, across_ref, left_in, across_in, out_ref):
    row, n = info_ref[3], 4
    r = lax.broadcasted_iota(jnp.int32, (BLK, BLK), 0)
    c = lax.broadcasted_iota(jnp.int32, (BLK, BLK), 1)
    low = diag_ref[...]
    for at in range(got_ref.shape[0]):
        low += jnp.where(info_ref[2] == at, 0.0, unpack(got_ref[at]))

    def put(at, value):
        cols = pl.ds(pl.multiple_of(at * BLK, BLK), BLK)
        out_ref[:, cols] = tile_ref[:, cols] - value

    put(row, jnp.where(c > r, low.T, low))
    put(lax.rem(row + 1, n), right_ref[...])
    put(lax.rem(row + 3, n), left_in[...].T)
    put(lax.rem(row + 2, n), across_ref[...] + across_in[...].T)


def ring(n, d):
    return [(i, (i + d) % n) for i in range(n)]


def f32_out(*shape):
    return jax.ShapeDtypeStruct(shape, F32)


def bf16_out(*shape):
    return jax.ShapeDtypeStruct(shape, BF16)


def on_device(diag_blocks, panel_blocks, ancestors, target_ids, target_tiles):
    nz, ny = lax.axis_size("z"), lax.axis_size("y")
    sn, anc, rows, width = panel_blocks.shape
    count = sn * anc
    half = count // sn
    z, y, core, row = (lax.axis_index(a).astype(jnp.int32) for a in ("z", "y", "core", "row"))
    info = jnp.stack([core, y, z, row, (z * ny + y) * 2 + core])
    at_row = row[None]
    panel = panel_blocks.reshape(sn, anc * rows, width)
    names = ancestors.reshape(count)

    def send(blocks, distance):
        return lax.ppermute(blocks, "row", ring(4, distance))

    def blocks(part):
        return part.reshape(-1, rows, part.shape[-1])

    def after_scatter(kernel, args, wide, name, **kwargs):
        return call(
            functools.partial(kernel, ny),
            [info, known, names, *args],
            [f32_out(nz, BLK, wide)] + [bf16_out(nz, BLK, wide)] * (ny - 1),
            [pltpu.VMEM((nz * ny, BLK, wide), F32)],
            name=name,
            smem=3,
            **kwargs,
        )

    def along_y(sends):
        return [lax.ppermute(s, "y", ring(ny, d + 1)) for d, s in enumerate(sends)]

    def sum_y(own, got, name, deps=(), diag=False):
        wide = own.shape[2]
        outs = [f32_out(BLK, wide), bf16_out(nz, BLK, wide)]
        kernel = functools.partial(sum_y_kernel, diag)
        own, sends = call(kernel, [info, own, *got], outs, name=name, deps=deps)
        return own, lax.all_to_all(sends, "z", 0, 0, tiled=True)

    w, solved, rounded, part = first_chunk(at_row, diag_blocks, panel, [])
    own = [blocks(rounded)]
    right = [send(own[0], -1)]
    hop = send(blocks(part), 1)
    ws = [w, factor_more(2, diag_blocks, [w], [])]
    solved, rounded, part = solve_more(2, at_row, ws[1], panel, solved)
    own.append(blocks(rounded))
    right.append(send(own[-1], -1))
    ws.append(factor_more(3, diag_blocks, ws, [hop, part]))
    across = [send(hop, 1)]
    solved, rounded, part, diag, packed = solve_more(3, at_row, ws[2], panel, solved, [*own, part])
    own.append(blocks(rounded))
    right.append(send(own[-1], -1))
    across.append(send(blocks(part), 2))
    their_diag = lax.ppermute(packed, "core", ring(2, 1))

    (known,) = call(
        known_kernel,
        [info, target_ids, names],
        [jax.ShapeDtypeStruct((1 + nz * ny * 2 * count // BLK, BLK), jnp.int32)],
        name="known",
        smem=3,
        deps=[diag, across[0], *right[:2]],
    )
    known = lax.psum(known, COL)
    own_diag, *sends = after_scatter(scatter_diag_kernel, [diag, their_diag], BLK, "scatter_diag")
    got_diag = along_y(sends)
    off_right, off_across = call(
        functools.partial(products_kernel, len(own)),
        [at_row, *own, *right, *across],
        [f32_out(count, BLK, BLK), f32_out(half, BLK, BLK)],
        name="products",
        deps=[own_diag],
    )
    their_right = lax.ppermute(off_right, "core", ring(2, 1))
    their_across = lax.ppermute(off_across, "core", ring(2, 1))
    own_off, *sends = after_scatter(
        scatter_off_kernel, [off_right, off_across, their_right, their_across], 2 * BLK, "scatter_off"
    )
    got_off = along_y(sends)
    own_diag, got_diag = sum_y(own_diag, got_diag, "sum_diag", [own_off], diag=True)
    own_off, got_off = sum_y(own_off, got_off, "sum_off", [got_diag])
    off_right, off_across = call(
        sum_z_kernel, [info, own_off, got_off], [f32_out(BLK, BLK)] * 2, name="last_sum"
    )
    from_left = send(off_right, 1)
    from_across = send(off_across, 2)
    (updated,) = call(
        finish_kernel,
        [info, target_tiles.reshape(rows, width), own_diag, got_diag]
        + [off_right, off_across, from_left, from_across],
        [f32_out(rows, width)],
        name="finish",
    )
    return solved.reshape(panel_blocks.shape), updated.reshape(target_tiles.shape)


def solution(mesh):
    devices = mesh.devices
    nz, ny = 8, 4
    fine = Mesh(devices.reshape(nz, ny, 2, devices.shape[1]), ("z", "y", "core", "row"))
    in_specs = (
        P(COL, None, None),
        P(COL, None, "row", None),
        P(COL, None),
        P(COL),
        P(COL, "row", None),
    )
    out_specs = (P(COL, None, "row", None), P(COL, "row", None))
    return jax.shard_map(
        on_device, mesh=fine, in_specs=in_specs, out_specs=out_specs, check_vma=False
    )
```

```python
import functools

import jax
import jax.numpy as jnp
from jax import lax
from jax.experimental import pallas as pl
from jax.experimental.pallas import tpu as pltpu
from jax.sharding import Mesh, PartitionSpec as P

F32 = jnp.float32
BF16 = jnp.bfloat16
BLK = 128
FIRST = 256
PAN = 16
FIRST_LIMIT = 48 * 1024 * 1024
VMEM_LIMIT = 24 * 1024 * 1024
SMALL_LIMIT = 8 * 1024 * 1024
COL = ("z", "y", "core")
COST = pl.CostEstimate(flops=10**6, bytes_accessed=10**4, transcendentals=0)


def split3(x):
    a = x.astype(BF16)
    rest = x - a.astype(F32)
    b = rest.astype(BF16)
    c = (rest - b.astype(F32)).astype(BF16)
    return a, b, c


def split2(x):
    a = x.astype(BF16)
    return a, (x - a.astype(F32)).astype(BF16)


def outer_product(left, right):
    a, b, c = split3(left)
    p, q, r = split3(right)
    return lax.dot_general(
        jnp.concatenate([a, a, a, b, b, c], axis=0),
        jnp.concatenate([p, q, r, p, q, p], axis=0),
        (((0,), (0,)), ((), ())),
        preferred_element_type=F32,
    )


def dot_dims(a, b, dims, precision=None):
    return lax.dot_general(a, b, (dims, ((), ())), precision=precision, preferred_element_type=F32)


def refined_reciprocal(d):
    r = pl.reciprocal(d, approx=True)
    r = r * (2.0 - d * r)
    return r * (2.0 - d * r)


def factor_panel(panel, k):
    half = PAN // 2
    lane1 = lax.broadcasted_iota(jnp.int32, (1, BLK), 1)
    sub = lax.broadcasted_iota(jnp.int32, (half, BLK), 0)
    lane = lax.broadcasted_iota(jnp.int32, (half, BLK), 1)
    top, bot = panel[:half], panel[half:]
    tops = [jnp.broadcast_to(top[:, k + c : k + c + 1], (half, BLK)) for c in range(PAN)]
    bots = [jnp.broadcast_to(bot[:, k + c : k + c + 1], (half, BLK)) for c in range(PAN)]
    diag_top = jnp.ones((half, BLK), F32)
    diag_bot = jnp.ones((half, BLK), F32)
    for i in range(PAN):
        if i < half:
            d = tops[i][i : i + 1]
            r = refined_reciprocal(d)
            mt = jnp.where(sub > i, tops[i] * r, 0.0)
            mb = bots[i] * r
            diag_top = jnp.where(sub == i, d, diag_top)
            for c in range(i + 1, PAN):
                row = tops[c][i : i + 1]
                tops[c] = tops[c] - mt * row
                bots[c] = bots[c] - mb * row
            pivot = top[i : i + 1] + jnp.where(lane1 == k + i, 1.0, 0.0)
            top = top - mt * pivot
            bot = bot - mb * pivot
        else:
            h = i - half
            d = bots[i][h : h + 1]
            r = refined_reciprocal(d)
            mb = jnp.where(sub > h, bots[i] * r, 0.0)
            diag_bot = jnp.where(sub == h, d, diag_bot)
            for c in range(i + 1, PAN):
                bots[c] = bots[c] - mb * bots[c][h : h + 1]
            pivot = bot[h : h + 1] + jnp.where(lane1 == k + i, 1.0, 0.0)
            bot = bot - mb * pivot

    def finish(rows, diag, first):
        at = lane - k - first
        rows = jnp.where(at == sub, 1.0, jnp.where((at > sub) & (lane < k + PAN), 0.0, rows))
        return rows * lax.rsqrt(diag)

    return jnp.concatenate([finish(top, diag_top, 0), finish(bot, diag_bot, half)], axis=0)


def factor_blocks(blocks):
    mats = list(blocks)
    done = [[] for _ in mats]
    for k in range(0, BLK, PAN):
        lane = lax.broadcasted_iota(jnp.int32, (PAN, BLK), 1)
        for s in range(len(mats)):
            rows = factor_panel(mats[s][:PAN], k)
            done[s].append(jnp.where(lane < k + PAN, rows, 0.0))
            if k + PAN < BLK:
                ahead = jnp.where(lane >= k + PAN, rows, 0.0)
                rest = mats[s][PAN:]
                at = lax.broadcasted_iota(jnp.int32, rest.shape, 1)
                rest = jnp.where((at >= k) & (at < k + PAN), 0.0, rest)
                mats[s] = rest - outer_product(ahead, rows)[k + PAN :]
    return [jnp.concatenate(rows, axis=0) for rows in done]


def factor_rows(k, s, row, w_prev):
    if not k:
        return row
    lane = lax.broadcasted_iota(jnp.int32, row.shape, 1)
    left = jnp.concatenate([w[:, BLK * k : BLK * (k + 1)] for w in w_prev], axis=0)
    right = jnp.concatenate(
        [jnp.where((lane >= BLK * (i + 1)) & (lane < BLK * k), 0.0, w) for i, w in enumerate(w_prev)],
        axis=0,
    )
    row = jnp.where(lane < BLK * k, 0.0, row)
    return row - dot_dims(left, right, ((0,), (0,)), lax.Precision.HIGHEST)


def factor_part(first, sn, diag_ref, *refs):
    w_ref = refs[-1]
    width = diag_ref.shape[2]
    w_prev = [
        [w[s, BLK * i : BLK * (i + 1), :] for w in refs[:-1] for i in range(w.shape[1] // BLK)]
        for s in range(sn)
    ]
    for at in range(diag_ref.shape[1] // BLK):
        k = first + at
        here = slice(BLK * k, BLK * (k + 1))
        rows = [
            factor_rows(k, s, diag_ref[s, BLK * at : BLK * (at + 1), :], w_prev[s]) for s in range(sn)
        ]
        inverses = factor_blocks([row[:, here] for row in rows])
        for s in range(sn):
            scaled = dot_dims(inverses[s], rows[s], ((1,), (0,)), lax.Precision.HIGHEST)
            lane = lax.broadcasted_iota(jnp.int32, (BLK, width), 1)
            inside = (lane >= BLK * k) & (lane < BLK * (k + 1))
            spread = jnp.concatenate([inverses[s]] * (width // BLK), axis=1)
            scaled = jnp.where(inside, spread, scaled)
            w_prev[s].append(scaled)
            w_ref[s, BLK * at : BLK * (at + 1), :] = scaled


def solve_part(start, stop, sn, info_ref, w_ref, b_ref, x_ref, r_refs, half_ref):
    tile = 256
    nt = ((1,), (1,))
    for s in range(sn):
        lane = lax.broadcasted_iota(jnp.int32, (stop - start, stop), 1)
        row = lax.broadcasted_iota(jnp.int32, (stop - start, stop), 0) + start
        w_hi, w_lo = split2(jnp.where(lane <= row, w_ref[s, :, :stop], 0.0))

        def step(t, carry):
            at = pl.ds(pl.multiple_of(t * tile, tile), tile)
            b_hi, b_lo = split2(b_ref[s, at, :])
            x = dot_dims(b_hi, w_hi, nt) + (dot_dims(b_hi, w_lo, nt) + dot_dims(b_lo, w_hi, nt))
            x_ref[s, at, :] = x
            r_refs[s][at, :] = x.astype(BF16)
            return carry

        lax.fori_loop(0, b_ref.shape[1] // tile, step, 0, unroll=True)
    chosen = jnp.where(info_ref[0] < 2, r_refs[1][...], r_refs[0][...])
    half_ref[...] = chosen


def first_kernel(sn, info_ref, diag_ref, b_hbm, w_ref, x_ref, r_ref, half_ref, b_ref, sem):
    copy = pltpu.make_async_copy(b_hbm.at[:, :, pl.ds(0, FIRST)], b_ref, sem)
    copy.start()
    factor_part(0, sn, diag_ref, w_ref)
    copy.wait()
    r_refs = [r_ref.at[s] for s in range(sn)]
    solve_part(0, FIRST, sn, info_ref, w_ref, b_ref, x_ref, r_refs, half_ref)


def second_kernel(sn, info_ref, w_ref, own_ref, b_ref, *refs):
    x_ref, r_ref, half_ref, product_ref, packed_ref = refs[2:]
    r_refs = [r_ref.at[s] for s in range(sn)]
    solve_part(FIRST, b_ref.shape[2], sn, info_ref, w_ref, b_ref, x_ref, r_refs, half_ref)
    anc = b_ref.shape[1] // BLK
    for s in range(sn):

        def square(c, carry):
            at = pl.ds(pl.multiple_of(c * BLK, BLK), BLK)
            mine = jnp.concatenate([own_ref[s * anc + c], r_refs[s][at, :]], axis=1)
            product = dot_dims(mine, mine, ((1,), (1,)))
            product_ref[s * anc + c] = product
            packed_ref[s * anc + c] = pack(product)
            return carry

        lax.fori_loop(0, anc, square, 0, unroll=4)


def whole(shape):
    return pl.BlockSpec(shape, lambda i: (0,) * len(shape))


def grid_call(kernel, args, in_specs, outs, name, scratch, limit, aliases={}):
    return pl.pallas_call(
        kernel,
        grid=(1,),
        in_specs=in_specs,
        out_specs=[spec for spec, _ in outs],
        out_shape=[shape for _, shape in outs],
        scratch_shapes=list(scratch),
        input_output_aliases=aliases,
        compiler_params=pltpu.CompilerParams(vmem_limit_bytes=limit),
        cost_estimate=COST,
        name=name,
    )(*args)


SMEM_SPEC = pl.BlockSpec(memory_space=pltpu.SMEM)
ANY_SPEC = pl.BlockSpec(memory_space=pl.ANY)


def first_chunk(row, diag_blocks, panel):
    sn, rows, width = panel.shape
    return grid_call(
        functools.partial(first_kernel, sn),
        [row, diag_blocks, panel],
        [SMEM_SPEC, pl.BlockSpec((sn, FIRST, width), lambda i: (0, 0, 0)), ANY_SPEC],
        [
            (whole((sn, FIRST, width)), f32_out(sn, FIRST, width)),
            (pl.BlockSpec((sn, rows, FIRST), lambda i: (0, 0, 0)), f32_out(sn, rows, width)),
            (whole((sn, rows, FIRST)), bf16_out(sn, rows, FIRST)),
            (whole((rows, FIRST)), bf16_out(rows, FIRST)),
        ],
        "first_chunk",
        [pltpu.VMEM((sn, rows, FIRST), F32), pltpu.SemaphoreType.DMA],
        FIRST_LIMIT,
    )


def second_factor(diag_blocks, w):
    sn, _, width = diag_blocks.shape
    return grid_call(
        functools.partial(factor_part, FIRST // BLK, sn),
        [diag_blocks, w],
        [pl.BlockSpec((sn, FIRST, width), lambda i: (0, 1, 0)), whole(w.shape)],
        [(whole(w.shape), f32_out(*w.shape))],
        "second_factor",
        [],
        VMEM_LIMIT,
    )[0]


def second_chunk(row, w, own, panel, solved, dep):
    sn, rows, width = panel.shape
    count = own.shape[0]
    return grid_call(
        functools.partial(second_kernel, sn),
        [row, w, own, panel, solved, dep],
        [SMEM_SPEC, whole(w.shape), whole(own.shape), whole(panel.shape), ANY_SPEC, ANY_SPEC],
        [
            (pl.BlockSpec((sn, rows, FIRST), lambda i: (0, 0, 1)), f32_out(sn, rows, width)),
            (whole((sn, rows, FIRST)), bf16_out(sn, rows, FIRST)),
            (whole((rows, FIRST)), bf16_out(rows, FIRST)),
            (whole((count, BLK, BLK)), f32_out(count, BLK, BLK)),
            (whole((count, BLK, BLK)), bf16_out(count, BLK, BLK)),
        ],
        "second_chunk",
        [],
        VMEM_LIMIT,
        {4: 0},
    )


def call(kernel, args, out_shape, scratch=(), name=None, smem=1, deps=(), through=()):
    n_args, n_more = len(args), len(deps) + len(through)
    n_outs = len(out_shape)
    specs = [SMEM_SPEC] * smem
    specs += [pl.BlockSpec(memory_space=pltpu.VMEM)] * (n_args - smem)

    def body(*refs):
        outs = refs[n_args + n_more : n_args + n_more + n_outs]
        kernel(*refs[:n_args], *outs, *refs[n_args + n_more + n_outs + len(through) :])

    return pl.pallas_call(
        body,
        in_specs=specs + [ANY_SPEC] * n_more,
        out_specs=[pl.BlockSpec(memory_space=pltpu.VMEM)] * n_outs + [ANY_SPEC] * len(through),
        out_shape=list(out_shape) + [jax.ShapeDtypeStruct(t.shape, t.dtype) for t in through],
        scratch_shapes=list(scratch),
        input_output_aliases={n_args + len(deps) + i: n_outs + i for i in range(len(through))},
        compiler_params=pltpu.CompilerParams(vmem_limit_bytes=SMALL_LIMIT),
        cost_estimate=COST,
        name=name,
    )(*args, *deps, *through)


def products_kernel(n, info_ref, *refs):
    own, right, across, (right_ref, across_ref) = refs[:n], refs[n : 2 * n], refs[2 * n : -2], refs[-2:]
    half = across_ref.shape[0]
    nt = ((1,), (1,))
    for s in range(2):

        def joined(group, c):
            return jnp.concatenate([r[s * half + c] for r in group], axis=1)

        def step(c, carry):
            right_ref[s * half + c] = dot_dims(joined(own, c), joined(right, c), nt)
            return carry

        def step_across(c, carry):
            other = jnp.concatenate([r[c] for r in across], axis=1)
            across_ref[c] = dot_dims(joined(own, c), other, nt)
            return carry

        lax.fori_loop(0, half, step, 0, unroll=4)

        @pl.when((info_ref[0] < 2) == (s == 0))
        def _():
            lax.fori_loop(0, half, step_across, 0, unroll=4)


def pack(block):
    lane = lax.broadcasted_iota(jnp.int32, (BLK, BLK), 1)
    row = lax.broadcasted_iota(jnp.int32, (BLK, BLK), 0)
    first = block
    hi = first.astype(BF16).astype(F32)
    rest = jnp.sum(jnp.where(lane == row, first - hi, 0.0), axis=1, keepdims=True)
    first = jnp.where(lane > row, 0.0, first)
    first = jnp.where(lane == row + 1, rest, first)
    last = jnp.sum(jnp.where((lane == row) & (row == BLK - 1), block - hi, 0.0), keepdims=True)
    first = jnp.where((row == 0) & (lane == BLK - 1), last, first)
    return first.astype(BF16)


def unpack(block):
    lane = lax.broadcasted_iota(jnp.int32, (BLK, BLK), 1)
    row = lax.broadcasted_iota(jnp.int32, (BLK, BLK), 0)
    first = block.astype(F32)
    last = jnp.sum(jnp.where((row == 0) & (lane == BLK - 1), first, 0.0), keepdims=True)
    rest = jnp.sum(jnp.where(lane == row + 1, first, 0.0), axis=1, keepdims=True)
    rest = jnp.where((row == BLK - 1), last, rest)
    first = jnp.where(lane == row, first + rest, first)
    first = jnp.where(lane > row, 0.0, first)
    return first


def known_kernel(info_ref, id_ref, names_ref, out_ref):
    me = info_ref[4]
    count = names_ref.shape[0]
    per = BLK // count
    lane = lax.broadcasted_iota(jnp.int32, out_ref.shape, 1)
    row = lax.broadcasted_iota(jnp.int32, out_ref.shape, 0)
    table = jnp.where((row == 0) & (lane == id_ref[0]), me, 0)
    mine = row == 1 + lax.div(me, per)
    for c in range(count):
        table = jnp.where(mine & (lane == lax.rem(me, per) * count + c), names_ref[c], table)
    out_ref[...] = table


def add_blocks(info_ref, known_ref, names, ref, acc, lanes, widen=lambda block: block):
    core = info_ref[0]

    def add(c, carry):
        p = known_ref[0, names(c)]

        @pl.when(lax.rem(p, 2) == core)
        def _():
            at = lax.div(p, 2)
            acc[at, :, lanes] += widen(ref[c])

        return carry

    lax.fori_loop(0, ref.shape[0], add, 0)


def name_tables(info_ref, known_ref, names_ref, count):
    other = info_ref[4] + 1 - 2 * info_ref[0]
    per = BLK // count
    return [
        lambda c: names_ref[c],
        lambda c: known_ref[1 + lax.div(other, per), lax.rem(other, per) * count + c],
    ]


def emit_y(ny, y, acc, own_ref, sends, narrow):
    def emit(z, carry):
        for d in range(ny):
            block = acc[z * ny + lax.rem(y + d, ny)]
            if d == 0:
                own_ref[z] = block
            else:
                sends[d - 1][z] = narrow(block)
        return carry

    lax.fori_loop(0, own_ref.shape[0], emit, 0)


def scatter_diag_kernel(ny, info_ref, known_ref, names_ref, mine_ref, theirs_ref, own_ref, *rest):
    sends, acc = rest[:-1], rest[-1]
    acc[...] = jnp.zeros_like(acc)
    mine, theirs = name_tables(info_ref, known_ref, names_ref, names_ref.shape[0])
    add_blocks(info_ref, known_ref, mine, mine_ref, acc, slice(None))
    add_blocks(info_ref, known_ref, theirs, theirs_ref, acc, slice(None), unpack)
    emit_y(ny, info_ref[1], acc, own_ref, sends, pack)


def scatter_off_kernel(ny, info_ref, known_ref, names_ref, *refs):
    (mine_ref, across_ref, theirs_ref, their_across_ref, own_ref), rest = refs[:5], refs[5:]
    sends, acc = rest[:-1], rest[-1]
    first = jnp.where(info_ref[3] < 2, 0, across_ref.shape[0])
    acc[...] = jnp.zeros_like(acc)
    tables = name_tables(info_ref, known_ref, names_ref, names_ref.shape[0])
    blocks = ((mine_ref, across_ref), (theirs_ref, their_across_ref))
    for names, (right, across) in zip(tables, blocks):
        add_blocks(info_ref, known_ref, names, right, acc, slice(0, BLK))
        add_blocks(info_ref, known_ref, lambda c: names(first + c), across, acc, slice(BLK, 2 * BLK))
    emit_y(ny, info_ref[1], acc, own_ref, sends, lambda block: block.astype(BF16))


def sum_y_kernel(diag, info_ref, own_ref, *refs):
    got, (out_ref, send_ref) = refs[:-2], refs[-2:]
    widen = unpack if diag else lambda block: block.astype(F32)
    narrow = pack if diag else lambda block: block.astype(BF16)

    def step(at, carry):
        total = own_ref[at]
        for ref in got:
            total += widen(ref[at])
        send_ref[at] = narrow(total)

        @pl.when(at == info_ref[2])
        def _():
            out_ref[...] = total

        return carry

    lax.fori_loop(0, own_ref.shape[0], step, 0)


def sum_z_kernel(info_ref, own_ref, got_ref, *out_refs):
    total = own_ref[...]
    for at in range(got_ref.shape[0]):
        total += jnp.where(info_ref[2] == at, 0.0, got_ref[at].astype(F32))
    for b, ref in enumerate(out_refs):
        ref[...] = total[:, BLK * b : BLK * (b + 1)]


def finish_kernel(info_ref, tile_ref, diag_ref, got_ref, right_ref, across_ref, left_in, across_in, out_ref):
    row, n = info_ref[3], 4
    r = lax.broadcasted_iota(jnp.int32, (BLK, BLK), 0)
    c = lax.broadcasted_iota(jnp.int32, (BLK, BLK), 1)
    low = diag_ref[...]
    for at in range(got_ref.shape[0]):
        low += jnp.where(info_ref[2] == at, 0.0, unpack(got_ref[at]))

    def put(at, value):
        cols = pl.ds(pl.multiple_of(at * BLK, BLK), BLK)
        out_ref[:, cols] = tile_ref[:, cols] - value

    put(row, jnp.where(c > r, low.T, low))
    put(lax.rem(row + 1, n), right_ref[...])
    put(lax.rem(row + 3, n), left_in[...].T)
    put(lax.rem(row + 2, n), across_ref[...] + across_in[...].T)


def ring(n, d):
    return [(i, (i + d) % n) for i in range(n)]


def f32_out(*shape):
    return jax.ShapeDtypeStruct(shape, F32)


def bf16_out(*shape):
    return jax.ShapeDtypeStruct(shape, BF16)


def on_device(diag_blocks, panel_blocks, ancestors, target_ids, target_tiles):
    nz, ny = lax.axis_size("z"), lax.axis_size("y")
    sn, anc, rows, width = panel_blocks.shape
    count = sn * anc
    half = count // sn
    z, y, core, row = (lax.axis_index(a).astype(jnp.int32) for a in ("z", "y", "core", "row"))
    info = jnp.stack([core, y, z, row, (z * ny + y) * 2 + core])
    at_row = row[None]
    panel = panel_blocks.reshape(sn, anc * rows, width)
    names = ancestors.reshape(count)

    def send(blocks, distance):
        return lax.ppermute(blocks, "row", ring(4, distance))

    def blocks(part):
        return part.reshape(-1, rows, part.shape[-1])

    def after_scatter(kernel, args, wide, name, **kwargs):
        return call(
            functools.partial(kernel, ny),
            [info, known, names, *args],
            [f32_out(nz, BLK, wide)] + [bf16_out(nz, BLK, wide)] * (ny - 1),
            [pltpu.VMEM((nz * ny, BLK, wide), F32)],
            name=name,
            smem=3,
            **kwargs,
        )

    def along_y(sends):
        return [lax.ppermute(s, "y", ring(ny, d + 1)) for d, s in enumerate(sends)]

    def sum_y(own, got, name, deps=(), diag=False):
        wide = own.shape[2]
        outs = [f32_out(BLK, wide), bf16_out(nz, BLK, wide)]
        kernel = functools.partial(sum_y_kernel, diag)
        own, sends = call(kernel, [info, own, *got], outs, name=name, deps=deps)
        return own, lax.all_to_all(sends, "z", 0, 0, tiled=True)

    w, solved, rounded, part = first_chunk(at_row, diag_blocks, panel)
    own = [blocks(rounded)]
    right = [send(own[0], -1)]
    hop = send(blocks(part), 1)
    w = second_factor(diag_blocks, w)
    solved, rounded, part, diag, packed = second_chunk(at_row, w, own[0], panel, solved, hop)
    own.append(blocks(rounded))
    right.append(send(own[1], -1))
    across = [send(hop, 1), send(blocks(part), 2)]
    their_diag = lax.ppermute(packed, "core", ring(2, 1))

    (known,) = call(
        known_kernel,
        [info, target_ids, names],
        [jax.ShapeDtypeStruct((1 + nz * ny * 2 * count // BLK, BLK), jnp.int32)],
        name="known",
        smem=3,
        deps=[diag, right[0]],
    )
    known = lax.psum(known, COL)
    own_diag, *sends = after_scatter(scatter_diag_kernel, [diag, their_diag], BLK, "scatter_diag")
    got_diag = along_y(sends)
    off_right, off_across = call(
        functools.partial(products_kernel, len(own)),
        [at_row, *own, *right, *across],
        [f32_out(count, BLK, BLK), f32_out(half, BLK, BLK)],
        name="products",
        deps=got_diag,
    )
    their_right = lax.ppermute(off_right, "core", ring(2, 1))
    their_across = lax.ppermute(off_across, "core", ring(2, 1))
    own_off, *sends = after_scatter(
        scatter_off_kernel, [off_right, off_across, their_right, their_across], 2 * BLK, "scatter_off"
    )
    got_off = along_y(sends)
    own_diag, got_diag = sum_y(own_diag, got_diag, "sum_diag", [own_off], diag=True)
    own_off, got_off = sum_y(own_off, got_off, "sum_off", [got_diag])
    off_right, off_across = call(
        sum_z_kernel, [info, own_off, got_off], [f32_out(BLK, BLK)] * 2, name="last_sum"
    )
    from_left = send(off_right, 1)
    from_across = send(off_across, 2)
    (updated,) = call(
        finish_kernel,
        [info, target_tiles.reshape(rows, width), own_diag, got_diag]
        + [off_right, off_across, from_left, from_across],
        [f32_out(rows, width)],
        name="finish",
    )
    return solved.reshape(panel_blocks.shape), updated.reshape(target_tiles.shape)


def solution(mesh):
    devices = mesh.devices
    nz, ny = 8, 4
    fine = Mesh(devices.reshape(nz, ny, 2, devices.shape[1]), ("z", "y", "core", "row"))
    in_specs = (
        P(COL, None, None),
        P(COL, None, "row", None),
        P(COL, None),
        P(COL),
        P(COL, "row", None),
    )
    out_specs = (P(COL, None, "row", None), P(COL, "row", None))
    return jax.shard_map(
        on_device, mesh=fine, in_specs=in_specs, out_specs=out_specs, check_vma=False
    )
```

```python
import functools

import jax
import jax.numpy as jnp
from jax import lax
from jax.experimental import pallas as pl
from jax.experimental.pallas import tpu as pltpu
from jax.sharding import Mesh, PartitionSpec as P

F32 = jnp.float32
BF16 = jnp.bfloat16
BLK = 128
FIRST = 256
PAN = 16
FIRST_LIMIT = 48 * 1024 * 1024
VMEM_LIMIT = 24 * 1024 * 1024
SMALL_LIMIT = 8 * 1024 * 1024
COL = ("z", "y", "core")
COST = pl.CostEstimate(flops=10**6, bytes_accessed=10**4, transcendentals=0)


def split3(x):
    a = x.astype(BF16)
    rest = x - a.astype(F32)
    b = rest.astype(BF16)
    c = (rest - b.astype(F32)).astype(BF16)
    return a, b, c


def split2(x):
    a = x.astype(BF16)
    return a, (x - a.astype(F32)).astype(BF16)


def outer_product(left, right):
    a, b, c = split3(left)
    p, q, r = split3(right)
    return lax.dot_general(
        jnp.concatenate([a, a, a, b, b, c], axis=0),
        jnp.concatenate([p, q, r, p, q, p], axis=0),
        (((0,), (0,)), ((), ())),
        preferred_element_type=F32,
    )


def dot_dims(a, b, dims, precision=None):
    return lax.dot_general(a, b, (dims, ((), ())), precision=precision, preferred_element_type=F32)


def refined_reciprocal(d):
    r = pl.reciprocal(d, approx=True)
    r = r * (2.0 - d * r)
    return r * (2.0 - d * r)


def factor_panel(panel, k):
    half = PAN // 2
    lane1 = lax.broadcasted_iota(jnp.int32, (1, BLK), 1)
    sub = lax.broadcasted_iota(jnp.int32, (half, BLK), 0)
    lane = lax.broadcasted_iota(jnp.int32, (half, BLK), 1)
    top, bot = panel[:half], panel[half:]
    tops = [jnp.broadcast_to(top[:, k + c : k + c + 1], (half, BLK)) for c in range(PAN)]
    bots = [jnp.broadcast_to(bot[:, k + c : k + c + 1], (half, BLK)) for c in range(PAN)]
    diag_top = jnp.ones((half, BLK), F32)
    diag_bot = jnp.ones((half, BLK), F32)
    for i in range(PAN):
        if i < half:
            d = tops[i][i : i + 1]
            r = refined_reciprocal(d)
            mt = jnp.where(sub > i, tops[i] * r, 0.0)
            mb = bots[i] * r
            diag_top = jnp.where(sub == i, d, diag_top)
            for c in range(i + 1, PAN):
                row = tops[c][i : i + 1]
                tops[c] = tops[c] - mt * row
                bots[c] = bots[c] - mb * row
            pivot = top[i : i + 1] + jnp.where(lane1 == k + i, 1.0, 0.0)
            top = top - mt * pivot
            bot = bot - mb * pivot
        else:
            h = i - half
            d = bots[i][h : h + 1]
            r = refined_reciprocal(d)
            mb = jnp.where(sub > h, bots[i] * r, 0.0)
            diag_bot = jnp.where(sub == h, d, diag_bot)
            for c in range(i + 1, PAN):
                bots[c] = bots[c] - mb * bots[c][h : h + 1]
            pivot = bot[h : h + 1] + jnp.where(lane1 == k + i, 1.0, 0.0)
            bot = bot - mb * pivot

    def finish(rows, diag, first):
        at = lane - k - first
        rows = jnp.where(at == sub, 1.0, jnp.where((at > sub) & (lane < k + PAN), 0.0, rows))
        return rows * lax.rsqrt(diag)

    return jnp.concatenate([finish(top, diag_top, 0), finish(bot, diag_bot, half)], axis=0)


def factor_blocks(blocks):
    mats = list(blocks)
    done = [[] for _ in mats]
    for k in range(0, BLK, PAN):
        lane = lax.broadcasted_iota(jnp.int32, (PAN, BLK), 1)
        for s in range(len(mats)):
            rows = factor_panel(mats[s][:PAN], k)
            done[s].append(jnp.where(lane < k + PAN, rows, 0.0))
            if k + PAN < BLK:
                ahead = jnp.where(lane >= k + PAN, rows, 0.0)
                rest = mats[s][PAN:]
                at = lax.broadcasted_iota(jnp.int32, rest.shape, 1)
                rest = jnp.where((at >= k) & (at < k + PAN), 0.0, rest)
                mats[s] = rest - outer_product(ahead, rows)[k + PAN :]
    return [jnp.concatenate(rows, axis=0) for rows in done]


def factor_rows(k, s, row, w_prev):
    if not k:
        return row
    lane = lax.broadcasted_iota(jnp.int32, row.shape, 1)
    left = jnp.concatenate([w[:, BLK * k : BLK * (k + 1)] for w in w_prev], axis=0)
    right = jnp.concatenate(
        [jnp.where((lane >= BLK * (i + 1)) & (lane < BLK * k), 0.0, w) for i, w in enumerate(w_prev)],
        axis=0,
    )
    row = jnp.where(lane < BLK * k, 0.0, row)
    return row - dot_dims(left, right, ((0,), (0,)), lax.Precision.HIGHEST)


def factor_part(first, sn, diag_ref, *refs):
    w_ref = refs[-1]
    width = diag_ref.shape[2]
    w_prev = [
        [w[s, BLK * i : BLK * (i + 1), :] for w in refs[:-1] for i in range(w.shape[1] // BLK)]
        for s in range(sn)
    ]
    for at in range(diag_ref.shape[1] // BLK):
        k = first + at
        here = slice(BLK * k, BLK * (k + 1))
        rows = [
            factor_rows(k, s, diag_ref[s, BLK * at : BLK * (at + 1), :], w_prev[s]) for s in range(sn)
        ]
        inverses = factor_blocks([row[:, here] for row in rows])
        for s in range(sn):
            scaled = dot_dims(inverses[s], rows[s], ((1,), (0,)), lax.Precision.HIGHEST)
            lane = lax.broadcasted_iota(jnp.int32, (BLK, width), 1)
            inside = (lane >= BLK * k) & (lane < BLK * (k + 1))
            spread = jnp.concatenate([inverses[s]] * (width // BLK), axis=1)
            scaled = jnp.where(inside, spread, scaled)
            w_prev[s].append(scaled)
            w_ref[s, BLK * at : BLK * (at + 1), :] = scaled


def solve_part(start, stop, sn, info_ref, w_ref, b_ref, x_ref, r_refs, half_ref):
    tile = 256
    nt = ((1,), (1,))
    for s in range(sn):
        lane = lax.broadcasted_iota(jnp.int32, (stop - start, stop), 1)
        row = lax.broadcasted_iota(jnp.int32, (stop - start, stop), 0) + start
        w_hi, w_lo = split2(jnp.where(lane <= row, w_ref[s, :, :stop], 0.0))

        def step(t, carry):
            at = pl.ds(pl.multiple_of(t * tile, tile), tile)
            b_hi, b_lo = split2(b_ref[s, at, :])
            x = dot_dims(b_hi, w_hi, nt) + (dot_dims(b_hi, w_lo, nt) + dot_dims(b_lo, w_hi, nt))
            x_ref[s, at, :] = x
            r_refs[s][at, :] = x.astype(BF16)
            return carry

        lax.fori_loop(0, b_ref.shape[1] // tile, step, 0, unroll=True)
    chosen = jnp.where(info_ref[0] < 2, r_refs[1][...], r_refs[0][...])
    half_ref[...] = chosen


def first_kernel(sn, info_ref, diag_ref, b_hbm, w_ref, x_ref, r_ref, half_ref, b_ref, sem):
    copy = pltpu.make_async_copy(b_hbm.at[:, :, pl.ds(0, FIRST)], b_ref, sem)
    copy.start()
    factor_part(0, sn, diag_ref, w_ref)
    copy.wait()
    r_refs = [r_ref.at[s] for s in range(sn)]
    solve_part(0, FIRST, sn, info_ref, w_ref, b_ref, x_ref, r_refs, half_ref)


def second_kernel(sn, info_ref, w_ref, own_ref, b_ref, *refs):
    x_ref, r_ref, half_ref, product_ref, packed_ref = refs[2:]
    r_refs = [r_ref.at[s] for s in range(sn)]
    solve_part(FIRST, b_ref.shape[2], sn, info_ref, w_ref, b_ref, x_ref, r_refs, half_ref)
    anc = b_ref.shape[1] // BLK
    for s in range(sn):

        def square(c, carry):
            at = pl.ds(pl.multiple_of(c * BLK, BLK), BLK)
            mine = jnp.concatenate([own_ref[s * anc + c], r_refs[s][at, :]], axis=1)
            product = dot_dims(mine, mine, ((1,), (1,)))
            product_ref[s * anc + c] = product
            packed_ref[s * anc + c] = pack(product)
            return carry

        lax.fori_loop(0, anc, square, 0, unroll=4)


def whole(shape):
    return pl.BlockSpec(shape, lambda i: (0,) * len(shape))


def grid_call(kernel, args, in_specs, outs, name, scratch, limit, aliases={}):
    return pl.pallas_call(
        kernel,
        grid=(1,),
        in_specs=in_specs,
        out_specs=[spec for spec, _ in outs],
        out_shape=[shape for _, shape in outs],
        scratch_shapes=list(scratch),
        input_output_aliases=aliases,
        compiler_params=pltpu.CompilerParams(vmem_limit_bytes=limit),
        cost_estimate=COST,
        name=name,
    )(*args)


SMEM_SPEC = pl.BlockSpec(memory_space=pltpu.SMEM)
ANY_SPEC = pl.BlockSpec(memory_space=pl.ANY)


def first_chunk(row, diag_blocks, panel):
    sn, rows, width = panel.shape
    return grid_call(
        functools.partial(first_kernel, sn),
        [row, diag_blocks, panel],
        [SMEM_SPEC, pl.BlockSpec((sn, FIRST, width), lambda i: (0, 0, 0)), ANY_SPEC],
        [
            (whole((sn, FIRST, width)), f32_out(sn, FIRST, width)),
            (pl.BlockSpec((sn, rows, FIRST), lambda i: (0, 0, 0)), f32_out(sn, rows, width)),
            (whole((sn, rows, FIRST)), bf16_out(sn, rows, FIRST)),
            (whole((rows, FIRST)), bf16_out(rows, FIRST)),
        ],
        "first_chunk",
        [pltpu.VMEM((sn, rows, FIRST), F32), pltpu.SemaphoreType.DMA],
        FIRST_LIMIT,
    )


def second_factor(diag_blocks, w):
    sn, _, width = diag_blocks.shape
    return grid_call(
        functools.partial(factor_part, FIRST // BLK, sn),
        [diag_blocks, w],
        [pl.BlockSpec((sn, FIRST, width), lambda i: (0, 1, 0)), whole(w.shape)],
        [(whole(w.shape), f32_out(*w.shape))],
        "second_factor",
        [],
        VMEM_LIMIT,
    )[0]


def second_chunk(row, w, own, panel, solved, dep):
    sn, rows, width = panel.shape
    count = own.shape[0]
    return grid_call(
        functools.partial(second_kernel, sn),
        [row, w, own, panel, solved, dep],
        [SMEM_SPEC, whole(w.shape), whole(own.shape), whole(panel.shape), ANY_SPEC, ANY_SPEC],
        [
            (pl.BlockSpec((sn, rows, FIRST), lambda i: (0, 0, 1)), f32_out(sn, rows, width)),
            (whole((sn, rows, FIRST)), bf16_out(sn, rows, FIRST)),
            (whole((rows, FIRST)), bf16_out(rows, FIRST)),
            (whole((count, BLK, BLK)), f32_out(count, BLK, BLK)),
            (whole((count, BLK, BLK)), bf16_out(count, BLK, BLK)),
        ],
        "second_chunk",
        [],
        VMEM_LIMIT,
        {4: 0},
    )


def call(kernel, args, out_shape, scratch=(), name=None, smem=1, deps=(), through=()):
    n_args, n_more = len(args), len(deps) + len(through)
    n_outs = len(out_shape)
    specs = [SMEM_SPEC] * smem
    specs += [pl.BlockSpec(memory_space=pltpu.VMEM)] * (n_args - smem)

    def body(*refs):
        outs = refs[n_args + n_more : n_args + n_more + n_outs]
        kernel(*refs[:n_args], *outs, *refs[n_args + n_more + n_outs + len(through) :])

    return pl.pallas_call(
        body,
        in_specs=specs + [ANY_SPEC] * n_more,
        out_specs=[pl.BlockSpec(memory_space=pltpu.VMEM)] * n_outs + [ANY_SPEC] * len(through),
        out_shape=list(out_shape) + [jax.ShapeDtypeStruct(t.shape, t.dtype) for t in through],
        scratch_shapes=list(scratch),
        input_output_aliases={n_args + len(deps) + i: n_outs + i for i in range(len(through))},
        compiler_params=pltpu.CompilerParams(vmem_limit_bytes=SMALL_LIMIT),
        cost_estimate=COST,
        name=name,
    )(*args, *deps, *through)


def products_kernel(n, info_ref, *refs):
    own, right, across, (right_ref, across_ref) = refs[:n], refs[n : 2 * n], refs[2 * n : -2], refs[-2:]
    half = across_ref.shape[0]
    nt = ((1,), (1,))
    for s in range(2):

        def joined(group, c):
            return jnp.concatenate([r[s * half + c] for r in group], axis=1)

        def step(c, carry):
            right_ref[s * half + c] = dot_dims(joined(own, c), joined(right, c), nt)
            return carry

        def step_across(c, carry):
            other = jnp.concatenate([r[c] for r in across], axis=1)
            across_ref[c] = dot_dims(joined(own, c), other, nt)
            return carry

        lax.fori_loop(0, half, step, 0, unroll=4)

        @pl.when((info_ref[0] < 2) == (s == 0))
        def _():
            lax.fori_loop(0, half, step_across, 0, unroll=4)


def places():
    lane = lax.broadcasted_iota(jnp.int32, (BLK, BLK), 1)
    row = lax.broadcasted_iota(jnp.int32, (BLK, BLK), 0)
    return lane, row


def pack(block):
    lane, row = places()
    rest = jnp.where(lane == row, block - block.astype(BF16).astype(F32), 0.0)
    moved = pltpu.roll(rest, BLK - 1, 0)
    first = pltpu.roll(rest[:8], BLK - 1, 1)
    upper = jnp.where(lane == row + 1, moved, 0.0)
    top = jnp.where((row[:8] == 0) & (lane[:8] == BLK - 1), first, upper[:8])
    upper = jnp.concatenate([top, upper[8:]], axis=0)
    return jnp.where(lane > row, upper, block).astype(BF16)


def unpack(block):
    lane, row = places()
    block = block.astype(F32)
    moved = pltpu.roll(block, 1, 0)
    first = pltpu.roll(block[:8], 1, 1)
    top = jnp.where(row[:8] == 0, first, moved[:8])
    rest = jnp.concatenate([top, moved[8:]], axis=0)
    return jnp.where(lane > row, 0.0, jnp.where(lane == row, block + rest, block))


def known_kernel(info_ref, id_ref, names_ref, out_ref):
    me = info_ref[4]
    count = names_ref.shape[0]
    per = BLK // count
    lane = lax.broadcasted_iota(jnp.int32, out_ref.shape, 1)
    row = lax.broadcasted_iota(jnp.int32, out_ref.shape, 0)
    table = jnp.where((row == 0) & (lane == id_ref[0]), me, 0)
    mine = row == 1 + lax.div(me, per)
    for c in range(count):
        table = jnp.where(mine & (lane == lax.rem(me, per) * count + c), names_ref[c], table)
    out_ref[...] = table


def add_blocks(info_ref, known_ref, names, ref, acc, lanes, widen=lambda block: block):
    core = info_ref[0]

    def add(c, carry):
        p = known_ref[0, names(c)]

        @pl.when(lax.rem(p, 2) == core)
        def _():
            at = lax.div(p, 2)
            acc[at, :, lanes] += widen(ref[c])

        return carry

    lax.fori_loop(0, ref.shape[0], add, 0)


def name_tables(info_ref, known_ref, names_ref, count):
    other = info_ref[4] + 1 - 2 * info_ref[0]
    per = BLK // count
    return [
        lambda c: names_ref[c],
        lambda c: known_ref[1 + lax.div(other, per), lax.rem(other, per) * count + c],
    ]


def emit_y(ny, y, acc, own_ref, sends, narrow):
    def emit(z, carry):
        for d in range(ny):
            block = acc[z * ny + lax.rem(y + d, ny)]
            if d == 0:
                own_ref[z] = block
            else:
                sends[d - 1][z] = narrow(block)
        return carry

    lax.fori_loop(0, own_ref.shape[0], emit, 0)


def scatter_diag_kernel(ny, info_ref, known_ref, names_ref, mine_ref, theirs_ref, own_ref, *rest):
    sends, acc = rest[:-1], rest[-1]
    acc[...] = jnp.zeros_like(acc)
    mine, theirs = name_tables(info_ref, known_ref, names_ref, names_ref.shape[0])
    add_blocks(info_ref, known_ref, mine, mine_ref, acc, slice(None))
    add_blocks(info_ref, known_ref, theirs, theirs_ref, acc, slice(None), unpack)
    emit_y(ny, info_ref[1], acc, own_ref, sends, pack)


def scatter_off_kernel(ny, info_ref, known_ref, names_ref, *refs):
    (mine_ref, across_ref, theirs_ref, their_across_ref, own_ref), rest = refs[:5], refs[5:]
    sends, acc = rest[:-1], rest[-1]
    first = jnp.where(info_ref[3] < 2, 0, across_ref.shape[0])
    acc[...] = jnp.zeros_like(acc)
    tables = name_tables(info_ref, known_ref, names_ref, names_ref.shape[0])
    blocks = ((mine_ref, across_ref), (theirs_ref, their_across_ref))
    for names, (right, across) in zip(tables, blocks):
        add_blocks(info_ref, known_ref, names, right, acc, slice(0, BLK))
        add_blocks(info_ref, known_ref, lambda c: names(first + c), across, acc, slice(BLK, 2 * BLK))
    emit_y(ny, info_ref[1], acc, own_ref, sends, lambda block: block.astype(BF16))


def sum_y_kernel(diag, info_ref, own_ref, *refs):
    got, (out_ref, send_ref) = refs[:-2], refs[-2:]
    widen = unpack if diag else lambda block: block.astype(F32)
    narrow = pack if diag else lambda block: block.astype(BF16)

    def step(at, carry):
        total = own_ref[at]
        for ref in got:
            total += widen(ref[at])
        send_ref[at] = narrow(total)

        @pl.when(at == info_ref[2])
        def _():
            out_ref[...] = total

        return carry

    lax.fori_loop(0, own_ref.shape[0], step, 0)


def sum_z_kernel(info_ref, own_ref, got_ref, *out_refs):
    total = own_ref[...]
    for at in range(got_ref.shape[0]):
        total += jnp.where(info_ref[2] == at, 0.0, got_ref[at].astype(F32))
    for b, ref in enumerate(out_refs):
        ref[...] = total[:, BLK * b : BLK * (b + 1)]


def finish_kernel(info_ref, tile_ref, diag_ref, got_ref, right_ref, across_ref, left_in, across_in, out_ref):
    row, n = info_ref[3], 4
    r = lax.broadcasted_iota(jnp.int32, (BLK, BLK), 0)
    c = lax.broadcasted_iota(jnp.int32, (BLK, BLK), 1)
    low = diag_ref[...]
    for at in range(got_ref.shape[0]):
        low += jnp.where(info_ref[2] == at, 0.0, unpack(got_ref[at]))

    def put(at, value):
        cols = pl.ds(pl.multiple_of(at * BLK, BLK), BLK)
        out_ref[:, cols] = tile_ref[:, cols] - value

    put(row, jnp.where(c > r, low.T, low))
    put(lax.rem(row + 1, n), right_ref[...])
    put(lax.rem(row + 3, n), left_in[...].T)
    put(lax.rem(row + 2, n), across_ref[...] + across_in[...].T)


def ring(n, d):
    return [(i, (i + d) % n) for i in range(n)]


def f32_out(*shape):
    return jax.ShapeDtypeStruct(shape, F32)


def bf16_out(*shape):
    return jax.ShapeDtypeStruct(shape, BF16)


def on_device(diag_blocks, panel_blocks, ancestors, target_ids, target_tiles):
    nz, ny = lax.axis_size("z"), lax.axis_size("y")
    sn, anc, rows, width = panel_blocks.shape
    count = sn * anc
    half = count // sn
    z, y, core, row = (lax.axis_index(a).astype(jnp.int32) for a in ("z", "y", "core", "row"))
    info = jnp.stack([core, y, z, row, (z * ny + y) * 2 + core])
    at_row = row[None]
    panel = panel_blocks.reshape(sn, anc * rows, width)
    names = ancestors.reshape(count)

    def send(blocks, distance):
        return lax.ppermute(blocks, "row", ring(4, distance))

    def blocks(part):
        return part.reshape(-1, rows, part.shape[-1])

    def after_scatter(kernel, args, wide, name, **kwargs):
        return call(
            functools.partial(kernel, ny),
            [info, known, names, *args],
            [f32_out(nz, BLK, wide)] + [bf16_out(nz, BLK, wide)] * (ny - 1),
            [pltpu.VMEM((nz * ny, BLK, wide), F32)],
            name=name,
            smem=3,
            **kwargs,
        )

    def along_y(sends):
        return [lax.ppermute(s, "y", ring(ny, d + 1)) for d, s in enumerate(sends)]

    def sum_y(own, got, name, deps=(), diag=False):
        wide = own.shape[2]
        outs = [f32_out(BLK, wide), bf16_out(nz, BLK, wide)]
        kernel = functools.partial(sum_y_kernel, diag)
        own, sends = call(kernel, [info, own, *got], outs, name=name, deps=deps)
        return own, lax.all_to_all(sends, "z", 0, 0, tiled=True)

    w, solved, rounded, part = first_chunk(at_row, diag_blocks, panel)
    own = [blocks(rounded)]
    right = [send(own[0], -1)]
    hop = send(blocks(part), 1)
    w = second_factor(diag_blocks, w)
    solved, rounded, part, diag, packed = second_chunk(at_row, w, own[0], panel, solved, hop)
    own.append(blocks(rounded))
    right.append(send(own[1], -1))
    across = [send(hop, 1)]
    hop = send(blocks(part), 1)
    their_diag = lax.ppermute(packed, "core", ring(2, 1))

    (known,) = call(
        known_kernel,
        [info, target_ids, names],
        [jax.ShapeDtypeStruct((1 + nz * ny * 2 * count // BLK, BLK), jnp.int32)],
        name="known",
        smem=3,
        deps=[diag, right[0]],
    )
    known = lax.psum(known, COL)
    (hop,) = call(lambda info: None, [info], [], name="pass_on", deps=[known], through=[hop])
    across.append(send(hop, 1))
    own_diag, *sends = after_scatter(scatter_diag_kernel, [diag, their_diag], BLK, "scatter_diag")
    got_diag = along_y(sends)
    off_right, off_across = call(
        functools.partial(products_kernel, len(own)),
        [at_row, *own, *right, *across],
        [f32_out(count, BLK, BLK), f32_out(half, BLK, BLK)],
        name="products",
        deps=[got_diag[0], got_diag[2]],
    )
    their_right = lax.ppermute(off_right, "core", ring(2, 1))
    their_across = lax.ppermute(off_across, "core", ring(2, 1))
    own_off, *sends = after_scatter(
        scatter_off_kernel, [off_right, off_across, their_right, their_across], 2 * BLK, "scatter_off"
    )
    got_off = along_y(sends)
    own_diag, got_diag = sum_y(own_diag, got_diag, "sum_diag", [own_off], diag=True)
    own_off, got_off = sum_y(own_off, got_off, "sum_off", [got_diag])
    off_right, off_across = call(
        sum_z_kernel, [info, own_off, got_off], [f32_out(BLK, BLK)] * 2, name="last_sum"
    )
    from_left = send(off_right, 1)
    from_across = send(off_across, 2)
    (updated,) = call(
        finish_kernel,
        [info, target_tiles.reshape(rows, width), own_diag, got_diag]
        + [off_right, off_across, from_left, from_across],
        [f32_out(rows, width)],
        name="finish",
    )
    return solved.reshape(panel_blocks.shape), updated.reshape(target_tiles.shape)


def solution(mesh):
    devices = mesh.devices
    nz, ny = 8, 4
    fine = Mesh(devices.reshape(nz, ny, 2, devices.shape[1]), ("z", "y", "core", "row"))
    in_specs = (
        P(COL, None, None),
        P(COL, None, "row", None),
        P(COL, None),
        P(COL),
        P(COL, "row", None),
    )
    out_specs = (P(COL, None, "row", None), P(COL, "row", None))
    return jax.shard_map(
        on_device, mesh=fine, in_specs=in_specs, out_specs=out_specs, check_vma=False
    )
```

```python
import functools

import jax
import jax.numpy as jnp
from jax import lax
from jax.experimental import pallas as pl
from jax.experimental.pallas import tpu as pltpu
from jax.sharding import Mesh, PartitionSpec as P

F32 = jnp.float32
BF16 = jnp.bfloat16
BLK = 128
FIRST = 256
PAN = 16
FIRST_LIMIT = 48 * 1024 * 1024
VMEM_LIMIT = 24 * 1024 * 1024
SMALL_LIMIT = 8 * 1024 * 1024
COL = ("z", "y", "core")
COST = pl.CostEstimate(flops=10**6, bytes_accessed=10**4, transcendentals=0)


def split3(x):
    a = x.astype(BF16)
    rest = x - a.astype(F32)
    b = rest.astype(BF16)
    c = (rest - b.astype(F32)).astype(BF16)
    return a, b, c


def split2(x):
    a = x.astype(BF16)
    return a, (x - a.astype(F32)).astype(BF16)


def outer_product(left, right):
    a, b, c = split3(left)
    p, q, r = split3(right)
    return lax.dot_general(
        jnp.concatenate([a, a, a, b, b, c], axis=0),
        jnp.concatenate([p, q, r, p, q, p], axis=0),
        (((0,), (0,)), ((), ())),
        preferred_element_type=F32,
    )


def dot_dims(a, b, dims, precision=None):
    return lax.dot_general(a, b, (dims, ((), ())), precision=precision, preferred_element_type=F32)


def refined_reciprocal(d):
    r = pl.reciprocal(d, approx=True)
    r = r * (2.0 - d * r)
    return r * (2.0 - d * r)


def factor_panel(panel, k):
    half = PAN // 2
    lane1 = lax.broadcasted_iota(jnp.int32, (1, BLK), 1)
    sub = lax.broadcasted_iota(jnp.int32, (half, BLK), 0)
    lane = lax.broadcasted_iota(jnp.int32, (half, BLK), 1)
    top, bot = panel[:half], panel[half:]
    tops = [jnp.broadcast_to(top[:, k + c : k + c + 1], (half, BLK)) for c in range(PAN)]
    bots = [jnp.broadcast_to(bot[:, k + c : k + c + 1], (half, BLK)) for c in range(PAN)]
    diag_top = jnp.ones((half, BLK), F32)
    diag_bot = jnp.ones((half, BLK), F32)
    for i in range(PAN):
        if i < half:
            d = tops[i][i : i + 1]
            r = refined_reciprocal(d)
            mt = jnp.where(sub > i, tops[i] * r, 0.0)
            mb = bots[i] * r
            diag_top = jnp.where(sub == i, d, diag_top)
            for c in range(i + 1, PAN):
                row = tops[c][i : i + 1]
                tops[c] = tops[c] - mt * row
                bots[c] = bots[c] - mb * row
            pivot = top[i : i + 1] + jnp.where(lane1 == k + i, 1.0, 0.0)
            top = top - mt * pivot
            bot = bot - mb * pivot
        else:
            h = i - half
            d = bots[i][h : h + 1]
            r = refined_reciprocal(d)
            mb = jnp.where(sub > h, bots[i] * r, 0.0)
            diag_bot = jnp.where(sub == h, d, diag_bot)
            for c in range(i + 1, PAN):
                bots[c] = bots[c] - mb * bots[c][h : h + 1]
            pivot = bot[h : h + 1] + jnp.where(lane1 == k + i, 1.0, 0.0)
            bot = bot - mb * pivot

    def finish(rows, diag, first):
        at = lane - k - first
        rows = jnp.where(at == sub, 1.0, jnp.where((at > sub) & (lane < k + PAN), 0.0, rows))
        return rows * lax.rsqrt(diag)

    return jnp.concatenate([finish(top, diag_top, 0), finish(bot, diag_bot, half)], axis=0)


def factor_blocks(blocks):
    mats = list(blocks)
    done = [[] for _ in mats]
    for k in range(0, BLK, PAN):
        lane = lax.broadcasted_iota(jnp.int32, (PAN, BLK), 1)
        for s in range(len(mats)):
            rows = factor_panel(mats[s][:PAN], k)
            done[s].append(jnp.where(lane < k + PAN, rows, 0.0))
            if k + PAN < BLK:
                ahead = jnp.where(lane >= k + PAN, rows, 0.0)
                rest = mats[s][PAN:]
                at = lax.broadcasted_iota(jnp.int32, rest.shape, 1)
                rest = jnp.where((at >= k) & (at < k + PAN), 0.0, rest)
                mats[s] = rest - outer_product(ahead, rows)[k + PAN :]
    return [jnp.concatenate(rows, axis=0) for rows in done]


def factor_rows(k, s, row, w_prev):
    if not k:
        return row
    lane = lax.broadcasted_iota(jnp.int32, row.shape, 1)
    left = jnp.concatenate([w[:, BLK * k : BLK * (k + 1)] for w in w_prev], axis=0)
    right = jnp.concatenate(
        [jnp.where((lane >= BLK * (i + 1)) & (lane < BLK * k), 0.0, w) for i, w in enumerate(w_prev)],
        axis=0,
    )
    row = jnp.where(lane < BLK * k, 0.0, row)
    return row - dot_dims(left, right, ((0,), (0,)), lax.Precision.HIGHEST)


def factor_part(first, sn, diag_ref, *refs):
    w_ref = refs[-1]
    width = diag_ref.shape[2]
    w_prev = [
        [w[s, BLK * i : BLK * (i + 1), :] for w in refs[:-1] for i in range(w.shape[1] // BLK)]
        for s in range(sn)
    ]
    for at in range(diag_ref.shape[1] // BLK):
        k = first + at
        here = slice(BLK * k, BLK * (k + 1))
        rows = [
            factor_rows(k, s, diag_ref[s, BLK * at : BLK * (at + 1), :], w_prev[s]) for s in range(sn)
        ]
        inverses = factor_blocks([row[:, here] for row in rows])
        for s in range(sn):
            scaled = dot_dims(inverses[s], rows[s], ((1,), (0,)), lax.Precision.HIGHEST)
            lane = lax.broadcasted_iota(jnp.int32, (BLK, width), 1)
            inside = (lane >= BLK * k) & (lane < BLK * (k + 1))
            spread = jnp.concatenate([inverses[s]] * (width // BLK), axis=1)
            scaled = jnp.where(inside, spread, scaled)
            w_prev[s].append(scaled)
            w_ref[s, BLK * at : BLK * (at + 1), :] = scaled


def solve_part(start, stop, sn, info_ref, w_ref, b_ref, x_ref, r_refs, half_ref):
    tile = 256
    nt = ((1,), (1,))
    for s in range(sn):
        lane = lax.broadcasted_iota(jnp.int32, (stop - start, stop), 1)
        row = lax.broadcasted_iota(jnp.int32, (stop - start, stop), 0) + start
        w_hi, w_lo = split2(jnp.where(lane <= row, w_ref[s, :, :stop], 0.0))

        def step(t, carry):
            at = pl.ds(pl.multiple_of(t * tile, tile), tile)
            b_hi, b_lo = split2(b_ref[s, at, :])
            x = dot_dims(b_hi, w_hi, nt) + (dot_dims(b_hi, w_lo, nt) + dot_dims(b_lo, w_hi, nt))
            x_ref[s, at, :] = x
            r_refs[s][at, :] = x.astype(BF16)
            return carry

        lax.fori_loop(0, b_ref.shape[1] // tile, step, 0, unroll=True)
    chosen = jnp.where(info_ref[0] < 2, r_refs[1][...], r_refs[0][...])
    half_ref[...] = chosen


def first_kernel(sn, info_ref, diag_ref, b_hbm, w_ref, x_ref, r_ref, half_ref, b_ref, sem):
    copy = pltpu.make_async_copy(b_hbm.at[:, :, pl.ds(0, FIRST)], b_ref, sem)
    copy.start()
    factor_part(0, sn, diag_ref, w_ref)
    copy.wait()
    r_refs = [r_ref.at[s] for s in range(sn)]
    solve_part(0, FIRST, sn, info_ref, w_ref, b_ref, x_ref, r_refs, half_ref)


def second_kernel(sn, info_ref, w_ref, own_ref, b_ref, hop_ref, _, x_ref, r_ref, both_ref, product_ref, packed_ref):
    for c in range(hop_ref.shape[0]):
        both_ref[BLK * c : BLK * (c + 1), :FIRST] = hop_ref[c]
    half_ref = both_ref.at[:, pl.ds(FIRST, FIRST)]
    r_refs = [r_ref.at[s] for s in range(sn)]
    solve_part(FIRST, b_ref.shape[2], sn, info_ref, w_ref, b_ref, x_ref, r_refs, half_ref)
    anc = b_ref.shape[1] // BLK
    for s in range(sn):

        def square(c, carry):
            at = pl.ds(pl.multiple_of(c * BLK, BLK), BLK)
            mine = jnp.concatenate([own_ref[s * anc + c], r_refs[s][at, :]], axis=1)
            product = dot_dims(mine, mine, ((1,), (1,)))
            product_ref[s * anc + c] = product
            packed_ref[s * anc + c] = pack(product)
            return carry

        lax.fori_loop(0, anc, square, 0, unroll=4)


def whole(shape):
    return pl.BlockSpec(shape, lambda i: (0,) * len(shape))


def grid_call(kernel, args, in_specs, outs, name, scratch, limit, aliases={}):
    return pl.pallas_call(
        kernel,
        grid=(1,),
        in_specs=in_specs,
        out_specs=[spec for spec, _ in outs],
        out_shape=[shape for _, shape in outs],
        scratch_shapes=list(scratch),
        input_output_aliases=aliases,
        compiler_params=pltpu.CompilerParams(vmem_limit_bytes=limit),
        cost_estimate=COST,
        name=name,
    )(*args)


SMEM_SPEC = pl.BlockSpec(memory_space=pltpu.SMEM)
ANY_SPEC = pl.BlockSpec(memory_space=pl.ANY)


def first_chunk(row, diag_blocks, panel):
    sn, rows, width = panel.shape
    return grid_call(
        functools.partial(first_kernel, sn),
        [row, diag_blocks, panel],
        [SMEM_SPEC, pl.BlockSpec((sn, FIRST, width), lambda i: (0, 0, 0)), ANY_SPEC],
        [
            (whole((sn, FIRST, width)), f32_out(sn, FIRST, width)),
            (pl.BlockSpec((sn, rows, FIRST), lambda i: (0, 0, 0)), f32_out(sn, rows, width)),
            (whole((sn, rows, FIRST)), bf16_out(sn, rows, FIRST)),
            (whole((rows, FIRST)), bf16_out(rows, FIRST)),
        ],
        "first_chunk",
        [pltpu.VMEM((sn, rows, FIRST), F32), pltpu.SemaphoreType.DMA],
        FIRST_LIMIT,
    )


def second_factor(diag_blocks, w):
    sn, _, width = diag_blocks.shape
    return grid_call(
        functools.partial(factor_part, FIRST // BLK, sn),
        [diag_blocks, w],
        [pl.BlockSpec((sn, FIRST, width), lambda i: (0, 1, 0)), whole(w.shape)],
        [(whole(w.shape), f32_out(*w.shape))],
        "second_factor",
        [],
        VMEM_LIMIT,
    )[0]


def second_chunk(row, w, own, panel, hop, solved):
    sn, rows, width = panel.shape
    count = own.shape[0]
    return grid_call(
        functools.partial(second_kernel, sn),
        [row, w, own, panel, hop, solved],
        [SMEM_SPEC, whole(w.shape), whole(own.shape), whole(panel.shape), whole(hop.shape), ANY_SPEC],
        [
            (pl.BlockSpec((sn, rows, FIRST), lambda i: (0, 0, 1)), f32_out(sn, rows, width)),
            (whole((sn, rows, FIRST)), bf16_out(sn, rows, FIRST)),
            (whole((rows, width)), bf16_out(rows, width)),
            (whole((count, BLK, BLK)), f32_out(count, BLK, BLK)),
            (whole((count, BLK, BLK)), bf16_out(count, BLK, BLK)),
        ],
        "second_chunk",
        [],
        VMEM_LIMIT,
        {5: 0},
    )


def call(kernel, args, out_shape, scratch=(), name=None, smem=1, deps=(), through=()):
    n_args, n_more = len(args), len(deps) + len(through)
    n_outs = len(out_shape)
    specs = [SMEM_SPEC] * smem
    specs += [pl.BlockSpec(memory_space=pltpu.VMEM)] * (n_args - smem)

    def body(*refs):
        outs = refs[n_args + n_more : n_args + n_more + n_outs]
        kernel(*refs[:n_args], *outs, *refs[n_args + n_more + n_outs + len(through) :])

    return pl.pallas_call(
        body,
        in_specs=specs + [ANY_SPEC] * n_more,
        out_specs=[pl.BlockSpec(memory_space=pltpu.VMEM)] * n_outs + [ANY_SPEC] * len(through),
        out_shape=list(out_shape) + [jax.ShapeDtypeStruct(t.shape, t.dtype) for t in through],
        scratch_shapes=list(scratch),
        input_output_aliases={n_args + len(deps) + i: n_outs + i for i in range(len(through))},
        compiler_params=pltpu.CompilerParams(vmem_limit_bytes=SMALL_LIMIT),
        cost_estimate=COST,
        name=name,
    )(*args, *deps, *through)


def products_kernel(n, info_ref, *refs):
    own, right, (near_ref, far_ref, *outs) = refs[:n], refs[n : 2 * n], refs[2 * n :]
    right_ref, across_ref, right_send, across_send = outs
    half = across_ref.shape[0]
    nt = ((1,), (1,))
    for s in range(2):

        def joined(group, c):
            return jnp.concatenate([r[s * half + c] for r in group], axis=1)

        def step(c, carry):
            product = dot_dims(joined(own, c), joined(right, c), nt)
            right_ref[s * half + c] = product
            right_send[s * half + c] = product.astype(BF16)
            return carry

        def step_across(c, carry):
            other = jnp.concatenate([near_ref[c, :, :FIRST], far_ref[c]], axis=1)
            product = dot_dims(joined(own, c), other, nt)
            across_ref[c] = product
            across_send[c] = product.astype(BF16)
            return carry

        lax.fori_loop(0, half, step, 0, unroll=4)

        @pl.when((info_ref[0] < 2) == (s == 0))
        def _():
            lax.fori_loop(0, half, step_across, 0, unroll=4)


def places():
    lane = lax.broadcasted_iota(jnp.int32, (BLK, BLK), 1)
    row = lax.broadcasted_iota(jnp.int32, (BLK, BLK), 0)
    return lane, row


def pack(block):
    lane, row = places()
    rest = jnp.where(lane == row, block - block.astype(BF16).astype(F32), 0.0)
    moved = pltpu.roll(rest, BLK - 1, 0)
    first = pltpu.roll(rest[:8], BLK - 1, 1)
    upper = jnp.where(lane == row + 1, moved, 0.0)
    top = jnp.where((row[:8] == 0) & (lane[:8] == BLK - 1), first, upper[:8])
    upper = jnp.concatenate([top, upper[8:]], axis=0)
    return jnp.where(lane > row, upper, block).astype(BF16)


def unpack(block):
    lane, row = places()
    block = block.astype(F32)
    moved = pltpu.roll(block, 1, 0)
    first = pltpu.roll(block[:8], 1, 1)
    top = jnp.where(row[:8] == 0, first, moved[:8])
    rest = jnp.concatenate([top, moved[8:]], axis=0)
    return jnp.where(lane > row, 0.0, jnp.where(lane == row, block + rest, block))


def pass_on_kernel(hop_ref, part_ref):
    part_ref[...] = hop_ref[:, :, FIRST:]


def known_kernel(info_ref, id_ref, names_ref, out_ref):
    me = info_ref[4]
    count = names_ref.shape[0]
    per = BLK // count
    lane = lax.broadcasted_iota(jnp.int32, out_ref.shape, 1)
    row = lax.broadcasted_iota(jnp.int32, out_ref.shape, 0)
    table = jnp.where((row == 0) & (lane == id_ref[0]), me, 0)
    mine = row == 1 + lax.div(me, per)
    for c in range(count):
        table = jnp.where(mine & (lane == lax.rem(me, per) * count + c), names_ref[c], table)
    out_ref[...] = table


def add_blocks(info_ref, known_ref, names, ref, acc, lanes, widen=lambda block: block):
    core = info_ref[0]

    def add(c, carry):
        p = known_ref[0, names(c)]

        @pl.when(lax.rem(p, 2) == core)
        def _():
            at = lax.div(p, 2)
            acc[at, :, lanes] += widen(ref[c]).astype(F32)

        return carry

    lax.fori_loop(0, ref.shape[0], add, 0)


def name_tables(info_ref, known_ref, names_ref, count):
    other = info_ref[4] + 1 - 2 * info_ref[0]
    per = BLK // count
    return [
        lambda c: names_ref[c],
        lambda c: known_ref[1 + lax.div(other, per), lax.rem(other, per) * count + c],
    ]


def emit_y(ny, y, acc, own_ref, sends, narrow):
    def emit(z, carry):
        for d in range(ny):
            block = acc[z * ny + lax.rem(y + d, ny)]
            if d == 0:
                own_ref[z] = block
            else:
                sends[d - 1][z] = narrow(block)
        return carry

    lax.fori_loop(0, own_ref.shape[0], emit, 0)


def scatter_diag_kernel(ny, info_ref, known_ref, names_ref, mine_ref, theirs_ref, own_ref, *rest):
    sends, acc = rest[:-1], rest[-1]
    acc[...] = jnp.zeros_like(acc)
    mine, theirs = name_tables(info_ref, known_ref, names_ref, names_ref.shape[0])
    add_blocks(info_ref, known_ref, mine, mine_ref, acc, slice(None))
    add_blocks(info_ref, known_ref, theirs, theirs_ref, acc, slice(None), unpack)
    emit_y(ny, info_ref[1], acc, own_ref, sends, pack)


def scatter_off_kernel(ny, info_ref, known_ref, names_ref, *refs):
    (mine_ref, across_ref, theirs_ref, their_across_ref, own_ref), rest = refs[:5], refs[5:]
    sends, acc = rest[:-1], rest[-1]
    first = jnp.where(info_ref[3] < 2, 0, across_ref.shape[0])
    acc[...] = jnp.zeros_like(acc)
    tables = name_tables(info_ref, known_ref, names_ref, names_ref.shape[0])
    blocks = ((mine_ref, across_ref), (theirs_ref, their_across_ref))
    for names, (right, across) in zip(tables, blocks):
        add_blocks(info_ref, known_ref, names, right, acc, slice(0, BLK))
        add_blocks(info_ref, known_ref, lambda c: names(first + c), across, acc, slice(BLK, 2 * BLK))
    emit_y(ny, info_ref[1], acc, own_ref, sends, lambda block: block.astype(BF16))


def sum_y_kernel(diag, info_ref, own_ref, *refs):
    got, (out_ref, send_ref) = refs[:-2], refs[-2:]
    widen = unpack if diag else lambda block: block.astype(F32)
    narrow = pack if diag else lambda block: block.astype(BF16)

    def step(at, carry):
        total = own_ref[at]
        for ref in got:
            total += widen(ref[at])
        send_ref[at] = narrow(total)

        @pl.when(at == info_ref[2])
        def _():
            out_ref[...] = total

        return carry

    lax.fori_loop(0, own_ref.shape[0], step, 0)


def sum_z_kernel(info_ref, own_ref, got_ref, *out_refs):
    total = own_ref[...]
    for at in range(got_ref.shape[0]):
        total += jnp.where(info_ref[2] == at, 0.0, got_ref[at].astype(F32))
    for b, ref in enumerate(out_refs):
        ref[...] = total[:, BLK * b : BLK * (b + 1)]


def finish_kernel(info_ref, tile_ref, diag_ref, got_ref, right_ref, across_ref, left_in, across_in, out_ref):
    row, n = info_ref[3], 4
    r = lax.broadcasted_iota(jnp.int32, (BLK, BLK), 0)
    c = lax.broadcasted_iota(jnp.int32, (BLK, BLK), 1)
    low = diag_ref[...]
    for at in range(got_ref.shape[0]):
        low += jnp.where(info_ref[2] == at, 0.0, unpack(got_ref[at]))

    def put(at, value):
        cols = pl.ds(pl.multiple_of(at * BLK, BLK), BLK)
        out_ref[:, cols] = tile_ref[:, cols] - value

    put(row, jnp.where(c > r, low.T, low))
    put(lax.rem(row + 1, n), right_ref[...])
    put(lax.rem(row + 3, n), left_in[...].T)
    put(lax.rem(row + 2, n), across_ref[...] + across_in[...].T)


def ring(n, d):
    return [(i, (i + d) % n) for i in range(n)]


def f32_out(*shape):
    return jax.ShapeDtypeStruct(shape, F32)


def bf16_out(*shape):
    return jax.ShapeDtypeStruct(shape, BF16)


def on_device(diag_blocks, panel_blocks, ancestors, target_ids, target_tiles):
    nz, ny = lax.axis_size("z"), lax.axis_size("y")
    sn, anc, rows, width = panel_blocks.shape
    count = sn * anc
    half = count // sn
    z, y, core, row = (lax.axis_index(a).astype(jnp.int32) for a in ("z", "y", "core", "row"))
    info = jnp.stack([core, y, z, row, (z * ny + y) * 2 + core])
    at_row = row[None]
    panel = panel_blocks.reshape(sn, anc * rows, width)
    names = ancestors.reshape(count)

    def send(blocks, distance):
        return lax.ppermute(blocks, "row", ring(4, distance))

    def blocks(part):
        return part.reshape(-1, rows, part.shape[-1])

    def after_scatter(kernel, args, wide, name, **kwargs):
        return call(
            functools.partial(kernel, ny),
            [info, known, names, *args],
            [f32_out(nz, BLK, wide)] + [bf16_out(nz, BLK, wide)] * (ny - 1),
            [pltpu.VMEM((nz * ny, BLK, wide), F32)],
            name=name,
            smem=3,
            **kwargs,
        )

    def along_y(sends):
        return [lax.ppermute(s, "y", ring(ny, d + 1)) for d, s in enumerate(sends)]

    def sum_y(own, got, name, deps=(), diag=False):
        wide = own.shape[2]
        outs = [f32_out(BLK, wide), bf16_out(nz, BLK, wide)]
        kernel = functools.partial(sum_y_kernel, diag)
        own, sends = call(kernel, [info, own, *got], outs, name=name, deps=deps)
        return own, lax.all_to_all(sends, "z", 0, 0, tiled=True)

    w, solved, rounded, part = first_chunk(at_row, diag_blocks, panel)
    own = [blocks(rounded)]
    right = [send(own[0], -1)]
    hop = send(blocks(part), 1)
    w = second_factor(diag_blocks, w)
    solved, rounded, part, diag, packed = second_chunk(at_row, w, own[0], panel, hop, solved)
    own.append(blocks(rounded))
    right.append(send(own[1], -1))
    hop = send(blocks(part), 1)
    their_diag = lax.ppermute(packed, "core", ring(2, 1))

    (known,) = call(
        known_kernel,
        [info, target_ids, names],
        [jax.ShapeDtypeStruct((1 + nz * ny * 2 * count // BLK, BLK), jnp.int32)],
        name="known",
        smem=3,
        deps=[diag, right[0]],
    )
    known = lax.psum(known, COL)
    (part,) = call(pass_on_kernel, [hop], [bf16_out(half, rows, FIRST)], name="pass_on", smem=0, deps=[known])
    across = [hop, send(part, 1)]
    own_diag, *sends = after_scatter(scatter_diag_kernel, [diag, their_diag], BLK, "scatter_diag")
    got_diag = along_y(sends)
    off_right, off_across, send_right, send_across = call(
        functools.partial(products_kernel, len(own)),
        [at_row, *own, *right, *across],
        [out(n, BLK, BLK) for out in (f32_out, bf16_out) for n in (count, half)],
        name="products",
        deps=[got_diag[0], got_diag[2]],
    )
    their_right = lax.ppermute(send_right, "core", ring(2, 1))
    their_across = lax.ppermute(send_across, "core", ring(2, 1))
    own_off, *sends = after_scatter(
        scatter_off_kernel, [off_right, off_across, their_right, their_across], 2 * BLK, "scatter_off"
    )
    got_off = along_y(sends)
    own_diag, got_diag = sum_y(own_diag, got_diag, "sum_diag", [own_off], diag=True)
    own_off, got_off = sum_y(own_off, got_off, "sum_off", [got_diag])
    off_right, off_across = call(
        sum_z_kernel, [info, own_off, got_off], [f32_out(BLK, BLK)] * 2, name="last_sum"
    )
    from_left = send(off_right, 1)
    from_across = send(off_across, 2)
    (updated,) = call(
        finish_kernel,
        [info, target_tiles.reshape(rows, width), own_diag, got_diag]
        + [off_right, off_across, from_left, from_across],
        [f32_out(rows, width)],
        name="finish",
    )
    return solved.reshape(panel_blocks.shape), updated.reshape(target_tiles.shape)


def solution(mesh):
    devices = mesh.devices
    nz, ny = 8, 4
    fine = Mesh(devices.reshape(nz, ny, 2, devices.shape[1]), ("z", "y", "core", "row"))
    in_specs = (
        P(COL, None, None),
        P(COL, None, "row", None),
        P(COL, None),
        P(COL),
        P(COL, "row", None),
    )
    out_specs = (P(COL, None, "row", None), P(COL, "row", None))
    return jax.shard_map(
        on_device, mesh=fine, in_specs=in_specs, out_specs=out_specs, check_vma=False
    )
```

```python
import functools

import jax
import jax.numpy as jnp
from jax import lax
from jax.experimental import pallas as pl
from jax.experimental.pallas import tpu as pltpu
from jax.sharding import Mesh, PartitionSpec as P

F32 = jnp.float32
BF16 = jnp.bfloat16
BLK = 128
FIRST = 256
PAN = 16
FIRST_LIMIT = 48 * 1024 * 1024
VMEM_LIMIT = 24 * 1024 * 1024
SMALL_LIMIT = 8 * 1024 * 1024
COL = ("z", "y", "core")
COST = pl.CostEstimate(flops=10**6, bytes_accessed=10**4, transcendentals=0)


def split3(x):
    a = x.astype(BF16)
    rest = x - a.astype(F32)
    b = rest.astype(BF16)
    c = (rest - b.astype(F32)).astype(BF16)
    return a, b, c


def split2(x):
    a = x.astype(BF16)
    return a, (x - a.astype(F32)).astype(BF16)


def outer_product(left, right):
    a, b, c = split3(left)
    p, q, r = split3(right)
    return lax.dot_general(
        jnp.concatenate([a, a, a, b, b, c], axis=0),
        jnp.concatenate([p, q, r, p, q, p], axis=0),
        (((0,), (0,)), ((), ())),
        preferred_element_type=F32,
    )


def dot_dims(a, b, dims, precision=None):
    return lax.dot_general(a, b, (dims, ((), ())), precision=precision, preferred_element_type=F32)


def refined_reciprocal(d):
    r = pl.reciprocal(d, approx=True)
    r = r * (2.0 - d * r)
    return r * (2.0 - d * r)


def factor_panel(panel, k):
    half = PAN // 2
    lane1 = lax.broadcasted_iota(jnp.int32, (1, BLK), 1)
    sub = lax.broadcasted_iota(jnp.int32, (half, BLK), 0)
    lane = lax.broadcasted_iota(jnp.int32, (half, BLK), 1)
    top, bot = panel[:half], panel[half:]
    tops = [jnp.broadcast_to(top[:, k + c : k + c + 1], (half, BLK)) for c in range(PAN)]
    bots = [jnp.broadcast_to(bot[:, k + c : k + c + 1], (half, BLK)) for c in range(PAN)]
    diag_top = jnp.ones((half, BLK), F32)
    diag_bot = jnp.ones((half, BLK), F32)
    for i in range(PAN):
        if i < half:
            d = tops[i][i : i + 1]
            r = refined_reciprocal(d)
            mt = jnp.where(sub > i, tops[i] * r, 0.0)
            mb = bots[i] * r
            diag_top = jnp.where(sub == i, d, diag_top)
            for c in range(i + 1, PAN):
                row = tops[c][i : i + 1]
                tops[c] = tops[c] - mt * row
                bots[c] = bots[c] - mb * row
            pivot = top[i : i + 1] + jnp.where(lane1 == k + i, 1.0, 0.0)
            top = top - mt * pivot
            bot = bot - mb * pivot
        else:
            h = i - half
            d = bots[i][h : h + 1]
            r = refined_reciprocal(d)
            mb = jnp.where(sub > h, bots[i] * r, 0.0)
            diag_bot = jnp.where(sub == h, d, diag_bot)
            for c in range(i + 1, PAN):
                bots[c] = bots[c] - mb * bots[c][h : h + 1]
            pivot = bot[h : h + 1] + jnp.where(lane1 == k + i, 1.0, 0.0)
            bot = bot - mb * pivot

    def finish(rows, diag, first):
        at = lane - k - first
        rows = jnp.where(at == sub, 1.0, jnp.where((at > sub) & (lane < k + PAN), 0.0, rows))
        return rows * lax.rsqrt(diag)

    return jnp.concatenate([finish(top, diag_top, 0), finish(bot, diag_bot, half)], axis=0)


def factor_blocks(blocks):
    mats = list(blocks)
    done = [[] for _ in mats]
    for k in range(0, BLK, PAN):
        lane = lax.broadcasted_iota(jnp.int32, (PAN, BLK), 1)
        for s in range(len(mats)):
            rows = factor_panel(mats[s][:PAN], k)
            done[s].append(jnp.where(lane < k + PAN, rows, 0.0))
            if k + PAN < BLK:
                ahead = jnp.where(lane >= k + PAN, rows, 0.0)
                rest = mats[s][PAN:]
                at = lax.broadcasted_iota(jnp.int32, rest.shape, 1)
                rest = jnp.where((at >= k) & (at < k + PAN), 0.0, rest)
                mats[s] = rest - outer_product(ahead, rows)[k + PAN :]
    return [jnp.concatenate(rows, axis=0) for rows in done]


def factor_rows(k, s, row, w_prev):
    if not k:
        return row
    lane = lax.broadcasted_iota(jnp.int32, row.shape, 1)
    left = jnp.concatenate([w[:, BLK * k : BLK * (k + 1)] for w in w_prev], axis=0)
    right = jnp.concatenate(
        [jnp.where((lane >= BLK * (i + 1)) & (lane < BLK * k), 0.0, w) for i, w in enumerate(w_prev)],
        axis=0,
    )
    row = jnp.where(lane < BLK * k, 0.0, row)
    return row - dot_dims(left, right, ((0,), (0,)), lax.Precision.HIGHEST)


def factor_part(first, sn, diag_ref, *refs):
    w_ref = refs[-1]
    width = diag_ref.shape[2]
    w_prev = [
        [w[s, BLK * i : BLK * (i + 1), :] for w in refs[:-1] for i in range(w.shape[1] // BLK)]
        for s in range(sn)
    ]
    for at in range(diag_ref.shape[1] // BLK):
        k = first + at
        here = slice(BLK * k, BLK * (k + 1))
        rows = [
            factor_rows(k, s, diag_ref[s, BLK * at : BLK * (at + 1), :], w_prev[s]) for s in range(sn)
        ]
        inverses = factor_blocks([row[:, here] for row in rows])
        for s in range(sn):
            scaled = dot_dims(inverses[s], rows[s], ((1,), (0,)), lax.Precision.HIGHEST)
            lane = lax.broadcasted_iota(jnp.int32, (BLK, width), 1)
            inside = (lane >= BLK * k) & (lane < BLK * (k + 1))
            spread = jnp.concatenate([inverses[s]] * (width // BLK), axis=1)
            scaled = jnp.where(inside, spread, scaled)
            w_prev[s].append(scaled)
            w_ref[s, BLK * at : BLK * (at + 1), :] = scaled


def solve_part(start, stop, sn, info_ref, w_ref, b_ref, x_ref, r_refs, half_ref):
    tile = 256
    nt = ((1,), (1,))
    for s in range(sn):
        lane = lax.broadcasted_iota(jnp.int32, (stop - start, stop), 1)
        row = lax.broadcasted_iota(jnp.int32, (stop - start, stop), 0) + start
        w_hi, w_lo = split2(jnp.where(lane <= row, w_ref[s, :, :stop], 0.0))

        def step(t, carry):
            at = pl.ds(pl.multiple_of(t * tile, tile), tile)
            b_hi, b_lo = split2(b_ref[s, at, :])
            x = dot_dims(b_hi, w_hi, nt) + (dot_dims(b_hi, w_lo, nt) + dot_dims(b_lo, w_hi, nt))
            x_ref[s, at, :] = x
            r_refs[s][at, :] = x.astype(BF16)
            return carry

        lax.fori_loop(0, b_ref.shape[1] // tile, step, 0, unroll=True)
    chosen = jnp.where(info_ref[0] < 2, r_refs[1][...], r_refs[0][...])
    half_ref[...] = chosen


def first_kernel(sn, info_ref, diag_ref, b_hbm, w_ref, x_ref, r_ref, half_ref, b_ref, sem):
    copy = pltpu.make_async_copy(b_hbm.at[:, :, pl.ds(0, FIRST)], b_ref, sem)
    copy.start()
    factor_part(0, sn, diag_ref, w_ref)
    copy.wait()
    r_refs = [r_ref.at[s] for s in range(sn)]
    solve_part(0, FIRST, sn, info_ref, w_ref, b_ref, x_ref, r_refs, half_ref)


def second_kernel(sn, info_ref, w_ref, own_ref, b_ref, *refs):
    x_ref, r_ref, half_ref, product_ref, packed_ref = refs[2:]
    r_refs = [r_ref.at[s] for s in range(sn)]
    solve_part(FIRST, b_ref.shape[2], sn, info_ref, w_ref, b_ref, x_ref, r_refs, half_ref)
    anc = b_ref.shape[1] // BLK
    for s in range(sn):

        def square(c, carry):
            at = pl.ds(pl.multiple_of(c * BLK, BLK), BLK)
            mine = jnp.concatenate([own_ref[s * anc + c], r_refs[s][at, :]], axis=1)
            product = dot_dims(mine, mine, ((1,), (1,)))
            product_ref[s * anc + c] = product
            packed_ref[s * anc + c] = pack(product)
            return carry

        lax.fori_loop(0, anc, square, 0, unroll=4)


def whole(shape):
    return pl.BlockSpec(shape, lambda i: (0,) * len(shape))


def grid_call(kernel, args, in_specs, outs, name, scratch, limit, aliases={}):
    return pl.pallas_call(
        kernel,
        grid=(1,),
        in_specs=in_specs,
        out_specs=[spec for spec, _ in outs],
        out_shape=[shape for _, shape in outs],
        scratch_shapes=list(scratch),
        input_output_aliases=aliases,
        compiler_params=pltpu.CompilerParams(vmem_limit_bytes=limit),
        cost_estimate=COST,
        name=name,
    )(*args)


SMEM_SPEC = pl.BlockSpec(memory_space=pltpu.SMEM)
ANY_SPEC = pl.BlockSpec(memory_space=pl.ANY)


def first_chunk(row, diag_blocks, panel):
    sn, rows, width = panel.shape
    return grid_call(
        functools.partial(first_kernel, sn),
        [row, diag_blocks, panel],
        [SMEM_SPEC, pl.BlockSpec((sn, FIRST, width), lambda i: (0, 0, 0)), ANY_SPEC],
        [
            (whole((sn, FIRST, width)), f32_out(sn, FIRST, width)),
            (pl.BlockSpec((sn, rows, FIRST), lambda i: (0, 0, 0)), f32_out(sn, rows, width)),
            (whole((sn, rows, FIRST)), bf16_out(sn, rows, FIRST)),
            (whole((rows, FIRST)), bf16_out(rows, FIRST)),
        ],
        "first_chunk",
        [pltpu.VMEM((sn, rows, FIRST), F32), pltpu.SemaphoreType.DMA],
        FIRST_LIMIT,
    )


def second_factor(diag_blocks, w):
    sn, _, width = diag_blocks.shape
    return grid_call(
        functools.partial(factor_part, FIRST // BLK, sn),
        [diag_blocks, w],
        [pl.BlockSpec((sn, FIRST, width), lambda i: (0, 1, 0)), whole(w.shape)],
        [(whole(w.shape), f32_out(*w.shape))],
        "second_factor",
        [],
        VMEM_LIMIT,
    )[0]


def second_chunk(row, w, own, panel, solved, dep):
    sn, rows, width = panel.shape
    count = own.shape[0]
    return grid_call(
        functools.partial(second_kernel, sn),
        [row, w, own, panel, solved, dep],
        [SMEM_SPEC, whole(w.shape), whole(own.shape), whole(panel.shape), ANY_SPEC, ANY_SPEC],
        [
            (pl.BlockSpec((sn, rows, FIRST), lambda i: (0, 0, 1)), f32_out(sn, rows, width)),
            (whole((sn, rows, FIRST)), bf16_out(sn, rows, FIRST)),
            (whole((rows, FIRST)), bf16_out(rows, FIRST)),
            (whole((count, BLK, BLK)), f32_out(count, BLK, BLK)),
            (whole((count, BLK, BLK)), bf16_out(count, BLK, BLK)),
        ],
        "second_chunk",
        [],
        VMEM_LIMIT,
        {4: 0},
    )


def call(kernel, args, out_shape, scratch=(), name=None, smem=1, deps=(), through=()):
    n_args, n_more = len(args), len(deps) + len(through)
    n_outs = len(out_shape)
    specs = [SMEM_SPEC] * smem
    specs += [pl.BlockSpec(memory_space=pltpu.VMEM)] * (n_args - smem)

    def body(*refs):
        outs = refs[n_args + n_more : n_args + n_more + n_outs]
        kernel(*refs[:n_args], *outs, *refs[n_args + n_more + n_outs + len(through) :])

    return pl.pallas_call(
        body,
        in_specs=specs + [ANY_SPEC] * n_more,
        out_specs=[pl.BlockSpec(memory_space=pltpu.VMEM)] * n_outs + [ANY_SPEC] * len(through),
        out_shape=list(out_shape) + [jax.ShapeDtypeStruct(t.shape, t.dtype) for t in through],
        scratch_shapes=list(scratch),
        input_output_aliases={n_args + len(deps) + i: n_outs + i for i in range(len(through))},
        compiler_params=pltpu.CompilerParams(vmem_limit_bytes=SMALL_LIMIT),
        cost_estimate=COST,
        name=name,
    )(*args, *deps, *through)


def products_kernel(n, info_ref, *refs):
    own, right, across, outs = refs[:n], refs[n : 2 * n], refs[2 * n : -4], refs[-4:]
    right_ref, across_ref, right_send, across_send = outs
    half = across_ref.shape[0]
    nt = ((1,), (1,))
    for s in range(2):

        def joined(group, c):
            return jnp.concatenate([r[s * half + c] for r in group], axis=1)

        def step(c, carry):
            product = dot_dims(joined(own, c), joined(right, c), nt)
            right_ref[s * half + c] = product
            right_send[s * half + c] = product.astype(BF16)
            return carry

        def step_across(c, carry):
            other = jnp.concatenate([r[c] for r in across], axis=1)
            product = dot_dims(joined(own, c), other, nt)
            across_ref[c] = product
            across_send[c] = product.astype(BF16)
            return carry

        lax.fori_loop(0, half, step, 0, unroll=4)

        @pl.when((info_ref[0] < 2) == (s == 0))
        def _():
            lax.fori_loop(0, half, step_across, 0, unroll=4)


def places():
    lane = lax.broadcasted_iota(jnp.int32, (BLK, BLK), 1)
    row = lax.broadcasted_iota(jnp.int32, (BLK, BLK), 0)
    return lane, row


def pack(block):
    lane, row = places()
    rest = jnp.where(lane == row, block - block.astype(BF16).astype(F32), 0.0)
    moved = pltpu.roll(rest, BLK - 1, 0)
    first = pltpu.roll(rest[:8], BLK - 1, 1)
    upper = jnp.where(lane == row + 1, moved, 0.0)
    top = jnp.where((row[:8] == 0) & (lane[:8] == BLK - 1), first, upper[:8])
    upper = jnp.concatenate([top, upper[8:]], axis=0)
    return jnp.where(lane > row, upper, block).astype(BF16)


def unpack(block):
    lane, row = places()
    block = block.astype(F32)
    moved = pltpu.roll(block, 1, 0)
    first = pltpu.roll(block[:8], 1, 1)
    top = jnp.where(row[:8] == 0, first, moved[:8])
    rest = jnp.concatenate([top, moved[8:]], axis=0)
    return jnp.where(lane > row, 0.0, jnp.where(lane == row, block + rest, block))


def known_kernel(info_ref, id_ref, names_ref, out_ref):
    me = info_ref[4]
    count = names_ref.shape[0]
    per = BLK // count
    lane = lax.broadcasted_iota(jnp.int32, out_ref.shape, 1)
    row = lax.broadcasted_iota(jnp.int32, out_ref.shape, 0)
    table = jnp.where((row == 0) & (lane == id_ref[0]), me, 0)
    mine = row == 1 + lax.div(me, per)
    for c in range(count):
        table = jnp.where(mine & (lane == lax.rem(me, per) * count + c), names_ref[c], table)
    out_ref[...] = table


def add_blocks(info_ref, known_ref, names, ref, acc, lanes, widen=lambda block: block):
    core = info_ref[0]

    def add(c, carry):
        p = known_ref[0, names(c)]

        @pl.when(lax.rem(p, 2) == core)
        def _():
            at = lax.div(p, 2)
            acc[at, :, lanes] += widen(ref[c]).astype(F32)

        return carry

    lax.fori_loop(0, ref.shape[0], add, 0)


def name_tables(info_ref, known_ref, names_ref, count):
    other = info_ref[4] + 1 - 2 * info_ref[0]
    per = BLK // count
    return [
        lambda c: names_ref[c],
        lambda c: known_ref[1 + lax.div(other, per), lax.rem(other, per) * count + c],
    ]


def emit_y(ny, y, acc, own_ref, sends, narrow):
    def emit(z, carry):
        for d in range(ny):
            block = acc[z * ny + lax.rem(y + d, ny)]
            if d == 0:
                own_ref[z] = block
            else:
                sends[d - 1][z] = narrow(block)
        return carry

    lax.fori_loop(0, own_ref.shape[0], emit, 0)


def scatter_diag_kernel(ny, info_ref, known_ref, names_ref, mine_ref, theirs_ref, own_ref, *rest):
    sends, acc = rest[:-1], rest[-1]
    acc[...] = jnp.zeros_like(acc)
    mine, theirs = name_tables(info_ref, known_ref, names_ref, names_ref.shape[0])
    add_blocks(info_ref, known_ref, mine, mine_ref, acc, slice(None))
    add_blocks(info_ref, known_ref, theirs, theirs_ref, acc, slice(None), unpack)
    emit_y(ny, info_ref[1], acc, own_ref, sends, pack)


def scatter_off_kernel(ny, info_ref, known_ref, names_ref, *refs):
    (mine_ref, across_ref, theirs_ref, their_across_ref, own_ref), rest = refs[:5], refs[5:]
    sends, acc = rest[:-1], rest[-1]
    first = jnp.where(info_ref[3] < 2, 0, across_ref.shape[0])
    acc[...] = jnp.zeros_like(acc)
    tables = name_tables(info_ref, known_ref, names_ref, names_ref.shape[0])
    blocks = ((mine_ref, across_ref), (theirs_ref, their_across_ref))
    for names, (right, across) in zip(tables, blocks):
        add_blocks(info_ref, known_ref, names, right, acc, slice(0, BLK))
        add_blocks(info_ref, known_ref, lambda c: names(first + c), across, acc, slice(BLK, 2 * BLK))
    emit_y(ny, info_ref[1], acc, own_ref, sends, lambda block: block.astype(BF16))


def sum_y_kernel(diag, info_ref, own_ref, *refs):
    got, (out_ref, send_ref) = refs[:-2], refs[-2:]
    widen = unpack if diag else lambda block: block.astype(F32)
    narrow = pack if diag else lambda block: block.astype(BF16)

    def step(at, carry):
        total = own_ref[at]
        for ref in got:
            total += widen(ref[at])
        send_ref[at] = narrow(total)

        @pl.when(at == info_ref[2])
        def _():
            out_ref[...] = total

        return carry

    lax.fori_loop(0, own_ref.shape[0], step, 0)


def sum_z_kernel(info_ref, own_ref, got_ref, *out_refs):
    total = own_ref[...]
    for at in range(got_ref.shape[0]):
        total += jnp.where(info_ref[2] == at, 0.0, got_ref[at].astype(F32))
    for b, ref in enumerate(out_refs):
        ref[...] = total[:, BLK * b : BLK * (b + 1)]


def finish_kernel(info_ref, tile_ref, diag_ref, got_ref, right_ref, across_ref, left_in, across_in, out_ref):
    row, n = info_ref[3], 4
    r = lax.broadcasted_iota(jnp.int32, (BLK, BLK), 0)
    c = lax.broadcasted_iota(jnp.int32, (BLK, BLK), 1)
    low = diag_ref[...]
    for at in range(got_ref.shape[0]):
        low += jnp.where(info_ref[2] == at, 0.0, unpack(got_ref[at]))

    def put(at, value):
        cols = pl.ds(pl.multiple_of(at * BLK, BLK), BLK)
        out_ref[:, cols] = tile_ref[:, cols] - value

    put(row, jnp.where(c > r, low.T, low))
    put(lax.rem(row + 1, n), right_ref[...])
    put(lax.rem(row + 3, n), left_in[...].T)
    put(lax.rem(row + 2, n), across_ref[...] + across_in[...].T)


def ring(n, d):
    return [(i, (i + d) % n) for i in range(n)]


def f32_out(*shape):
    return jax.ShapeDtypeStruct(shape, F32)


def bf16_out(*shape):
    return jax.ShapeDtypeStruct(shape, BF16)


def on_device(diag_blocks, panel_blocks, ancestors, target_ids, target_tiles):
    nz, ny = lax.axis_size("z"), lax.axis_size("y")
    sn, anc, rows, width = panel_blocks.shape
    count = sn * anc
    half = count // sn
    z, y, core, row = (lax.axis_index(a).astype(jnp.int32) for a in ("z", "y", "core", "row"))
    info = jnp.stack([core, y, z, row, (z * ny + y) * 2 + core])
    at_row = row[None]
    panel = panel_blocks.reshape(sn, anc * rows, width)
    names = ancestors.reshape(count)

    def send(blocks, distance):
        return lax.ppermute(blocks, "row", ring(4, distance))

    def blocks(part):
        return part.reshape(-1, rows, part.shape[-1])

    def after_scatter(kernel, args, wide, name, **kwargs):
        return call(
            functools.partial(kernel, ny),
            [info, known, names, *args],
            [f32_out(nz, BLK, wide)] + [bf16_out(nz, BLK, wide)] * (ny - 1),
            [pltpu.VMEM((nz * ny, BLK, wide), F32)],
            name=name,
            smem=3,
            **kwargs,
        )

    def along_y(sends):
        return [lax.ppermute(s, "y", ring(ny, d + 1)) for d, s in enumerate(sends)]

    def sum_y(own, got, name, deps=(), diag=False):
        wide = own.shape[2]
        outs = [f32_out(BLK, wide), bf16_out(nz, BLK, wide)]
        kernel = functools.partial(sum_y_kernel, diag)
        own, sends = call(kernel, [info, own, *got], outs, name=name, deps=deps)
        return own, lax.all_to_all(sends, "z", 0, 0, tiled=True)

    w, solved, rounded, part = first_chunk(at_row, diag_blocks, panel)
    own = [blocks(rounded)]
    right = [send(own[0], -1)]
    hop = send(blocks(part), 1)
    w = second_factor(diag_blocks, w)
    solved, rounded, part, diag, packed = second_chunk(at_row, w, own[0], panel, solved, hop)
    own.append(blocks(rounded))
    right.append(send(own[1], -1))
    across = [send(hop, 1)]
    hop = send(blocks(part), 1)
    their_diag = lax.ppermute(packed, "core", ring(2, 1))

    (known,) = call(
        known_kernel,
        [info, target_ids, names],
        [jax.ShapeDtypeStruct((1 + nz * ny * 2 * count // BLK, BLK), jnp.int32)],
        name="known",
        smem=3,
        deps=[diag, right[0]],
    )
    known = lax.psum(known, COL)
    (hop,) = call(lambda info: None, [info], [], name="pass_on", deps=[known], through=[hop])
    across.append(send(hop, 1))
    own_diag, *sends = after_scatter(scatter_diag_kernel, [diag, their_diag], BLK, "scatter_diag")
    got_diag = along_y(sends)
    off_right, off_across, send_right, send_across = call(
        functools.partial(products_kernel, len(own)),
        [at_row, *own, *right, *across],
        [out(n, BLK, BLK) for out in (f32_out, bf16_out) for n in (count, half)],
        name="products",
        deps=got_diag,
    )
    their_right = lax.ppermute(send_right, "core", ring(2, 1))
    their_across = lax.ppermute(send_across, "core", ring(2, 1))
    own_off, *sends = after_scatter(
        scatter_off_kernel, [off_right, off_across, their_right, their_across], 2 * BLK, "scatter_off"
    )
    got_off = along_y(sends)
    own_diag, got_diag = sum_y(own_diag, got_diag, "sum_diag", [own_off], diag=True)
    own_off, got_off = sum_y(own_off, got_off, "sum_off", [got_diag])
    off_right, off_across = call(
        sum_z_kernel, [info, own_off, got_off], [f32_out(BLK, BLK)] * 2, name="last_sum"
    )
    from_left = send(off_right, 1)
    from_across = send(off_across, 2)
    (updated,) = call(
        finish_kernel,
        [info, target_tiles.reshape(rows, width), own_diag, got_diag]
        + [off_right, off_across, from_left, from_across],
        [f32_out(rows, width)],
        name="finish",
    )
    return solved.reshape(panel_blocks.shape), updated.reshape(target_tiles.shape)


def solution(mesh):
    devices = mesh.devices
    nz, ny = 8, 4
    fine = Mesh(devices.reshape(nz, ny, 2, devices.shape[1]), ("z", "y", "core", "row"))
    in_specs = (
        P(COL, None, None),
        P(COL, None, "row", None),
        P(COL, None),
        P(COL),
        P(COL, "row", None),
    )
    out_specs = (P(COL, None, "row", None), P(COL, "row", None))
    return jax.shard_map(
        on_device, mesh=fine, in_specs=in_specs, out_specs=out_specs, check_vma=False
    )
```
